32 devices in a mesh: seq: 8 (over z, x), fsdp: 4 (over y, core).
Axes of the slice: x: 2, y: 2, z: 4, core: 2. Of those that a mesh axis runs over, the one named last changes fastest.
Arguments:
- layer_input: bfloat16 [4, 1024, 2880], P('fsdp', 'seq'), may hold values from -6 to 6
- attn_gain: bfloat16 [2880], P('fsdp'), may hold values from 0.25 to 1.75
- query_matrix: bfloat16 [2880, 4096], P(None, ('seq', 'fsdp')), may hold values from -0.109375 to 0.109375
- query_bias_vector: bfloat16 [4096], P(('seq', 'fsdp')), may hold values from -3 to 3
- key_matrix: bfloat16 [2880, 512], P(None, ('seq', 'fsdp')), may hold values from -0.109375 to 0.109375
- key_bias_vector: bfloat16 [512], P(('seq', 'fsdp')), may hold values from -3 to 3
- value_matrix: bfloat16 [2880, 512], P(None, ('seq', 'fsdp')), may hold values from -0.109375 to 0.109375
- value_bias_vector: bfloat16 [512], P(('seq', 'fsdp')), may hold values from -1.75 to 1.75
- sink_logit_values: bfloat16 [64], P('fsdp'), may hold values from -4 to 4
- output_matrix: bfloat16 [4096, 2880], P(('seq', 'fsdp')), may hold values from -0.375 to 0.375
- output_bias_vector: bfloat16 [2880], P('fsdp'), may hold values from -1.75 to 1.75
- ffn_gain: bfloat16 [2880], P('fsdp'), may hold values from 0.25 to 1.75
- router_weight: bfloat16 [2880, 8], P('fsdp'), may hold values from -0.0546875 to 0.0546875
- router_bias: bfloat16 [8], P('fsdp'), may hold values from -1.5 to 1.5
- expert_gate_up: bfloat16 [8, 2, 2880, 2880], P('seq', None, None, 'fsdp'), may hold values from -0.109375 to 0.109375
- expert_gate_up_bias: bfloat16 [8, 2, 2880], P('seq', None, 'fsdp'), may hold values from -1.25 to 1.25
- expert_down: bfloat16 [8, 2880, 2880], P('seq', 'fsdp'), may hold values from -0.21875 to 0.21875
- expert_down_bias: bfloat16 [8, 2880], P(None, 'fsdp'), may hold values from -1.25 to 1.25
- route_ids: int32 [4, 1024, 4], P('fsdp', 'seq'), may hold values from 0 to 7, all different within a row; in each aligned block of 128 rows (0 to 127, 128 to 255, ..., all dimensions but the last counted through in order) at most 80 rows name the same one
- doc_lengths: int32 [4, 3], replicated, may hold values from 1 to 960, 1024 in all within a row
- out_cotangent: bfloat16 [4, 1024, 2880], P('fsdp', 'seq'), may hold values from -6 to 6
Outputs:
- layer_output: bfloat16 [4, 1024, 2880], P('fsdp', 'seq')
- input_grad: float32 [4, 1024, 2880], P('fsdp', 'seq')
- attn_gain_grad: float32 [2880], P('fsdp')
- query_weight_grad: float32 [2880, 4096], P(None, ('seq', 'fsdp'))
- query_bias_grad: float32 [4096], P(('seq', 'fsdp'))
- key_weight_grad: float32 [2880, 512], P(None, ('seq', 'fsdp'))
- key_bias_grad: float32 [512], P(('seq', 'fsdp'))
- value_weight_grad: float32 [2880, 512], P(None, ('seq', 'fsdp'))
- value_bias_grad: float32 [512], P(('seq', 'fsdp'))
- sink_grad: float32 [64], P('fsdp')
- output_weight_grad: float32 [4096, 2880], P(('seq', 'fsdp'))
- output_bias_grad: float32 [2880], P('fsdp')
- ffn_gain_grad: float32 [2880], P('fsdp')
- router_weight_grad: float32 [2880, 8], P('fsdp')
- router_bias_grad: float32 [8], P('fsdp')
- expert_gate_up_grad: float32 [8, 2, 2880, 2880], P('seq', None, None, 'fsdp')
- expert_gate_up_bias_grad: float32 [8, 2, 2880], P('seq', None, 'fsdp')
- expert_down_grad: float32 [8, 2880, 2880], P('seq', 'fsdp')
- expert_down_bias_grad: float32 [8, 2880], P(None, 'fsdp')
The draws below stay inside these ranges and needn't reach their ends.
Inputs may be any that keep to these rules, and one draw needn't show every extreme that they name: `route_ids`: in the 128 rows of one device no expert is named more than 80 times; some expert is named exactly 80 times. `doc_lengths`: each row sums to 1024; its largest entry is 960.
All inputs are finite; a program needn't handle non-finite values.
Results may differ from the reference program's by a relative error of at most 0.024.
Values may be sent and summed in bfloat16 or wider, within the bound.
No kernel may reach another device: no remote copies, remote signals or barrier semaphores. Data moves between devices by JAX's collectives and lax.ppermute only.
A program may use at most 384 MiB of HBM per device.

```python
import math
from functools import partial
import jax
import jax.numpy as jnp
import numpy as np
from jax import lax

MODEL_DIM = 2880
QUERY_HEADS = 64
KEY_VALUE_HEADS = 8
HEAD_DIM = 64
FF = 2880
TOPK = 4
WINDOW_LENGTH = 128
NDOCS = 3
TOK_DEV = 128
EXPERTS = 8
SEQUENCE_COUNT = 4
SEQUENCE_LENGTH = 1024
CAP = 80
N_SEQ = 8
N_FSDP = 4


def block_levels(stream_key, shape, shards, low, high):
    loudness, own = 1.0, jax.random.fold_in(stream_key, 6)
    for axis_at, shards_of in shards:
        steps = jnp.exp(jax.random.uniform(jax.random.fold_in(own, axis_at), (shards_of,), jnp.float32, low / len(shards), high / len(shards)))
        loudness = loudness * jnp.repeat(steps, shape[axis_at] // shards_of).reshape([-1 if axis == axis_at else 1 for axis in range(len(shape))])
    return loudness


def split_up(number_of, total, reach, slope):
    loads = [(1 << 20) // math.isqrt(rank ** slope) + 1 for rank in range(2, number_of + 1)]
    spare, given = total - reach - (number_of - 1), [1] * (number_of - 1)
    while spare > 0:
        movable = [i for i in range(number_of - 1) if given[i] < reach]
        mass, left = sum([loads[i] for i in movable]), spare
        for i in movable:
            extra = min(reach - given[i], max(1, left * loads[i] // mass), spare)
            given[i] = given[i] + extra
            spare = spare - extra
    return np.array([reach] + given)


def ragged_sizes(own_key, count, total, limit, slope):
    if count == 2:
        one = jax.random.randint(own_key, (), max(1, total - limit), min(limit, total - 1) + 1)
        return jnp.stack([one, total - one])
    lengths = jnp.asarray(split_up(count, total, limit, slope), jnp.int32)
    couples = (count - 1) // 2
    source_of, sink = lengths[1:1 + 2 * couples:2], lengths[2:2 + 2 * couples:2]
    slack = jnp.minimum(source_of - 1, limit - sink)
    moved = jax.random.randint(jax.random.fold_in(own_key, 1), (couples,), 0, 1 << 20) % (slack + 1)
    lengths = lengths.at[1:1 + 2 * couples:2].set(source_of - moved).at[2:2 + 2 * couples:2].set(sink + moved)
    return lengths[jax.random.permutation(jax.random.fold_in(own_key, 2), count)]


def routed_block(key, own, number, rows, number_of, top, most, skew):
    order = jax.random.permutation(key, number_of)
    crowded, usual = shares(number_of, rows * top, most, skew, True), shares(number_of, rows * top, most, skew, False)
    places = jnp.arange(number_of)

    def named(lengths, rotation):
        used = int((lengths > 0).sum())
        fixed = max(1, used // 4)
        shifted = fixed + (places - fixed + rotation * (used - fixed)) % max(1, number_of - fixed)
        return jnp.zeros((number_of,), jnp.int32).at[order[jnp.where(places < fixed, places, shifted)]].set(jnp.asarray(lengths, jnp.int32))

    lengths = jnp.where(number % 4 == 0, named(crowded, number // 4), named(usual, number - number // 4 - 1))
    mixed = jax.random.permutation(jax.random.fold_in(own, 3), number_of)
    giver, receiver = mixed[0:number_of // 2 * 2:2], mixed[1:number_of // 2 * 2:2]
    margin = jnp.minimum(lengths[giver] - 1, most - lengths[receiver]) // 2
    margin = jnp.where((giver == order[0]) | (receiver == order[0]) | (lengths[receiver] == 0), 0, jnp.maximum(margin, 0))
    shifted = jax.random.randint(jax.random.fold_in(own, 4), (number_of // 2,), 0, 1 << 20) % (margin + 1)
    lengths = lengths.at[giver].add(-shifted).at[receiver].add(shifted)
    members = jnp.searchsorted(jnp.cumsum(lengths), jnp.arange(rows * top), side="right").astype(jnp.int32)
    table = members.reshape(top, rows).T
    table = table[jax.random.permutation(jax.random.fold_in(own, 1), rows)]
    rotation = jax.random.randint(jax.random.fold_in(own, 2), (rows, 1), 0, top)
    return jnp.take_along_axis(table, (jnp.arange(top)[None, :] + rotation) % top, axis=1)


def shares(count, total, most, slope, full):
    portions = [(1 << 20) // math.isqrt(rank ** slope) + 1 for rank in range(1, count + 1)]
    largest = most if full else min(most, max(-(-total // count), total * portions[0] // sum(portions)))
    least = 1 if total - largest >= count - 1 else 0
    holding, surplus = [largest] + [least] * (count - 1), total - largest - least * (count - 1)
    while surplus > 0:
        candidates = [i for i in range(1, count) if holding[i] < largest] or [i for i in range(1, count) if holding[i] < most]
        whole, remaining = sum([portions[i] for i in candidates]), surplus
        for i in candidates:
            addition = min(most - holding[i], max(1, remaining * portions[i] // whole), surplus)
            holding[i] = holding[i] + addition
            surplus = surplus - addition
    return np.array(holding)


def normal_values(rng, extent, spread, most, shards=(), kind=jnp.bfloat16):
    values = spread * jax.random.normal(rng, extent, jnp.float32)
    if shards:
        values = values * block_levels(rng, extent, shards, -0.22, 0.18)
    return jnp.clip(values, -most, most).astype(kind)


def setup_inputs(seed: int = 0) -> dict:
    keys = jax.random.split(jax.random.key(seed), 22)
    layer_input = normal_values(keys[0], (SEQUENCE_COUNT, SEQUENCE_LENGTH, MODEL_DIM), 1.0, 6.0, ((0, 4), (1, 8)))
    attn_gain = jnp.clip(1.0 + 0.15 * jax.random.normal(keys[1], (MODEL_DIM,), jnp.float32), 0.25, 1.75).astype(jnp.bfloat16)
    query_matrix = normal_values(keys[2], (MODEL_DIM, QUERY_HEADS * HEAD_DIM), MODEL_DIM ** -0.5, 0.109375, ((1, 32),))
    query_bias_vector = normal_values(keys[3], (QUERY_HEADS * HEAD_DIM,), 0.5, 3.0, ((0, 32),))
    key_matrix = normal_values(keys[4], (MODEL_DIM, KEY_VALUE_HEADS * HEAD_DIM), MODEL_DIM ** -0.5, 0.109375, ((1, 32),))
    key_bias_vector = normal_values(keys[5], (KEY_VALUE_HEADS * HEAD_DIM,), 0.5, 3.0, ((0, 32),))
    value_matrix = normal_values(keys[6], (MODEL_DIM, KEY_VALUE_HEADS * HEAD_DIM), MODEL_DIM ** -0.5, 0.109375, ((1, 32),))
    value_bias_vector = normal_values(keys[7], (KEY_VALUE_HEADS * HEAD_DIM,), 0.3, 1.75, ((0, 32),))
    sink_logit_values = normal_values(keys[8], (QUERY_HEADS,), 1.0, 4.0, ((0, 4),))
    output_matrix = normal_values(keys[9], (QUERY_HEADS * HEAD_DIM, MODEL_DIM), (QUERY_HEADS * HEAD_DIM // 16) ** -0.5, 0.375, ((0, 32),))
    output_bias_vector = normal_values(keys[10], (MODEL_DIM,), 0.3, 1.75, ((0, 4),))
    ffn_gain = jnp.clip(1.0 + 0.15 * jax.random.normal(keys[11], (MODEL_DIM,), jnp.float32), 0.25, 1.75).astype(jnp.bfloat16)
    router_weight = normal_values(keys[12], (MODEL_DIM, EXPERTS), (4 * MODEL_DIM) ** -0.5, 0.0546875, ((0, 4),))
    router_bias = normal_values(keys[13], (EXPERTS,), 0.25, 1.5, ((0, 4),))
    expert_gate_up = normal_values(keys[14], (EXPERTS, 2, MODEL_DIM, FF), MODEL_DIM ** -0.5, 0.109375, ((0, 8), (3, 4)))
    expert_gate_up_bias = normal_values(keys[15], (EXPERTS, 2, FF), 0.2, 1.25, ((0, 8), (2, 4)))
    expert_down = normal_values(keys[16], (EXPERTS, FF, MODEL_DIM), (FF // 4) ** -0.5, 0.21875, ((0, 8), (1, 4)))
    expert_down_bias = normal_values(keys[17], (EXPERTS, MODEL_DIM), 0.2, 1.25, ((1, 4),))
    route_ids_keys = jax.random.split(jax.random.fold_in(keys[18], 1), SEQUENCE_COUNT * SEQUENCE_LENGTH // TOK_DEV)
    route_ids_turns = jax.random.permutation(jax.random.fold_in(keys[18], 3), SEQUENCE_COUNT * SEQUENCE_LENGTH // TOK_DEV)
    route_ids = jax.vmap(lambda own, number: routed_block(jax.random.fold_in(keys[18], 2), own, number, TOK_DEV, EXPERTS, TOPK, CAP, 1))(route_ids_keys, route_ids_turns).reshape((SEQUENCE_COUNT, SEQUENCE_LENGTH, TOPK))
    doc_lengths = jax.vmap(lambda own: ragged_sizes(own, NDOCS, SEQUENCE_LENGTH, SEQUENCE_LENGTH - TOK_DEV // 2, 0))(jax.random.split(keys[19], SEQUENCE_COUNT)).reshape((SEQUENCE_COUNT, NDOCS)).astype(jnp.int32)
    out_cotangent = normal_values(keys[20], (SEQUENCE_COUNT, SEQUENCE_LENGTH, MODEL_DIM), 1.0, 6.0, ((0, 4), (1, 8)))
    return dict(layer_input=layer_input, attn_gain=attn_gain, query_matrix=query_matrix, query_bias_vector=query_bias_vector, key_matrix=key_matrix, key_bias_vector=key_bias_vector, value_matrix=value_matrix, value_bias_vector=value_bias_vector, sink_logit_values=sink_logit_values, output_matrix=output_matrix, output_bias_vector=output_bias_vector, ffn_gain=ffn_gain, router_weight=router_weight, router_bias=router_bias, expert_gate_up=expert_gate_up, expert_gate_up_bias=expert_gate_up_bias, expert_down=expert_down, expert_down_bias=expert_down_bias, route_ids=route_ids, doc_lengths=doc_lengths, out_cotangent=out_cotangent)


ROPE_BASE = 150000.0
NORM_EPS = 1e-05
GLU_ALPHA = 1.702
GLU_LIMIT = 7.0
EXACT_PRECISION = lax.Precision.HIGHEST

@jax.custom_vjp
def reduced_precision(v):
    return lax.optimization_barrier(v.astype(jnp.bfloat16)).astype(jnp.float32)

@jax.custom_vjp
def reduced_backward(v):
    return v

def low_keep(v):
    return (reduced_precision(v), None)

def low_pass(kept, grad):
    return (grad,)

def back_keep(v):
    return (v, None)

def back_low(kept, grad):
    return (reduced_precision(grad),)
reduced_precision.defvjp(low_keep, low_pass)
reduced_backward.defvjp(back_keep, back_low)

def rms_scale(values):
    return lax.rsqrt(lax.optimization_barrier(jnp.mean(values * values, axis=-1, keepdims=True)) + NORM_EPS)

def rope_tables(positions):
    frequency = ROPE_BASE ** (-jnp.arange(HEAD_DIM // 2, dtype=jnp.float32) * 2.0 / HEAD_DIM)
    angles = positions.astype(jnp.float32)[:, None] * frequency[None, :]
    return (jnp.cos(angles), jnp.sin(angles))

def apply_rotary(values, cosine_values, sine_values, direction):
    half_size = values.shape[-1] // 2
    first_half = values[..., :half_size]
    second = values[..., half_size:]
    cosine_b = cosine_values[:, None, :]
    sine_b = direction * sine_values[:, None, :]
    return jnp.concatenate([first_half * cosine_b - second * sine_b, second * cosine_b + first_half * sine_b], axis=-1)

def swiglu(gate_pre, up_pre):
    gate_soft = GLU_LIMIT - jax.nn.softplus(GLU_LIMIT - gate_pre)
    up_soft = GLU_LIMIT * jnp.tanh(up_pre / GLU_LIMIT)
    return (up_soft + 1.0) * gate_soft * jax.nn.sigmoid(GLU_ALPHA * gate_soft)

def attend_sequence(query_rows, key_row_values, value_row_values, doc_ids, sink_logit_values):
    length = query_rows.shape[0]
    rows_per_block = min(512, length)
    query_groups = QUERY_HEADS // KEY_VALUE_HEADS
    empty_rows = jnp.zeros((WINDOW_LENGTH, KEY_VALUE_HEADS, HEAD_DIM), query_rows.dtype)
    keys_padded = jnp.concatenate([empty_rows, key_row_values], axis=0)
    values_padded = jnp.concatenate([empty_rows, value_row_values], axis=0)
    docs_padded = jnp.concatenate([jnp.zeros((WINDOW_LENGTH,), jnp.int32), doc_ids], axis=0)
    sink_logit_grid = sink_logit_values.reshape(KEY_VALUE_HEADS, query_groups)

    def one_block(block_first_row):
        query_row_block = lax.dynamic_slice_in_dim(query_rows, block_first_row, rows_per_block, 0).reshape(rows_per_block, KEY_VALUE_HEADS, query_groups, HEAD_DIM)
        key_block = lax.dynamic_slice_in_dim(keys_padded, block_first_row, rows_per_block + WINDOW_LENGTH, 0)
        value_block = lax.dynamic_slice_in_dim(values_padded, block_first_row, rows_per_block + WINDOW_LENGTH, 0)
        query_pos = block_first_row + jnp.arange(rows_per_block, dtype=jnp.int32)
        key_pos = block_first_row - WINDOW_LENGTH + jnp.arange(rows_per_block + WINDOW_LENGTH, dtype=jnp.int32)
        query_doc = lax.dynamic_slice_in_dim(doc_ids, block_first_row, rows_per_block, 0)
        key_doc = lax.dynamic_slice_in_dim(docs_padded, block_first_row, rows_per_block + WINDOW_LENGTH, 0)
        offset = query_pos[:, None] - key_pos[None, :]
        allowed = (key_pos[None, :] >= 0) & (offset >= 0) & (offset <= WINDOW_LENGTH) & (query_doc[:, None] == key_doc[None, :])
        scores = reduced_backward(jnp.einsum('qhgd,khd->hgqk', query_row_block, key_block, precision=EXACT_PRECISION) * 0.125)
        scores = jnp.where(allowed[None, None], scores, -1e+30)
        sink_col = sink_logit_grid[:, :, None]
        top_score = jnp.maximum(lax.optimization_barrier(jnp.max(scores, axis=-1)), sink_col)
        exp_scores = jnp.exp(scores - top_score[..., None])
        denominator = lax.optimization_barrier(jnp.sum(exp_scores, axis=-1)) + jnp.exp(sink_col - top_score)
        probabilities = reduced_precision(exp_scores / denominator[..., None])
        mixed_heads = jnp.einsum('hgqk,khd->qhgd', probabilities, value_block, precision=EXACT_PRECISION)
        return mixed_heads.reshape(rows_per_block, QUERY_HEADS * HEAD_DIM)
    starts = jnp.arange(length // rows_per_block, dtype=jnp.int32) * rows_per_block
    return lax.map(jax.checkpoint(one_block), starts).reshape(length, QUERY_HEADS * HEAD_DIM)

def forward(route_flat, member_weight, rows_order, live_mask, doc_ids, layer_input, attn_gain, query_matrix, query_bias_vector, key_matrix, key_bias_vector, value_matrix, value_bias_vector, sink_logit_values, output_matrix, output_bias_vector, ffn_gain, router_weight, router_bias, expert_gate_up, expert_gate_up_bias, expert_down, expert_down_bias):
    normalized_input = reduced_precision(layer_input * rms_scale(layer_input) * attn_gain)
    query_linear = reduced_backward(jnp.einsum('phn,nx->phx', normalized_input, query_matrix, precision=EXACT_PRECISION) + query_bias_vector)
    key_linear = reduced_backward(jnp.einsum('phn,nx->phx', normalized_input, key_matrix, precision=EXACT_PRECISION) + key_bias_vector)
    value_linear = reduced_backward(jnp.einsum('phn,nx->phx', normalized_input, value_matrix, precision=EXACT_PRECISION) + value_bias_vector)
    positions = jnp.arange(SEQUENCE_LENGTH, dtype=jnp.int32)
    cosine_values, sine_values = rope_tables(positions)
    query_rows = reduced_precision(apply_rotary(query_linear.reshape(SEQUENCE_COUNT, SEQUENCE_LENGTH, QUERY_HEADS, HEAD_DIM), cosine_values, sine_values, 1.0))
    key_row_values = reduced_precision(apply_rotary(key_linear.reshape(SEQUENCE_COUNT, SEQUENCE_LENGTH, KEY_VALUE_HEADS, HEAD_DIM), cosine_values, sine_values, 1.0))
    value_row_values = reduced_precision(value_linear).reshape(SEQUENCE_COUNT, SEQUENCE_LENGTH, KEY_VALUE_HEADS, HEAD_DIM)
    head_output = jnp.stack([attend_sequence(query_rows[seq_index], key_row_values[seq_index], value_row_values[seq_index], doc_ids[seq_index], sink_logit_values) for seq_index in range(SEQUENCE_COUNT)])
    head_output = reduced_backward(reduced_precision(head_output))
    attention_output = reduced_backward(jnp.einsum('tvg,gk->tvk', head_output, output_matrix, precision=EXACT_PRECISION) + output_bias_vector)
    resid_mid = layer_input + attention_output
    normed_mid = reduced_precision(resid_mid * rms_scale(resid_mid) * ffn_gain)
    flat_mid = normed_mid.reshape(-1, MODEL_DIM)
    logits = jnp.dot(flat_mid, router_weight, precision=EXACT_PRECISION) + router_bias
    picked = jnp.take_along_axis(logits, route_flat, axis=1)
    gate_probs = jax.nn.softmax(picked, axis=-1)
    expert_gate = lax.optimization_barrier(jnp.sum(gate_probs[:, :, None] * member_weight, axis=1)).T

    def expert_step(mixture, packed):
        gate_up_w, gate_up_b, down_w, down_b, rows_at, live_row, share_row = packed
        row_values = reduced_backward(flat_mid[rows_at])
        gate_pre = reduced_backward(jnp.dot(row_values, gate_up_w[0], precision=EXACT_PRECISION) + gate_up_b[0])
        up_pre = reduced_backward(jnp.dot(row_values, gate_up_w[1], precision=EXACT_PRECISION) + gate_up_b[1])
        hidden = reduced_precision(swiglu(gate_pre, up_pre))
        result = reduced_backward(reduced_precision(jnp.dot(hidden, down_w, precision=EXACT_PRECISION) + down_b))
        weight = share_row[rows_at] * live_row
        return (mixture.at[rows_at].add(weight[:, None] * result), None)
    mixture, _ = lax.scan(expert_step, jnp.zeros_like(flat_mid), (expert_gate_up, expert_gate_up_bias, expert_down, expert_down_bias, rows_order, live_mask, expert_gate))
    return resid_mid + mixture.reshape(SEQUENCE_COUNT, SEQUENCE_LENGTH, MODEL_DIM)

def reference(layer_input, attn_gain, query_matrix, query_bias_vector, key_matrix, key_bias_vector, value_matrix, value_bias_vector, sink_logit_values, output_matrix, output_bias_vector, ffn_gain, router_weight, router_bias, expert_gate_up, expert_gate_up_bias, expert_down, expert_down_bias, route_ids, doc_lengths, out_cotangent):
    route_flat = route_ids.reshape(-1, TOPK).astype(jnp.int32)
    member = route_flat[:, :, None] == jnp.arange(EXPERTS, dtype=jnp.int32)[None, None, :]
    member_weight = member.astype(jnp.float32)
    hit_mask = jnp.any(member, axis=1).T
    rows_order = jnp.argsort(jnp.where(hit_mask, 0, 1).astype(jnp.int32), axis=1, stable=True)[:, :CAP * N_SEQ * N_FSDP].astype(jnp.int32)
    live_mask = jnp.take_along_axis(hit_mask, rows_order, axis=1).astype(jnp.float32)
    positions = jnp.arange(SEQUENCE_LENGTH, dtype=jnp.int32)
    doc_ends = jnp.cumsum(doc_lengths.astype(jnp.int32), axis=1)
    doc_ids = lax.optimization_barrier(jnp.sum((positions[None, :, None] >= doc_ends[:, None, :]).astype(jnp.int32), axis=2)).astype(jnp.int32)
    floats = [argument.astype(jnp.float32) for argument in (layer_input, attn_gain, query_matrix, query_bias_vector, key_matrix, key_bias_vector, value_matrix, value_bias_vector, sink_logit_values, output_matrix, output_bias_vector, ffn_gain, router_weight, router_bias, expert_gate_up, expert_gate_up_bias, expert_down, expert_down_bias)]
    final_out, pullback = jax.vjp(partial(forward, route_flat, member_weight, rows_order, live_mask, doc_ids), *floats)
    gradients = pullback(out_cotangent.astype(jnp.float32))
    return (final_out.astype(jnp.bfloat16), gradients[0], gradients[1], gradients[2], gradients[3], gradients[4], gradients[5], gradients[6], gradients[7], gradients[8], gradients[9], gradients[10], gradients[11], gradients[12], gradients[13], gradients[14], gradients[15], gradients[16], gradients[17])
```

```python
import jax
import jax.numpy as jnp
from jax import lax
from jax.sharding import PartitionSpec as P

QUERY_HEADS = 64
KEY_VALUE_HEADS = 8
HEAD_DIM = 64
WINDOW_LENGTH = 128


ROPE_BASE = 150000.0
NORM_EPS = 1e-05
GLU_ALPHA = 1.702
GLU_LIMIT = 7.0
EXACT = lax.Precision.HIGHEST
BF = jnp.bfloat16
F32 = jnp.float32


def rms_scale(values):
    return lax.rsqrt(jnp.mean(values * values, axis=-1, keepdims=True) + NORM_EPS)


def rope_tables(positions):
    frequency = ROPE_BASE ** (-jnp.arange(HEAD_DIM // 2, dtype=jnp.float32) * 2.0 / HEAD_DIM)
    angles = positions.astype(jnp.float32)[:, None] * frequency[None, :]
    return (jnp.cos(angles), jnp.sin(angles))


def apply_rotary(values, cosine_values, sine_values, direction):
    half_size = HEAD_DIM // 2
    rows, width = values.shape
    grid = values.reshape(rows, width // HEAD_DIM, HEAD_DIM)
    first_half = grid[..., :half_size]
    second = grid[..., half_size:]
    cosine_b = cosine_values[:, None, :]
    sine_b = direction * sine_values[:, None, :]
    turned = jnp.concatenate(
        [first_half * cosine_b - second * sine_b, second * cosine_b + first_half * sine_b], axis=-1
    )
    return turned.reshape(rows, width)


def swiglu(gate_pre, up_pre):
    gate_soft = GLU_LIMIT - jax.nn.softplus(GLU_LIMIT - gate_pre)
    up_soft = GLU_LIMIT * jnp.tanh(up_pre / GLU_LIMIT)
    return (up_soft + 1.0) * gate_soft * jax.nn.sigmoid(GLU_ALPHA * gate_soft)


def dot(left, right, left_dim, right_dim, precision=None):
    return lax.dot_general(
        left,
        right,
        (((left_dim,), (right_dim,)), ((), ())),
        precision=precision,
        preferred_element_type=jnp.float32,
    )


def gather_seq(block):
    return lax.all_gather(block, "seq", axis=0, tiled=True)


def scatter_seq(partial_rows):
    return lax.psum_scatter(partial_rows, "seq", scatter_dimension=0, tiled=True)


def gather_fsdp(block):
    return lax.all_gather(block, "fsdp", axis=0, tiled=True)


def scatter_fsdp(partial_rows):
    return lax.psum_scatter(partial_rows, "fsdp", scatter_dimension=0, tiled=True)


def split_low(values):
    high = values.astype(BF)
    low = (values - high.astype(F32)).astype(BF)
    return high, low


def with_previous(blocks):
    before = jnp.concatenate([jnp.zeros_like(blocks[:1]), blocks[:-1]], axis=0)
    return jnp.concatenate([before, blocks], axis=1)


def masked_scores(query_grid, key_all, allowed):
    scores = (
        jnp.einsum("nqhgd,nkhd->nhgqk", query_grid, key_all, preferred_element_type=F32) * 0.125
    )
    return jnp.where(allowed[:, None, None], scores, -1e30)


def window_mask(doc_row, block_count, block_rows):
    doc_ends = jnp.cumsum(doc_row)
    starts = jnp.arange(block_count, dtype=jnp.int32)[:, None] * block_rows
    positions = starts + jnp.arange(block_rows, dtype=jnp.int32)[None, :]
    key_pos = starts - block_rows + jnp.arange(2 * block_rows, dtype=jnp.int32)[None, :]
    query_doc = jnp.sum((positions[:, :, None] >= doc_ends).astype(jnp.int32), axis=2)
    key_doc = jnp.sum((key_pos[:, :, None] >= doc_ends).astype(jnp.int32), axis=2)
    offset = positions[:, :, None] - key_pos[:, None, :]
    inside = (key_pos[:, None, :] >= 0) & (offset >= 0) & (offset <= WINDOW_LENGTH)
    return inside & (query_doc[:, :, None] == key_doc[:, None, :])


def per_device(
    layer_input,
    attn_gain,
    query_matrix,
    query_bias_vector,
    key_matrix,
    key_bias_vector,
    value_matrix,
    value_bias_vector,
    sink_logit_values,
    output_matrix,
    output_bias_vector,
    ffn_gain,
    router_weight,
    router_bias,
    expert_gate_up,
    expert_gate_up_bias,
    expert_down,
    expert_down_bias,
    route_ids,
    doc_lengths,
    out_cotangent,
):
    seq_count = lax.axis_size("seq")
    fsdp_count = lax.axis_size("fsdp")
    seq_index = lax.axis_index("seq")
    fsdp_index = lax.axis_index("fsdp")
    tokens_here, width = layer_input.shape[1:]
    choose_count = route_ids.shape[2]
    expert_count = seq_count
    block_rows = WINDOW_LENGTH
    length = seq_count * tokens_here
    block_count = length // block_rows
    capacity = max(2, tokens_here * choose_count * 5 // (4 * expert_count)) * seq_count
    padded = -(-(width + 2 * expert_count) // 128) * 128
    heads_here = QUERY_HEADS // seq_count
    kv_here = max(1, KEY_VALUE_HEADS // seq_count)
    group = heads_here // kv_here
    shared_kv = seq_count > KEY_VALUE_HEADS
    q_width, kv_width = heads_here * HEAD_DIM, kv_here * HEAD_DIM

    rows_x = gather_seq(layer_input[0])
    member_here = jnp.any(
        route_ids[0][:, :, None] == jnp.arange(expert_count, dtype=jnp.int32), axis=1
    )
    cot_here = out_cotangent[0]
    cot_packed = jnp.concatenate(
        [
            cot_here,
            member_here.astype(BF),
            jnp.zeros((tokens_here, padded - width - expert_count), BF),
        ],
        axis=1,
    )
    cot_rows = gather_seq(cot_packed)

    part = attn_gain.shape[0]
    q_part, kv_part = query_bias_vector.shape[0], key_bias_vector.shape[0]
    tiny = jnp.concatenate(
        [sink_logit_values, router_bias, query_bias_vector, key_bias_vector, value_bias_vector]
    )
    tiny = jnp.concatenate([tiny, jnp.zeros((part - tiny.shape[0],), BF)])
    small = jnp.concatenate(
        [
            attn_gain[None],
            ffn_gain[None],
            output_bias_vector[None],
            tiny[None],
            expert_down_bias,
            router_weight.T,
        ],
        axis=0,
    )
    small_all = lax.all_gather(small, "fsdp", axis=0)
    wide = jnp.swapaxes(small_all, 0, 1).reshape(small.shape[0], width).astype(F32)
    attn_gain_f, ffn_gain_f, out_bias_f = wide[0], wide[1], wide[2]
    down_bias_f = wide[4 : 4 + expert_count]
    router_t = wide[4 + expert_count :].astype(BF)
    tiny_all = small_all[:, 3]
    places = [0]
    for piece in (sink_logit_values, router_bias, query_bias_vector, key_bias_vector, value_bias_vector):
        places.append(places[-1] + piece.shape[0])
    sinks_f, router_bias_f, q_bias, k_bias, v_bias = (
        tiny_all[:, a:b].reshape(-1).astype(F32) for a, b in zip(places[:-1], places[1:])
    )
    wq = lax.all_gather(query_matrix, "fsdp", axis=1, tiled=True)
    wo = lax.all_gather(output_matrix, "fsdp", axis=0, tiled=True)
    if shared_kv:
        share = seq_count // KEY_VALUE_HEADS
        kv_head = seq_index // share

        def own_head(piece, axis):
            whole = lax.all_gather(piece, ("seq", "fsdp"), axis=axis, tiled=True)
            return lax.dynamic_slice_in_dim(whole, kv_head * HEAD_DIM, HEAD_DIM, axis)

        wk, wv = own_head(key_matrix, 1), own_head(value_matrix, 1)
        k_bias = own_head(key_bias_vector, 0).astype(F32)
        v_bias = own_head(value_bias_vector, 0).astype(F32)
    else:
        wkv = lax.all_gather(jnp.stack([key_matrix, value_matrix]), "fsdp", axis=2, tiled=True)
        wk, wv = wkv[0], wkv[1]
    sinks_here = lax.dynamic_slice_in_dim(sinks_f, seq_index * heads_here, heads_here, 0)
    sink_grid = sinks_here.reshape(kv_here, group)

    rows_f = rows_x.astype(F32)
    unit_rows = rows_f * rms_scale(rows_f)
    normed_rows = (unit_rows * attn_gain_f).astype(BF)
    cosine_values, sine_values = rope_tables(jnp.arange(length, dtype=jnp.int32))
    query = apply_rotary(
        dot(normed_rows, wq, 1, 0) + q_bias, cosine_values, sine_values, 1.0
    ).astype(BF)
    keys = apply_rotary(
        dot(normed_rows, wk, 1, 0) + k_bias, cosine_values, sine_values, 1.0
    ).astype(BF)
    values = (dot(normed_rows, wv, 1, 0) + v_bias).astype(BF)
    doc_row = lax.dynamic_slice_in_dim(doc_lengths, fsdp_index, 1, 0)[0]
    allowed = window_mask(doc_row, block_count, block_rows)
    query_grid = query.reshape(block_count, block_rows, kv_here, group, HEAD_DIM)
    key_all = with_previous(keys.reshape(block_count, block_rows, kv_here, HEAD_DIM))
    value_all = with_previous(values.reshape(block_count, block_rows, kv_here, HEAD_DIM))
    scores = masked_scores(query_grid, key_all, allowed)
    sink_col = sink_grid[None, :, :, None]
    top_score = jnp.maximum(jnp.max(scores, axis=-1), sink_col)
    exp_scores = jnp.exp(scores - top_score[..., None])
    denominator = jnp.sum(exp_scores, axis=-1) + jnp.exp(sink_col - top_score)
    log_total = top_score + jnp.log(denominator)
    probabilities = exp_scores / denominator[..., None]
    heads = jnp.einsum(
        "nhgqk,nkhd->nqhgd", probabilities.astype(BF), value_all, preferred_element_type=F32
    )
    heads = heads.reshape(length, q_width).astype(BF)
    attn_sum = scatter_seq(dot(heads, wo, 1, 0).astype(BF))

    resid_in = layer_input[0].astype(F32)
    resid_mid = resid_in + attn_sum.astype(F32) + out_bias_f
    norm_two = rms_scale(resid_mid)
    unit_mid = resid_mid * norm_two
    normed_mid = (unit_mid * ffn_gain_f).astype(BF)
    logits = dot(normed_mid, router_t, 1, 1) + router_bias_f
    gates = jax.nn.softmax(jnp.where(member_here, logits, -1e30), axis=-1)
    gates = jnp.where(member_here, gates, 0.0)
    gate_high, gate_low = split_low(gates)
    mid_packed = jnp.concatenate(
        [
            normed_mid,
            gate_high,
            gate_low,
            jnp.zeros((tokens_here, padded - width - 2 * expert_count), BF),
        ],
        axis=1,
    )
    mid_rows = gather_seq(mid_packed)

    expert_lane = (jnp.arange(expert_count, dtype=jnp.int32) == seq_index).astype(F32)
    member_row = dot(cot_rows[:, width : width + expert_count].astype(F32), expert_lane[:, None], 1, 0)[:, 0] > 0.5
    slot = jnp.cumsum(member_row.astype(jnp.int32)) - 1
    select = (
        (jnp.arange(capacity, dtype=jnp.int32)[:, None] == slot[None, :]) & member_row[None, :]
    ).astype(BF)
    cot_arrived = gather_fsdp(dot(select, cot_rows, 1, 0).astype(BF))[:, :width]
    arrived = gather_fsdp(dot(select, mid_rows, 1, 0).astype(BF))
    tail = arrived[:, width:].astype(F32)
    gate_col = jnp.sum(
        (tail[:, :expert_count] + tail[:, expert_count : 2 * expert_count]) * expert_lane,
        axis=1,
        keepdims=True,
    )
    expert_rows = arrived[:, :width]
    gate_w, up_w, down_w = expert_gate_up[0, 0], expert_gate_up[0, 1], expert_down[0]
    gate_pre = dot(expert_rows, gate_w, 1, 0) + expert_gate_up_bias[0, 0].astype(F32)
    up_pre = dot(expert_rows, up_w, 1, 0) + expert_gate_up_bias[0, 1].astype(F32)
    hidden_f, glu_back = jax.vjp(swiglu, gate_pre, up_pre)
    hidden = hidden_f.astype(BF).astype(F32)
    hidden_gated = (hidden * gate_col).astype(BF)
    mix_part = dot(hidden_gated, down_w, 1, 0).astype(BF)
    grad_hidden = dot(cot_arrived, down_w, 1, 1)
    gate_grad_part = jnp.sum(hidden * grad_hidden, axis=1)
    grad_gate_pre, grad_up_pre = glu_back(grad_hidden * gate_col)
    grad_gate_low = grad_gate_pre.astype(BF)
    grad_up_low = grad_up_pre.astype(BF)
    row_part = (dot(grad_gate_low, gate_w, 1, 1) + dot(grad_up_low, up_w, 1, 1)).astype(BF)
    down_grad = dot(hidden_gated, cot_arrived, 0, 0)
    gate_up_grad = jnp.stack(
        [dot(expert_rows, grad_gate_low, 0, 0), dot(expert_rows, grad_up_low, 0, 0)]
    )
    gate_up_bias_grad = jnp.stack(
        [jnp.sum(grad_gate_low.astype(F32), axis=0), jnp.sum(grad_up_low.astype(F32), axis=0)]
    )

    row_sum = scatter_fsdp(row_part)
    gate_grad = scatter_fsdp(gate_grad_part)
    grad_high, grad_low = split_low(gate_grad[:, None] * expert_lane)
    back_packed = jnp.concatenate(
        [
            row_sum,
            grad_high,
            grad_low,
            jnp.zeros((capacity, padded - width - 2 * expert_count), BF),
        ],
        axis=1,
    )
    back = scatter_seq(dot(select, back_packed, 0, 0).astype(BF))
    mix_sum = scatter_fsdp(mix_part)
    mixture = scatter_seq(dot(select, mix_sum, 0, 0).astype(BF)).astype(F32)
    mixture = mixture + dot(gates, down_bias_f, 1, 0, EXACT)
    layer_output = (resid_mid + mixture).astype(BF)[None]

    back_tail = back[:, width:].astype(F32)
    cot_f = cot_here.astype(F32)
    grad_gates = (
        back_tail[:, :expert_count]
        + back_tail[:, expert_count : 2 * expert_count]
        + dot(cot_f, down_bias_f, 1, 1, EXACT)
    )
    mean_gate = jnp.sum(gates * grad_gates, axis=-1, keepdims=True)
    grad_logits = gates * (grad_gates - mean_gate)
    router_grad_t = dot(grad_logits, normed_mid.astype(F32), 0, 0, EXACT)
    router_bias_grad = jnp.sum(grad_logits, axis=0)
    down_bias_grad = dot(gates, cot_f, 0, 0, EXACT)
    grad_normed_mid = back[:, :width].astype(F32) + dot(grad_logits, router_t.astype(F32), 1, 0, EXACT)
    ffn_gain_grad = jnp.sum(grad_normed_mid * unit_mid, axis=0)
    grad_unit_mid = grad_normed_mid * ffn_gain_f
    grad_mid = (
        norm_two
        * (grad_unit_mid - unit_mid * jnp.mean(grad_unit_mid * unit_mid, axis=-1, keepdims=True))
        + cot_f
    )
    grad_attn = grad_mid.astype(BF)
    out_bias_grad = jnp.sum(grad_attn.astype(F32), axis=0)

    attn_rows = gather_seq(grad_attn)
    out_w_part = dot(heads, attn_rows, 0, 0)
    grad_heads = dot(attn_rows, wo, 1, 1).astype(BF)
    grad_heads_grid = grad_heads.reshape(query_grid.shape)
    probs_again = jnp.exp(masked_scores(query_grid, key_all, allowed) - log_total[..., None])
    sink_prob = jnp.exp(sink_col - log_total)
    grad_probs = jnp.einsum(
        "nqhgd,nkhd->nhgqk", grad_heads_grid, value_all, preferred_element_type=F32
    )
    row_delta = jnp.sum(probs_again * grad_probs, axis=-1)
    grad_scores = (probs_again * (grad_probs - row_delta[..., None])).astype(BF)
    sink_here_grad = -jnp.sum(sink_prob * row_delta, axis=(0, 3)).reshape(heads_here)
    grad_query = (
        jnp.einsum("nhgqk,nkhd->nqhgd", grad_scores, key_all, preferred_element_type=F32) * 0.125
    ).reshape(length, q_width)

    def to_owner(grad_all):
        own = grad_all[:, block_rows:]
        later = grad_all[1:, :block_rows]
        later = jnp.concatenate([later, jnp.zeros_like(own[:1])], axis=0)
        return (own + later).reshape(length, kv_width)

    grad_key = to_owner(
        jnp.einsum("nhgqk,nqhgd->nkhd", grad_scores, query_grid, preferred_element_type=F32) * 0.125
    )
    grad_value = to_owner(
        jnp.einsum(
            "nhgqk,nqhgd->nkhd",
            probs_again.astype(BF),
            grad_heads_grid,
            preferred_element_type=F32,
        )
    )
    grad_query_lin = apply_rotary(grad_query, cosine_values, sine_values, -1.0).astype(BF)
    grad_key_lin = apply_rotary(grad_key, cosine_values, sine_values, -1.0).astype(BF)
    grad_value_lin = grad_value.astype(BF)
    normed_part = (
        dot(grad_query_lin, wq, 1, 1) + dot(grad_key_lin, wk, 1, 1) + dot(grad_value_lin, wv, 1, 1)
    )
    grad_normed_in = scatter_seq(normed_part.astype(BF)).astype(F32)
    query_w_part = dot(grad_query_lin, normed_rows, 0, 0)
    key_w_part = dot(grad_key_lin, normed_rows, 0, 0)
    value_w_part = dot(grad_value_lin, normed_rows, 0, 0)
    query_b_part = jnp.sum(grad_query_lin.astype(F32), axis=0)
    key_b_part = jnp.sum(grad_key_lin.astype(F32), axis=0)
    value_b_part = jnp.sum(grad_value_lin.astype(F32), axis=0)
    attn_gain_grad = jnp.sum(normed_part * unit_rows, axis=0)

    resid_scale = rms_scale(resid_in)
    unit_in = resid_in * resid_scale
    grad_unit_in = grad_normed_in * attn_gain_f
    input_grad = (
        resid_scale
        * (grad_unit_in - unit_in * jnp.mean(grad_unit_in * unit_in, axis=-1, keepdims=True))
        + grad_mid
    )

    query_w_own = scatter_fsdp(query_w_part).T
    out_w_own = scatter_fsdp(out_w_part)
    query_b_own = scatter_fsdp(query_b_part)
    if shared_kv:

        def whole_sum(part_grad, head_axis_rows):
            whole = jnp.zeros((KEY_VALUE_HEADS * HEAD_DIM,) + part_grad.shape[1:], F32)
            whole = lax.dynamic_update_slice_in_dim(whole, part_grad, kv_head * HEAD_DIM, 0)
            return lax.psum_scatter(whole, ("seq", "fsdp"), scatter_dimension=0, tiled=True)

        key_w_own = whole_sum(key_w_part, True).T
        value_w_own = whole_sum(value_w_part, True).T
        key_b_own, value_b_own = whole_sum(key_b_part, False), whole_sum(value_b_part, False)
    else:
        key_w_own = scatter_fsdp(key_w_part).T
        value_w_own = scatter_fsdp(value_w_part).T
        key_b_own, value_b_own = scatter_fsdp(key_b_part), scatter_fsdp(value_b_part)

    sink_all_grad = lax.dynamic_update_slice_in_dim(
        jnp.zeros((QUERY_HEADS,), F32), sink_here_grad, seq_index * heads_here, 0
    )
    tiny_grad = jnp.concatenate([sink_all_grad, router_bias_grad])
    tiny_grad = jnp.concatenate([tiny_grad, jnp.zeros((width - tiny_grad.shape[0],), F32)])
    small_grad = jnp.concatenate(
        [
            attn_gain_grad[None],
            out_bias_grad[None],
            ffn_gain_grad[None],
            tiny_grad[None],
            down_bias_grad,
            router_grad_t,
        ],
        axis=0,
    )
    small_sum = lax.psum(small_grad, ("seq", "fsdp"))

    def own_part(whole_array, axis_number):
        piece_size = whole_array.shape[axis_number] // fsdp_count
        return lax.dynamic_slice_in_dim(
            whole_array, fsdp_index * piece_size, piece_size, axis_number
        )

    small_own = own_part(small_sum, 1)
    return (
        layer_output,
        input_grad[None],
        small_own[0],
        query_w_own,
        query_b_own,
        key_w_own,
        key_b_own,
        value_w_own,
        value_b_own,
        own_part(small_sum[3, :QUERY_HEADS], 0),
        out_w_own,
        small_own[1],
        small_own[2],
        small_own[4 + expert_count :].T,
        own_part(small_sum[3, QUERY_HEADS : QUERY_HEADS + expert_count], 0),
        gate_up_grad[None],
        gate_up_bias_grad[None],
        down_grad[None],
        small_own[4 : 4 + expert_count],
    )


def solution(mesh):
    return jax.shard_map(
        per_device,
        mesh=mesh,
        in_specs=(
            P("fsdp", "seq", None),
            P("fsdp"),
            P(None, ("seq", "fsdp")),
            P(("seq", "fsdp")),
            P(None, ("seq", "fsdp")),
            P(("seq", "fsdp")),
            P(None, ("seq", "fsdp")),
            P(("seq", "fsdp")),
            P("fsdp"),
            P(("seq", "fsdp"), None),
            P("fsdp"),
            P("fsdp"),
            P("fsdp", None),
            P("fsdp"),
            P("seq", None, None, "fsdp"),
            P("seq", None, "fsdp"),
            P("seq", "fsdp", None),
            P(None, "fsdp"),
            P("fsdp", "seq", None),
            P(),
            P("fsdp", "seq", None),
        ),
        out_specs=(
            P("fsdp", "seq", None),
            P("fsdp", "seq", None),
            P("fsdp"),
            P(None, ("seq", "fsdp")),
            P(("seq", "fsdp")),
            P(None, ("seq", "fsdp")),
            P(("seq", "fsdp")),
            P(None, ("seq", "fsdp")),
            P(("seq", "fsdp")),
            P("fsdp"),
            P(("seq", "fsdp"), None),
            P("fsdp"),
            P("fsdp"),
            P("fsdp", None),
            P("fsdp"),
            P("seq", None, None, "fsdp"),
            P("seq", None, "fsdp"),
            P("seq", "fsdp", None),
            P(None, "fsdp"),
        ),
        check_vma=False,
    )
```

```python
import jax
import jax.numpy as jnp
from jax import lax
from jax.sharding import PartitionSpec as P

QUERY_HEADS = 64
KEY_VALUE_HEADS = 8
HEAD_DIM = 64
WINDOW_LENGTH = 128


ROPE_BASE = 150000.0
NORM_EPS = 1e-05
GLU_ALPHA = 1.702
GLU_LIMIT = 7.0
EXACT = lax.Precision.HIGHEST
BF = jnp.bfloat16
F32 = jnp.float32


def rms_scale(values):
    return lax.rsqrt(jnp.mean(values * values, axis=-1, keepdims=True) + NORM_EPS)


def rope_tables(positions):
    frequency = ROPE_BASE ** (-jnp.arange(HEAD_DIM // 2, dtype=jnp.float32) * 2.0 / HEAD_DIM)
    angles = positions.astype(jnp.float32)[:, None] * frequency[None, :]
    return (jnp.cos(angles), jnp.sin(angles))


def apply_rotary(values, cosine_values, sine_values, direction):
    half_size = HEAD_DIM // 2
    rows, width = values.shape
    grid = values.reshape(rows, width // HEAD_DIM, HEAD_DIM)
    first_half = grid[..., :half_size]
    second = grid[..., half_size:]
    cosine_b = cosine_values[:, None, :]
    sine_b = direction * sine_values[:, None, :]
    turned = jnp.concatenate(
        [first_half * cosine_b - second * sine_b, second * cosine_b + first_half * sine_b], axis=-1
    )
    return turned.reshape(rows, width)


def swiglu(gate_pre, up_pre):
    gate_soft = GLU_LIMIT - jax.nn.softplus(GLU_LIMIT - gate_pre)
    up_soft = GLU_LIMIT * jnp.tanh(up_pre / GLU_LIMIT)
    return (up_soft + 1.0) * gate_soft * jax.nn.sigmoid(GLU_ALPHA * gate_soft)


def dot(left, right, left_dim, right_dim, precision=None):
    return lax.dot_general(
        left,
        right,
        (((left_dim,), (right_dim,)), ((), ())),
        precision=precision,
        preferred_element_type=jnp.float32,
    )


def tie(*arrays):
    return lax.optimization_barrier(arrays)


class Line:
    def __init__(self):
        index = lax.axis_index("seq")
        self.place, self.side = index // 2, index % 2
        at_low, at_high = self.place == 0, self.place == 3
        self.at_end = at_low | at_high
        self.at_low = at_low
        place = self.place
        self.order = [
            place,
            jnp.where(at_low, 1, place - 1),
            jnp.where(at_low, 2, jnp.where(at_high, 1, place + 1)),
            jnp.where(place < 2, 3, 0),
        ]

    @staticmethod
    def along(block, moves):
        route = [(2 * i + k, 2 * j + k) for i, j in moves for k in range(2)]
        return lax.ppermute(block, "seq", route)

    @staticmethod
    def across(block):
        return lax.ppermute(block, "seq", [(i, i ^ 1) for i in range(8)])

    def as_pair(self, own, other):
        first = jnp.where(self.side == 0, own, other)
        second = jnp.where(self.side == 0, other, own)
        return jnp.concatenate([first, second], axis=0)

    def gather(self, block):
        up, down, side_0 = (
            self.along(block, [(0, 1), (1, 2), (2, 3)]),
            self.along(block, [(1, 0), (2, 1), (3, 2)]),
            self.across(block),
        )
        up, down, side_0 = tie(up, down, side_0)
        near = jnp.where(self.at_low, down, up)
        up_2, down_2, side_1 = (
            self.along(up, [(1, 2), (2, 3)]),
            self.along(down, [(2, 1), (1, 0)]),
            self.across(near),
        )
        up_2, down_2, side_1, down = tie(up_2, down_2, side_1, down)
        second = up_2 + down_2
        far = jnp.where(self.at_end, second, down)
        third, side_2 = self.along(second, [(2, 3), (1, 0)]), self.across(far)
        third, side_2, second = tie(third, side_2, second)
        last = jnp.where(self.at_end, third, second)
        side_3 = self.across(last)
        return [
            self.as_pair(block, side_0),
            self.as_pair(near, side_1),
            self.as_pair(far, side_2),
            self.as_pair(last, side_3),
        ]

    def halves(self, pair):
        rows = pair.shape[0] // 2
        own = lax.dynamic_slice_in_dim(pair, self.side * rows, rows, 0)
        other = lax.dynamic_slice_in_dim(pair, (1 - self.side) * rows, rows, 0)
        return own, other

    def scatter(self, pairs):
        own, other = zip(*(self.halves(pair) for pair in pairs))
        side_3 = self.across(other[3])
        sum_3 = own[3].astype(F32) + side_3.astype(F32)
        sent, later = tie(sum_3.astype(BF), other[2])
        step_1, side_2 = self.along(sent, [(0, 1), (3, 2)]), self.across(later)
        step_1, side_2, later = tie(step_1, side_2, other[1])
        sum_2 = own[2].astype(F32) + side_2.astype(F32)
        sent = jnp.where(self.at_end, sum_2, sum_3 + step_1.astype(F32)).astype(BF)
        up, down, side_1 = (
            self.along(sent, [(0, 1), (1, 2)]),
            self.along(sent, [(3, 2), (2, 1)]),
            self.across(later),
        )
        up, down, side_1, later = tie(up, down, side_1, other[0])
        sum_1 = own[1].astype(F32) + side_1.astype(F32)
        sent_up = jnp.where(self.at_low, sum_1, sum_2 + up.astype(F32)).astype(BF)
        sent_down = (sum_1 + down.astype(F32)).astype(BF)
        up, down, side_0 = (
            self.along(sent_up, [(0, 1), (1, 2), (2, 3)]),
            self.along(sent_down, [(1, 0), (2, 1), (3, 2)]),
            self.across(later),
        )
        return (
            own[0].astype(F32) + side_0.astype(F32) + up.astype(F32) + down.astype(F32)
        )


class Whole:
    def __init__(self):
        self.order = [jnp.int32(0)]

    def gather(self, block):
        return [gather_seq(block)]

    def scatter(self, pairs):
        return scatter_seq(pairs[0]).astype(F32)


def gather_seq(block):
    return lax.all_gather(block, "seq", axis=0, tiled=True)


def scatter_seq(partial_rows):
    return lax.psum_scatter(partial_rows, "seq", scatter_dimension=0, tiled=True)


def scatter_fsdp(partial_rows):
    return lax.psum_scatter(partial_rows, "fsdp", scatter_dimension=0, tiled=True)


def to_core(block):
    return lax.ppermute(block, "fsdp", [(i, i ^ 1) for i in range(4)])


def to_chip(block):
    return lax.ppermute(block, "fsdp", [(i, i ^ 2) for i in range(4)])


def split_low(values):
    high = values.astype(BF)
    low = (values - high.astype(F32)).astype(BF)
    return high, low


def with_previous(blocks):
    before = jnp.concatenate([jnp.zeros_like(blocks[:1]), blocks[:-1]], axis=0)
    return jnp.concatenate([before, blocks], axis=1)


def masked_scores(query_grid, key_all, allowed):
    scores = (
        jnp.einsum("nqhgd,nkhd->nhgqk", query_grid, key_all, preferred_element_type=F32) * 0.125
    )
    return jnp.where(allowed[:, None, None], scores, -1e30)


def window_mask(doc_row, block_count, block_rows):
    doc_ends = jnp.cumsum(doc_row)
    starts = jnp.arange(block_count, dtype=jnp.int32)[:, None] * block_rows
    positions = starts + jnp.arange(block_rows, dtype=jnp.int32)[None, :]
    key_pos = starts - block_rows + jnp.arange(2 * block_rows, dtype=jnp.int32)[None, :]
    query_doc = jnp.sum((positions[:, :, None] >= doc_ends).astype(jnp.int32), axis=2)
    key_doc = jnp.sum((key_pos[:, :, None] >= doc_ends).astype(jnp.int32), axis=2)
    offset = positions[:, :, None] - key_pos[:, None, :]
    inside = (key_pos[:, None, :] >= 0) & (offset >= 0) & (offset <= WINDOW_LENGTH)
    return inside & (query_doc[:, :, None] == key_doc[:, None, :])


def per_device(
    layer_input,
    attn_gain,
    query_matrix,
    query_bias_vector,
    key_matrix,
    key_bias_vector,
    value_matrix,
    value_bias_vector,
    sink_logit_values,
    output_matrix,
    output_bias_vector,
    ffn_gain,
    router_weight,
    router_bias,
    expert_gate_up,
    expert_gate_up_bias,
    expert_down,
    expert_down_bias,
    route_ids,
    doc_lengths,
    out_cotangent,
):
    seq_count = lax.axis_size("seq")
    fsdp_count = lax.axis_size("fsdp")
    seq_index = lax.axis_index("seq")
    fsdp_index = lax.axis_index("fsdp")
    tokens_here, width = layer_input.shape[1:]
    choose_count = route_ids.shape[2]
    expert_count = seq_count
    block_rows = WINDOW_LENGTH
    length = seq_count * tokens_here
    block_count = length // block_rows
    block_capacity = max(2, tokens_here * choose_count * 5 // (4 * expert_count))
    capacity = block_capacity * seq_count
    padded = -(-(width + 2 * expert_count) // 128) * 128
    heads_here = QUERY_HEADS // seq_count
    kv_here = max(1, KEY_VALUE_HEADS // seq_count)
    group = heads_here // kv_here
    shared_kv = seq_count > KEY_VALUE_HEADS
    q_width, kv_width = heads_here * HEAD_DIM, kv_here * HEAD_DIM

    line = Line() if seq_count == 8 else Whole()
    chunk = length // len(line.order)
    starts = [place * chunk for place in line.order]

    rows_x = jnp.zeros((length, width), BF)
    for start, pair in zip(starts, line.gather(layer_input[0])):
        rows_x = lax.dynamic_update_slice_in_dim(rows_x, pair, start, 0)
    member_here = jnp.any(
        route_ids[0][:, :, None] == jnp.arange(expert_count, dtype=jnp.int32), axis=1
    )
    cot_here = out_cotangent[0]
    cot_packed = jnp.concatenate(
        [
            cot_here,
            member_here.astype(BF),
            jnp.zeros((tokens_here, padded - width - expert_count), BF),
        ],
        axis=1,
    )
    cot_rows = gather_seq(cot_packed)

    part = attn_gain.shape[0]
    q_part, kv_part = query_bias_vector.shape[0], key_bias_vector.shape[0]
    tiny = jnp.concatenate(
        [sink_logit_values, router_bias, query_bias_vector, key_bias_vector, value_bias_vector]
    )
    tiny = jnp.concatenate([tiny, jnp.zeros((part - tiny.shape[0],), BF)])
    small = jnp.concatenate(
        [
            attn_gain[None],
            ffn_gain[None],
            output_bias_vector[None],
            tiny[None],
            expert_down_bias,
            router_weight.T,
        ],
        axis=0,
    )
    small_all = lax.all_gather(small, "fsdp", axis=0)
    wide = jnp.swapaxes(small_all, 0, 1).reshape(small.shape[0], width).astype(F32)
    attn_gain_f, ffn_gain_f, out_bias_f = wide[0], wide[1], wide[2]
    down_bias_f = wide[4 : 4 + expert_count]
    router_t = wide[4 + expert_count :].astype(BF)
    tiny_all = small_all[:, 3]
    places = [0]
    for piece in (sink_logit_values, router_bias, query_bias_vector, key_bias_vector, value_bias_vector):
        places.append(places[-1] + piece.shape[0])
    sinks_f, router_bias_f, q_bias, k_bias, v_bias = (
        tiny_all[:, a:b].reshape(-1).astype(F32) for a, b in zip(places[:-1], places[1:])
    )
    wq = lax.all_gather(query_matrix, "fsdp", axis=1, tiled=True)
    wo = lax.all_gather(output_matrix, "fsdp", axis=0, tiled=True)
    if shared_kv:
        share = seq_count // KEY_VALUE_HEADS
        kv_head = seq_index // share

        def own_head(piece, axis):
            whole = lax.all_gather(piece, ("seq", "fsdp"), axis=axis, tiled=True)
            return lax.dynamic_slice_in_dim(whole, kv_head * HEAD_DIM, HEAD_DIM, axis)

        wk, wv = own_head(key_matrix, 1), own_head(value_matrix, 1)
        k_bias = own_head(key_bias_vector, 0).astype(F32)
        v_bias = own_head(value_bias_vector, 0).astype(F32)
    else:
        wkv = lax.all_gather(jnp.stack([key_matrix, value_matrix]), "fsdp", axis=2, tiled=True)
        wk, wv = wkv[0], wkv[1]
    sinks_here = lax.dynamic_slice_in_dim(sinks_f, seq_index * heads_here, heads_here, 0)
    sink_grid = sinks_here.reshape(kv_here, group)

    rows_f = rows_x.astype(F32)
    unit_rows = rows_f * rms_scale(rows_f)
    normed_rows = (unit_rows * attn_gain_f).astype(BF)
    cosine_values, sine_values = rope_tables(jnp.arange(length, dtype=jnp.int32))
    query = apply_rotary(
        dot(normed_rows, wq, 1, 0) + q_bias, cosine_values, sine_values, 1.0
    ).astype(BF)
    keys = apply_rotary(
        dot(normed_rows, wk, 1, 0) + k_bias, cosine_values, sine_values, 1.0
    ).astype(BF)
    values = (dot(normed_rows, wv, 1, 0) + v_bias).astype(BF)
    doc_row = lax.dynamic_slice_in_dim(doc_lengths, fsdp_index, 1, 0)[0]
    allowed = window_mask(doc_row, block_count, block_rows)
    query_grid = query.reshape(block_count, block_rows, kv_here, group, HEAD_DIM)
    key_all = with_previous(keys.reshape(block_count, block_rows, kv_here, HEAD_DIM))
    value_all = with_previous(values.reshape(block_count, block_rows, kv_here, HEAD_DIM))
    scores = masked_scores(query_grid, key_all, allowed)
    sink_col = sink_grid[None, :, :, None]
    top_score = jnp.maximum(jnp.max(scores, axis=-1), sink_col)
    exp_scores = jnp.exp(scores - top_score[..., None])
    denominator = jnp.sum(exp_scores, axis=-1) + jnp.exp(sink_col - top_score)
    log_total = top_score + jnp.log(denominator)
    probabilities = exp_scores / denominator[..., None]
    heads = jnp.einsum(
        "nhgqk,nkhd->nqhgd", probabilities.astype(BF), value_all, preferred_element_type=F32
    )
    heads = heads.reshape(length, q_width).astype(BF)

    def taken(rows, start):
        return lax.dynamic_slice_in_dim(rows, start, chunk, 0)

    attn_sum = line.scatter([dot(taken(heads, start), wo, 1, 0).astype(BF) for start in starts])

    resid_in = layer_input[0].astype(F32)
    resid_mid = resid_in + attn_sum + out_bias_f
    norm_two = rms_scale(resid_mid)
    unit_mid = resid_mid * norm_two
    normed_mid = (unit_mid * ffn_gain_f).astype(BF)
    logits = dot(normed_mid, router_t, 1, 1) + router_bias_f
    gates = jax.nn.softmax(jnp.where(member_here, logits, -1e30), axis=-1)
    gates = jnp.where(member_here, gates, 0.0)
    gate_high, gate_low = split_low(gates)
    mid_packed = jnp.concatenate(
        [
            normed_mid,
            gate_high,
            gate_low,
            jnp.zeros((tokens_here, padded - width - 2 * expert_count), BF),
        ],
        axis=1,
    )
    expert_lane = (jnp.arange(expert_count, dtype=jnp.int32) == seq_index).astype(F32)
    member_rows = cot_rows[:, width : width + expert_count].astype(F32)
    member_row = jnp.sum(member_rows * expert_lane, axis=1) > 0.5
    selects = []
    for start in starts:
        member = taken(member_row, start).reshape(-1, tokens_here)
        slot = jnp.cumsum(member.astype(jnp.int32), axis=1) - 1
        slot = slot + (jnp.arange(member.shape[0], dtype=jnp.int32) * block_capacity)[:, None]
        slot = jnp.where(member, slot, -1).reshape(-1)
        slots = block_capacity * (chunk // tokens_here)
        selects.append((jnp.arange(slots, dtype=jnp.int32)[:, None] == slot[None, :]).astype(BF))
    cot_own = jnp.concatenate(
        [
            dot(select, taken(cot_rows, start)[:, :width], 1, 0).astype(BF)
            for select, start in zip(selects, starts)
        ]
    )
    cot_core, cot_chip = to_core(cot_own), to_chip(cot_own)
    cot_near = jnp.concatenate([cot_own, cot_core])
    cot_far = jnp.concatenate([cot_chip, to_core(cot_chip)])
    own_parts, core_parts, chip_parts, both_parts = [], [], [], []
    for select, pair in zip(selects, line.gather(mid_packed)):
        rows = dot(select, pair, 1, 0).astype(BF)
        rows_chip = to_chip(rows)
        own_parts.append(rows)
        core_parts.append(to_core(rows))
        chip_parts.append(rows_chip)
        both_parts.append(to_core(rows_chip))
    near = jnp.concatenate(own_parts + core_parts)
    far = jnp.concatenate(chip_parts + both_parts)
    gate_w, up_w, down_w = expert_gate_up[0, 0], expert_gate_up[0, 1], expert_down[0]

    def expert(arrived, cot_arrived):
        tail = arrived[:, width:].astype(F32)
        gate_col = jnp.sum(
            (tail[:, :expert_count] + tail[:, expert_count : 2 * expert_count]) * expert_lane,
            axis=1,
            keepdims=True,
        )
        expert_rows = arrived[:, :width]
        gate_pre = dot(expert_rows, gate_w, 1, 0) + expert_gate_up_bias[0, 0].astype(F32)
        up_pre = dot(expert_rows, up_w, 1, 0) + expert_gate_up_bias[0, 1].astype(F32)
        hidden_f, glu_back = jax.vjp(swiglu, gate_pre, up_pre)
        hidden = hidden_f.astype(BF).astype(F32)
        hidden_gated = (hidden * gate_col).astype(BF)
        grad_hidden = dot(cot_arrived, down_w, 1, 1)
        gate_grad_part = jnp.sum(hidden * grad_hidden, axis=1)
        grad_gate_pre, grad_up_pre = glu_back(grad_hidden * gate_col)
        grad_gate_low = grad_gate_pre.astype(BF)
        grad_up_low = grad_up_pre.astype(BF)
        row_part = (dot(grad_gate_low, gate_w, 1, 1) + dot(grad_up_low, up_w, 1, 1)).astype(BF)
        return expert_rows, hidden_gated, grad_gate_low, grad_up_low, gate_grad_part, row_part

    rows_n, hidden_n, gate_n, up_n, gate_part_n, row_part_n = expert(near, cot_near)
    rows_o, hidden_o, gate_o, up_o, gate_part_o, row_part_o = expert(far, cot_far)

    half = capacity

    def return_rows(near_part, far_part):
        from_core_near, from_core_far = to_core(near_part[half:]), to_core(far_part[half:])
        near_sum = near_part[:half].astype(F32) + from_core_near.astype(F32)
        far_sum = far_part[:half].astype(F32) + from_core_far.astype(F32)
        far_sum = far_sum.astype(far_part.dtype)
        sums = []
        for at in reversed(range(len(starts))):
            first = at * slots
            arrived = to_chip(far_sum[first : first + slots])
            sums.append(near_sum[first : first + slots] + arrived.astype(F32))
        return sums[::-1]

    row_sums = return_rows(row_part_n, row_part_o)
    gate_sums = return_rows(gate_part_n[:, None], gate_part_o[:, None])
    back_pairs = []
    for select, row_sum, gate_sum in zip(selects, row_sums, gate_sums):
        grad_high, grad_low = split_low(gate_sum * expert_lane)
        back_packed = jnp.concatenate(
            [
                row_sum.astype(BF),
                grad_high,
                grad_low,
                jnp.zeros((slots, padded - width - 2 * expert_count), BF),
            ],
            axis=1,
        )
        back_pairs.append(dot(select, back_packed, 0, 0).astype(BF))
    back = line.scatter(back_pairs)

    mix_sums = return_rows(
        dot(hidden_n, down_w, 1, 0).astype(BF), dot(hidden_o, down_w, 1, 0).astype(BF)
    )
    mix_dense = jnp.zeros((length, width), BF)
    for select, start, mix_sum in zip(selects, starts, mix_sums):
        mix_dense = lax.dynamic_update_slice_in_dim(
            mix_dense, dot(select, mix_sum.astype(BF), 0, 0).astype(BF), start, 0
        )
    mixture = scatter_seq(mix_dense).astype(F32)
    mixture = mixture + dot(gates, down_bias_f, 1, 0, EXACT)
    layer_output = (resid_mid + mixture).astype(BF)[None]
    down_grad = dot(hidden_n, cot_near, 0, 0) + dot(hidden_o, cot_far, 0, 0)
    gate_up_grad = jnp.stack(
        [
            dot(rows_n, gate_n, 0, 0) + dot(rows_o, gate_o, 0, 0),
            dot(rows_n, up_n, 0, 0) + dot(rows_o, up_o, 0, 0),
        ]
    )

    def column_sum(near_part, far_part):
        return jnp.sum(near_part.astype(F32), axis=0) + jnp.sum(far_part.astype(F32), axis=0)

    gate_up_bias_grad = jnp.stack([column_sum(gate_n, gate_o), column_sum(up_n, up_o)])

    back_tail = back[:, width:]
    cot_f = cot_here.astype(F32)
    grad_gates = (
        back_tail[:, :expert_count]
        + back_tail[:, expert_count : 2 * expert_count]
        + dot(cot_f, down_bias_f, 1, 1, EXACT)
    )
    mean_gate = jnp.sum(gates * grad_gates, axis=-1, keepdims=True)
    grad_logits = gates * (grad_gates - mean_gate)
    router_grad_t = dot(grad_logits, normed_mid.astype(F32), 0, 0, EXACT)
    router_bias_grad = jnp.sum(grad_logits, axis=0)
    down_bias_grad = dot(gates, cot_f, 0, 0, EXACT)
    grad_normed_mid = back[:, :width] + dot(grad_logits, router_t.astype(F32), 1, 0, EXACT)
    ffn_gain_grad = jnp.sum(grad_normed_mid * unit_mid, axis=0)
    grad_unit_mid = grad_normed_mid * ffn_gain_f
    grad_mid = (
        norm_two
        * (grad_unit_mid - unit_mid * jnp.mean(grad_unit_mid * unit_mid, axis=-1, keepdims=True))
        + cot_f
    )
    grad_attn = grad_mid.astype(BF)
    out_bias_grad = jnp.sum(grad_attn.astype(F32), axis=0)

    attn_rows = jnp.zeros((length, width), BF)
    for start, pair in zip(starts, line.gather(grad_attn)):
        attn_rows = lax.dynamic_update_slice_in_dim(attn_rows, pair, start, 0)
    out_w_part = dot(heads, attn_rows, 0, 0)
    grad_heads = dot(attn_rows, wo, 1, 1).astype(BF)
    grad_heads_grid = grad_heads.reshape(query_grid.shape)
    probs_again = jnp.exp(masked_scores(query_grid, key_all, allowed) - log_total[..., None])
    sink_prob = jnp.exp(sink_col - log_total)
    grad_probs = jnp.einsum(
        "nqhgd,nkhd->nhgqk", grad_heads_grid, value_all, preferred_element_type=F32
    )
    row_delta = jnp.sum(probs_again * grad_probs, axis=-1)
    grad_scores = (probs_again * (grad_probs - row_delta[..., None])).astype(BF)
    sink_here_grad = -jnp.sum(sink_prob * row_delta, axis=(0, 3)).reshape(heads_here)
    grad_query = (
        jnp.einsum("nhgqk,nkhd->nqhgd", grad_scores, key_all, preferred_element_type=F32) * 0.125
    ).reshape(length, q_width)

    def to_owner(grad_all):
        own = grad_all[:, block_rows:]
        later = grad_all[1:, :block_rows]
        later = jnp.concatenate([later, jnp.zeros_like(own[:1])], axis=0)
        return (own + later).reshape(length, kv_width)

    grad_key = to_owner(
        jnp.einsum("nhgqk,nqhgd->nkhd", grad_scores, query_grid, preferred_element_type=F32) * 0.125
    )
    grad_value = to_owner(
        jnp.einsum(
            "nhgqk,nqhgd->nkhd",
            probs_again.astype(BF),
            grad_heads_grid,
            preferred_element_type=F32,
        )
    )
    grad_query_lin = apply_rotary(grad_query, cosine_values, sine_values, -1.0).astype(BF)
    grad_key_lin = apply_rotary(grad_key, cosine_values, sine_values, -1.0).astype(BF)
    grad_value_lin = grad_value.astype(BF)
    attn_gain_grad = jnp.zeros((width,), F32)
    normed_parts = []
    for start in starts:
        normed_part = (
            dot(taken(grad_query_lin, start), wq, 1, 1)
            + dot(taken(grad_key_lin, start), wk, 1, 1)
            + dot(taken(grad_value_lin, start), wv, 1, 1)
        )
        attn_gain_grad = attn_gain_grad + jnp.sum(normed_part * taken(unit_rows, start), axis=0)
        normed_parts.append(normed_part.astype(BF))
    grad_normed_in = line.scatter(normed_parts)
    query_w_part = dot(grad_query_lin, normed_rows, 0, 0)
    key_w_part = dot(grad_key_lin, normed_rows, 0, 0)
    value_w_part = dot(grad_value_lin, normed_rows, 0, 0)
    query_b_part = jnp.sum(grad_query_lin.astype(F32), axis=0)
    key_b_part = jnp.sum(grad_key_lin.astype(F32), axis=0)
    value_b_part = jnp.sum(grad_value_lin.astype(F32), axis=0)

    resid_scale = rms_scale(resid_in)
    unit_in = resid_in * resid_scale
    grad_unit_in = grad_normed_in * attn_gain_f
    input_grad = (
        resid_scale
        * (grad_unit_in - unit_in * jnp.mean(grad_unit_in * unit_in, axis=-1, keepdims=True))
        + grad_mid
    )

    query_w_own = scatter_fsdp(query_w_part).T
    out_w_own = scatter_fsdp(out_w_part)
    query_b_own = scatter_fsdp(query_b_part)
    if shared_kv:

        def whole_sum(part_grad, head_axis_rows):
            whole = jnp.zeros((KEY_VALUE_HEADS * HEAD_DIM,) + part_grad.shape[1:], F32)
            whole = lax.dynamic_update_slice_in_dim(whole, part_grad, kv_head * HEAD_DIM, 0)
            return lax.psum_scatter(whole, ("seq", "fsdp"), scatter_dimension=0, tiled=True)

        key_w_own = whole_sum(key_w_part, True).T
        value_w_own = whole_sum(value_w_part, True).T
        key_b_own, value_b_own = whole_sum(key_b_part, False), whole_sum(value_b_part, False)
    else:
        key_w_own = scatter_fsdp(key_w_part).T
        value_w_own = scatter_fsdp(value_w_part).T
        key_b_own, value_b_own = scatter_fsdp(key_b_part), scatter_fsdp(value_b_part)

    sink_all_grad = lax.dynamic_update_slice_in_dim(
        jnp.zeros((QUERY_HEADS,), F32), sink_here_grad, seq_index * heads_here, 0
    )
    tiny_grad = jnp.concatenate([sink_all_grad, router_bias_grad])
    tiny_grad = jnp.concatenate([tiny_grad, jnp.zeros((width - tiny_grad.shape[0],), F32)])
    small_grad = jnp.concatenate(
        [
            out_bias_grad[None],
            ffn_gain_grad[None],
            tiny_grad[None],
            down_bias_grad,
            router_grad_t,
        ],
        axis=0,
    )
    small_sum = lax.psum(small_grad, ("seq", "fsdp"))

    def own_part(whole_array, axis_number):
        piece_size = whole_array.shape[axis_number] // fsdp_count
        return lax.dynamic_slice_in_dim(
            whole_array, fsdp_index * piece_size, piece_size, axis_number
        )

    small_own = own_part(small_sum, 1)
    attn_gain_sum = lax.psum(attn_gain_grad, ("seq", "fsdp"))
    return (
        layer_output,
        input_grad[None],
        own_part(attn_gain_sum, 0),
        query_w_own,
        query_b_own,
        key_w_own,
        key_b_own,
        value_w_own,
        value_b_own,
        own_part(small_sum[2, :QUERY_HEADS], 0),
        out_w_own,
        small_own[0],
        small_own[1],
        small_own[3 + expert_count :].T,
        own_part(small_sum[2, QUERY_HEADS : QUERY_HEADS + expert_count], 0),
        gate_up_grad[None],
        gate_up_bias_grad[None],
        down_grad[None],
        small_own[3 : 3 + expert_count],
    )


def solution(mesh):
    return jax.shard_map(
        per_device,
        mesh=mesh,
        in_specs=(
            P("fsdp", "seq", None),
            P("fsdp"),
            P(None, ("seq", "fsdp")),
            P(("seq", "fsdp")),
            P(None, ("seq", "fsdp")),
            P(("seq", "fsdp")),
            P(None, ("seq", "fsdp")),
            P(("seq", "fsdp")),
            P("fsdp"),
            P(("seq", "fsdp"), None),
            P("fsdp"),
            P("fsdp"),
            P("fsdp", None),
            P("fsdp"),
            P("seq", None, None, "fsdp"),
            P("seq", None, "fsdp"),
            P("seq", "fsdp", None),
            P(None, "fsdp"),
            P("fsdp", "seq", None),
            P(),
            P("fsdp", "seq", None),
        ),
        out_specs=(
            P("fsdp", "seq", None),
            P("fsdp", "seq", None),
            P("fsdp"),
            P(None, ("seq", "fsdp")),
            P(("seq", "fsdp")),
            P(None, ("seq", "fsdp")),
            P(("seq", "fsdp")),
            P(None, ("seq", "fsdp")),
            P(("seq", "fsdp")),
            P("fsdp"),
            P(("seq", "fsdp"), None),
            P("fsdp"),
            P("fsdp"),
            P("fsdp", None),
            P("fsdp"),
            P("seq", None, None, "fsdp"),
            P("seq", None, "fsdp"),
            P("seq", "fsdp", None),
            P(None, "fsdp"),
        ),
        check_vma=False,
    )
```

```python
import jax
import jax.numpy as jnp
from jax import lax
from jax.experimental import pallas as pl
from jax.experimental.pallas import tpu as pltpu
from jax.sharding import PartitionSpec as P

QUERY_HEADS = 64
KEY_VALUE_HEADS = 8
HEAD_DIM = 64
WINDOW_LENGTH = 128


ROPE_BASE = 150000.0
NORM_EPS = 1e-05
GLU_ALPHA = 1.702
GLU_LIMIT = 7.0
EXACT = lax.Precision.HIGHEST
BF = jnp.bfloat16
F32 = jnp.float32
VMEM_BYTES = 60 * 2**20


def dot(left, right, left_dim, right_dim, precision=None):
    return lax.dot_general(
        left,
        right,
        (((left_dim,), (right_dim,)), ((), ())),
        precision=precision,
        preferred_element_type=jnp.float32,
    )


def turn_halves(values, cosines, sines):
    rows, width = values.shape
    half = HEAD_DIM // 2
    lane = lax.broadcasted_iota(jnp.int32, (rows, width), 1) % HEAD_DIM
    ahead = pltpu.roll(values, width - half, 1)
    behind = pltpu.roll(values, half, 1)
    other = jnp.where(lane < half, ahead, behind)
    copies = width // cosines.shape[1]
    wide_cos = jnp.concatenate([cosines] * copies, axis=1)
    wide_sin = jnp.concatenate([sines] * copies, axis=1)
    return values * wide_cos + other * wide_sin


def turn_keys(pair, cosines, sines, direction):
    lane = lax.broadcasted_iota(jnp.int32, pair.shape, 1)
    keys = lane < HEAD_DIM
    return turn_halves(pair, jnp.where(keys, cosines, 1.0), jnp.where(keys, direction * sines, 0.0))


def stack_heads(rows):
    return jnp.concatenate(
        [rows[:, at : at + HEAD_DIM] for at in range(0, rows.shape[1], HEAD_DIM)], axis=0
    )


def unstack_heads(stacked, rows):
    return jnp.concatenate(
        [stacked[at : at + rows] for at in range(0, stacked.shape[0], rows)], axis=1
    )


def block_probs(block, ends_ref, sinks_ref, queries, keys, rows):
    heads = queries.shape[0] // rows
    spread = lax.broadcasted_iota(jnp.int32, (rows, 2 * rows), 0)
    key_at = lax.broadcasted_iota(jnp.int32, (rows, 2 * rows), 1)
    position = block * rows + spread
    key_pos = (block - 1) * rows + key_at
    offset = position - key_pos
    allowed = (key_pos >= 0) & (offset >= 0) & (offset <= WINDOW_LENGTH)
    for document in range(ends_ref.shape[0]):
        end = ends_ref[document]
        allowed = allowed & ((position >= end) == (key_pos >= end))
    scores = dot(queries, keys, 1, 1) * 0.125
    scores = scores.reshape(heads, rows, 2 * rows)
    scores = jnp.where(allowed[None], scores, -1e30)
    head = lax.broadcasted_iota(jnp.int32, (heads, rows, 1), 0)
    sink = jnp.zeros((heads, rows, 1), F32)
    for at in range(heads):
        sink = jnp.where(head == at, sinks_ref[at], sink)
    top = jnp.maximum(jnp.max(scores, axis=-1, keepdims=True), sink)
    weights = jnp.exp(scores - top)
    sink_weight = jnp.exp(sink - top)
    inverse = 1.0 / (jnp.sum(weights, axis=-1, keepdims=True) + sink_weight)
    probs = (weights * inverse).reshape(heads * rows, 2 * rows)
    return probs, sink_weight * inverse


def attend_kernel(
    ends_ref, sinks_ref, lin_ref, before_ref, cos_ref, sin_ref, cos_before_ref, sin_before_ref,
    turned_ref, heads_ref,
):
    block = pl.program_id(0)
    rows = lin_ref.shape[0]
    wide = lin_ref.shape[1] - 2 * HEAD_DIM
    cosines, sines = cos_ref[...], sin_ref[...]
    queries = turn_halves(lin_ref[:, :wide], cosines, sines).astype(BF)
    own = turn_keys(lin_ref[:, wide:], cosines, sines, 1.0).astype(BF)
    before = turn_keys(before_ref[...], cos_before_ref[...], sin_before_ref[...], 1.0).astype(BF)
    turned_ref[:, :wide] = queries
    turned_ref[:, wide:] = own
    pair = jnp.concatenate([before, own], axis=0)
    probs, _ = block_probs(
        block, ends_ref, sinks_ref, stack_heads(queries), pair[:, :HEAD_DIM], rows
    )
    mixed = dot(probs.astype(BF), pair[:, HEAD_DIM:], 1, 0)
    heads_ref[...] = unstack_heads(mixed.astype(BF), rows)


def attend(lin, cosines, sines, doc_ends, sinks):
    length, full = lin.shape
    rows = WINDOW_LENGTH
    wide = full - 2 * HEAD_DIM
    pair_at = wide // (2 * HEAD_DIM)
    smem = pl.BlockSpec(memory_space=pltpu.SMEM)
    here = lambda block: (block, 0)
    previous = lambda block: (jnp.maximum(block - 1, 0), 0)
    table = pl.BlockSpec((rows, 2 * HEAD_DIM), here)
    table_before = pl.BlockSpec((rows, 2 * HEAD_DIM), previous)
    return pl.pallas_call(
        attend_kernel,
        grid=(length // rows,),
        in_specs=[
            smem,
            smem,
            pl.BlockSpec((rows, full), here),
            pl.BlockSpec((rows, 2 * HEAD_DIM), lambda block: (jnp.maximum(block - 1, 0), pair_at)),
            table,
            table,
            table_before,
            table_before,
        ],
        out_specs=[pl.BlockSpec((rows, full), here), pl.BlockSpec((rows, wide), here)],
        out_shape=[
            jax.ShapeDtypeStruct((length, full), BF),
            jax.ShapeDtypeStruct((length, wide), BF),
        ],
        compiler_params=pltpu.CompilerParams(vmem_limit_bytes=VMEM_BYTES),
        cost_estimate=pl.CostEstimate(
            flops=8 * length * rows * full, bytes_accessed=10 * length * full,
            transcendentals=2 * length * rows * wide // HEAD_DIM,
        ),
    )(doc_ends, sinks, lin, lin, cosines, sines, cosines, sines)


def attend_back_kernel(
    ends_ref, sinks_ref, turned_ref, before_ref, cos_ref, sin_ref, grad_ref,
    out_ref, sums_ref, sink_ref, carry_ref,
):
    step = pl.program_id(0)
    block = pl.num_programs(0) - 1 - step
    rows = turned_ref.shape[0]
    wide = turned_ref.shape[1] - 2 * HEAD_DIM

    @pl.when(step == 0)
    def _():
        carry_ref[...] = jnp.zeros_like(carry_ref)
        sums_ref[...] = jnp.zeros_like(sums_ref)
        sink_ref[...] = jnp.zeros_like(sink_ref)

    queries = stack_heads(turned_ref[:, :wide])
    grads = stack_heads(grad_ref[...])
    pair = jnp.concatenate([before_ref[...], turned_ref[:, wide:]], axis=0)
    keys, values = pair[:, :HEAD_DIM], pair[:, HEAD_DIM:]
    probs, sink_share = block_probs(block, ends_ref, sinks_ref, queries, keys, rows)
    grad_probs = dot(grads, values, 1, 1)
    row_delta = jnp.sum(probs * grad_probs, axis=-1, keepdims=True)
    grad_scores = (probs * (grad_probs - row_delta)).astype(BF)
    heads = wide // HEAD_DIM
    sink_part = sink_share * row_delta.reshape(heads, rows, 1)
    sink_ref[...] -= jnp.broadcast_to(jnp.sum(sink_part, axis=1), sink_ref.shape)
    grad_query = unstack_heads(dot(grad_scores, keys, 1, 0) * 0.125, rows)
    grad_pair = jnp.concatenate(
        [dot(grad_scores, queries, 0, 0) * 0.125, dot(probs.astype(BF), grads, 0, 0)], axis=1
    )
    own_pair = grad_pair[rows:] + carry_ref[...]
    carry_ref[...] = grad_pair[:rows]
    cosines, sines = cos_ref[...], sin_ref[...]
    query_out = turn_halves(grad_query, cosines, -sines).astype(BF)
    pair_out = turn_keys(own_pair, cosines, sines, -1.0).astype(BF)
    out_ref[:, :wide] = query_out
    out_ref[:, wide:] = pair_out
    sums_ref[:, :wide] += jnp.broadcast_to(
        jnp.sum(query_out.astype(F32), axis=0, keepdims=True), (sums_ref.shape[0], wide)
    )
    sums_ref[:, wide:] += jnp.broadcast_to(
        jnp.sum(pair_out.astype(F32), axis=0, keepdims=True), (sums_ref.shape[0], 2 * HEAD_DIM)
    )


def attend_back(turned, cosines, sines, doc_ends, sinks, grads):
    length, full = turned.shape
    rows = WINDOW_LENGTH
    wide = full - 2 * HEAD_DIM
    heads = wide // HEAD_DIM
    pair_at = wide // (2 * HEAD_DIM)
    last = length // rows - 1
    smem = pl.BlockSpec(memory_space=pltpu.SMEM)
    here = lambda step: (last - step, 0)
    still = lambda step: (0, 0)
    table = pl.BlockSpec((rows, 2 * HEAD_DIM), here)
    grad_all, sums, sink_grad = pl.pallas_call(
        attend_back_kernel,
        grid=(length // rows,),
        in_specs=[
            smem,
            smem,
            pl.BlockSpec((rows, full), here),
            pl.BlockSpec(
                (rows, 2 * HEAD_DIM), lambda step: (jnp.maximum(last - step - 1, 0), pair_at)
            ),
            table,
            table,
            pl.BlockSpec((rows, wide), here),
        ],
        out_specs=[
            pl.BlockSpec((rows, full), here),
            pl.BlockSpec((8, full), still),
            pl.BlockSpec((heads, 128), still),
        ],
        out_shape=[
            jax.ShapeDtypeStruct((length, full), BF),
            jax.ShapeDtypeStruct((8, full), F32),
            jax.ShapeDtypeStruct((heads, 128), F32),
        ],
        scratch_shapes=[pltpu.VMEM((rows, 2 * HEAD_DIM), F32)],
        compiler_params=pltpu.CompilerParams(vmem_limit_bytes=VMEM_BYTES),
        cost_estimate=pl.CostEstimate(
            flops=20 * length * rows * full, bytes_accessed=10 * length * full,
            transcendentals=2 * length * rows * heads,
        ),
    )(doc_ends, sinks, turned, turned, cosines, sines, grads)
    return grad_all, sums[0], sink_grad[:, 0]


def rms_scale(values):
    return lax.rsqrt(jnp.mean(values * values, axis=-1, keepdims=True) + NORM_EPS)


def rope_tables(length):
    lane = jnp.arange(2 * HEAD_DIM, dtype=jnp.int32)
    frequency = ROPE_BASE ** (-(lane % (HEAD_DIM // 2)).astype(F32) * 2.0 / HEAD_DIM)
    angles = jnp.arange(length, dtype=F32)[:, None] * frequency[None, :]
    sign = jnp.where(lane % HEAD_DIM < HEAD_DIM // 2, -1.0, 1.0)
    return jnp.cos(angles), jnp.sin(angles) * sign


def swiglu(gate_pre, up_pre):
    gate_soft = GLU_LIMIT - jax.nn.softplus(GLU_LIMIT - gate_pre)
    up_soft = GLU_LIMIT * jnp.tanh(up_pre / GLU_LIMIT)
    return (up_soft + 1.0) * gate_soft * jax.nn.sigmoid(GLU_ALPHA * gate_soft)


class Work:
    def __init__(self):
        self.waiting = []
        self.done = {}
        self.pool = {}

    def add(self, name, make, *inputs):
        self.waiting.append([name, make, list(inputs)])

    def run(self, entry):
        _, make, inputs = entry
        return make(*(self.done[item] if isinstance(item, str) else item for item in inputs))

    def take(self, name):
        while name not in self.done:
            entry = self.waiting.pop(0)
            self.done[entry[0]] = self.run(entry)
        return self.done[name]

    def tie(self, *arrays, count=0, pool=()):
        taken = []
        for entry in self.waiting[:count]:
            result = self.run(entry)
            self.done[entry[0]] = result
            taken.append((entry[0], result))
        self.waiting = self.waiting[count:]
        coming = self.waiting[:2]
        held = [[item for item in entry[2] if not isinstance(item, str)] for entry in coming]
        arrays, made, held, pooled = lax.optimization_barrier(
            (arrays, [r for _, r in taken], held, [self.pool[name] for name in pool])
        )
        self.pool.update(zip(pool, pooled))
        for (name, _), result in zip(taken, made):
            self.done[name] = result
        for entry, kept in zip(coming, held):
            kept = list(kept)
            entry[2] = [item if isinstance(item, str) else kept.pop(0) for item in entry[2]]
        return arrays


class Line:
    def __init__(self, work):
        self.work = work
        index = lax.axis_index("seq")
        self.place, self.side = index // 2, index % 2
        at_low, at_high = self.place == 0, self.place == 3
        self.at_end = at_low | at_high
        self.at_low = at_low
        place = self.place
        self.order = [
            place,
            jnp.where(at_low, 1, place - 1),
            jnp.where(at_low, 2, jnp.where(at_high, 1, place + 1)),
            jnp.where(place < 2, 3, 0),
        ]

    @staticmethod
    def along(block, moves):
        route = [(2 * i + k, 2 * j + k) for i, j in moves for k in range(2)]
        return lax.ppermute(block, "seq", route)

    @staticmethod
    def across(block):
        return lax.ppermute(block, "seq", [(i, i ^ 1) for i in range(8)])

    def as_pair(self, own, other):
        first = jnp.where(self.side == 0, own, other)
        second = jnp.where(self.side == 0, other, own)
        return jnp.concatenate([first, second], axis=0)

    def gather(self, block, use, later=None, counts=(0, 0, 0, 0), pools=((), (), (), ())):
        tie = self.work.tie
        later = later or (lambda at, used: ())
        up, down, side_0 = (
            self.along(block, [(0, 1), (1, 2), (2, 3)]),
            self.along(block, [(1, 0), (2, 1), (3, 2)]),
            self.across(block),
        )
        up, down, side_0 = tie(up, down, side_0, count=counts[0], pool=pools[0])
        near = jnp.where(self.at_low, down, up)
        up_2, down_2, side_1 = (
            self.along(up, [(1, 2), (2, 3)]),
            self.along(down, [(2, 1), (1, 0)]),
            self.across(near),
        )
        used_0 = use(0, self.as_pair(block, side_0))
        up_2, down_2, side_1, down, near, used_0 = tie(
            up_2, down_2, side_1, down, near, used_0, count=counts[1], pool=pools[1]
        )
        sent_0 = later(0, used_0)
        second = up_2 + down_2
        far = jnp.where(self.at_end, second, down)
        third, side_2 = self.along(second, [(2, 3), (1, 0)]), self.across(far)
        used_1 = use(1, self.as_pair(near, side_1))
        third, side_2, second, far, used_1, sent_0 = tie(
            third, side_2, second, far, used_1, sent_0, count=counts[2], pool=pools[2]
        )
        sent_1 = later(1, used_1)
        last = jnp.where(self.at_end, third, second)
        side_3 = self.across(last)
        used_2 = use(2, self.as_pair(far, side_2))
        side_3, last, used_2, sent_1 = tie(
            side_3, last, used_2, sent_1, count=counts[3], pool=pools[3]
        )
        sent_2 = later(2, used_2)
        used_3 = use(3, self.as_pair(last, side_3))
        return [used_0, used_1, used_2, used_3], [sent_0, sent_1, sent_2, later(3, used_3)]

    def halves(self, pair):
        rows = pair.shape[0] // 2
        own = lax.dynamic_slice_in_dim(pair, self.side * rows, rows, 0)
        other = lax.dynamic_slice_in_dim(pair, (1 - self.side) * rows, rows, 0)
        return own, other

    def scatter(self, term, counts=(0, 0, 0, 0)):
        tie = self.work.tie
        own_3, other_3 = self.halves(term(3))
        side_3 = self.across(other_3)
        own_2, other_2 = self.halves(term(2))
        side_3, other_2, own_2 = tie(side_3, other_2, own_2, count=counts[0])
        sum_3 = own_3.astype(F32) + side_3.astype(F32)
        step_1, side_2 = self.along(sum_3.astype(BF), [(0, 1), (3, 2)]), self.across(other_2)
        own_1, other_1 = self.halves(term(1))
        step_1, side_2, other_1, own_1 = tie(step_1, side_2, other_1, own_1, count=counts[1])
        sum_2 = own_2.astype(F32) + side_2.astype(F32)
        sent = jnp.where(self.at_end, sum_2, sum_3 + step_1.astype(F32)).astype(BF)
        up, down, side_1 = (
            self.along(sent, [(0, 1), (1, 2)]),
            self.along(sent, [(3, 2), (2, 1)]),
            self.across(other_1),
        )
        own_0, other_0 = self.halves(term(0))
        up, down, side_1, own_0, other_0 = tie(up, down, side_1, own_0, other_0, count=counts[2])
        sum_1 = own_1.astype(F32) + side_1.astype(F32)
        sent_up = jnp.where(self.at_low, sum_1, sum_2 + up.astype(F32)).astype(BF)
        sent_down = (sum_1 + down.astype(F32)).astype(BF)
        up, down, side_0 = (
            self.along(sent_up, [(0, 1), (1, 2), (2, 3)]),
            self.along(sent_down, [(1, 0), (2, 1), (3, 2)]),
            self.across(other_0),
        )
        if counts[3]:
            up, down, side_0 = tie(up, down, side_0, count=counts[3])
        return own_0.astype(F32) + side_0.astype(F32) + up.astype(F32) + down.astype(F32)


class Whole:
    def __init__(self, work):
        self.order = [jnp.int32(0)]

    def gather(self, block, use, later=None, counts=(), pools=()):
        used = use(0, gather_seq(block))
        return [used], [later(0, used) if later else ()]

    def scatter(self, term, counts=()):
        return scatter_seq(term(0)).astype(F32)


def gather_seq(block):
    return lax.all_gather(block, "seq", axis=0, tiled=True)


def scatter_seq(partial_rows):
    return lax.psum_scatter(partial_rows, "seq", scatter_dimension=0, tiled=True)


def to_core(block):
    return lax.ppermute(block, "fsdp", [(i, i ^ 1) for i in range(4)])


def to_chip(block):
    return lax.ppermute(block, "fsdp", [(i, i ^ 2) for i in range(4)])


def split_low(values):
    high = values.astype(BF)
    low = (values - high.astype(F32)).astype(BF)
    return high, low


def place_rows(whole, piece, start):
    return lax.dynamic_update_slice_in_dim(whole, piece, start, 0)


def per_device(
    layer_input,
    attn_gain,
    query_matrix,
    query_bias_vector,
    key_matrix,
    key_bias_vector,
    value_matrix,
    value_bias_vector,
    sink_logit_values,
    output_matrix,
    output_bias_vector,
    ffn_gain,
    router_weight,
    router_bias,
    expert_gate_up,
    expert_gate_up_bias,
    expert_down,
    expert_down_bias,
    route_ids,
    doc_lengths,
    out_cotangent,
):
    seq_count = lax.axis_size("seq")
    fsdp_count = lax.axis_size("fsdp")
    seq_index = lax.axis_index("seq")
    fsdp_index = lax.axis_index("fsdp")
    tokens_here, width = layer_input.shape[1:]
    choose_count = route_ids.shape[2]
    expert_count = seq_count
    length = seq_count * tokens_here
    block_capacity = max(2, tokens_here * choose_count * 5 // (4 * expert_count))
    capacity = block_capacity * seq_count
    padded = -(-(width + 3 * expert_count) // 128) * 128
    heads_here = QUERY_HEADS // seq_count
    shared_kv = seq_count > KEY_VALUE_HEADS
    q_width = heads_here * HEAD_DIM
    q_part, kv_part = query_matrix.shape[1], key_matrix.shape[1]
    work = Work()
    line = Line(work) if seq_count == 8 else Whole(work)
    chunk = length // len(line.order)
    starts = [place * chunk for place in line.order]
    last = len(starts) - 1

    def taken(rows, start):
        return lax.dynamic_slice_in_dim(rows, start, chunk, 0)

    member_here = jnp.any(
        route_ids[0][:, :, None] == jnp.arange(expert_count, dtype=jnp.int32), axis=1
    )
    cot_here = out_cotangent[0]
    ranks = jnp.cumsum(member_here.astype(jnp.int32), axis=0)
    slot_here = jnp.where(member_here, ranks, 0).astype(BF)

    part = attn_gain.shape[0]
    near_first = [fsdp_index ^ turn for turn in range(fsdp_count)]

    def from_all(piece):
        core, chip = to_core(piece), to_chip(piece)
        return [piece, core, chip, to_core(chip)]

    def in_order(pieces):
        core_bit, chip_bit = fsdp_index % 2 == 0, fsdp_index < 2
        pairs = []
        for own, other in ((pieces[0], pieces[1]), (pieces[2], pieces[3])):
            pairs.append((jnp.where(core_bit, own, other), jnp.where(core_bit, other, own)))
        first = [jnp.where(chip_bit, a, b) for a, b in zip(*pairs)]
        second = [jnp.where(chip_bit, b, a) for a, b in zip(*pairs)]
        return first + second

    kv_head = seq_index // max(1, seq_count // KEY_VALUE_HEADS)

    def parameters(
        attn_gain,
        ffn_gain,
        output_bias_vector,
        sink_logit_values,
        router_bias,
        query_bias_vector,
        key_bias_vector,
        value_bias_vector,
        expert_down_bias,
        router_weight,
        query_matrix,
        output_matrix,
        key_matrix,
        value_matrix,
    ):
        tiny = jnp.concatenate(
            [sink_logit_values, router_bias, query_bias_vector, key_bias_vector, value_bias_vector]
        )
        tiny = jnp.concatenate([tiny, jnp.zeros((part - tiny.shape[0],), BF)])
        small = jnp.concatenate(
            [
                attn_gain[None],
                ffn_gain[None],
                output_bias_vector[None],
                tiny[None],
                expert_down_bias,
                router_weight.T,
            ],
            axis=0,
        )
        small_all = jnp.stack(in_order(from_all(small)))
        wide = jnp.swapaxes(small_all, 0, 1).reshape(small.shape[0], width).astype(F32)
        attn_gain_f, ffn_gain_f, out_bias_f = wide[0], wide[1], wide[2]
        down_bias_f = wide[4 : 4 + expert_count]
        router_t = wide[4 + expert_count :].astype(BF)
        tiny_all = small_all[:, 3]
        places = [0]
        for piece in (sink_logit_values, router_bias, query_bias_vector, key_bias_vector, value_bias_vector):
            places.append(places[-1] + piece.shape[0])
        sinks_f, router_bias_f, q_bias, k_bias, v_bias = (
            tiny_all[:, a:b].astype(F32) for a, b in zip(places[:-1], places[1:])
        )
        sinks_f, router_bias_f = sinks_f.reshape(-1), router_bias_f.reshape(-1)
        k_bias, v_bias = k_bias.reshape(-1), v_bias.reshape(-1)
        q_bias = jnp.concatenate(
            [lax.dynamic_slice_in_dim(q_bias, at, 1, 0)[0] for at in near_first]
        )
        pieces = from_all(jnp.concatenate([query_matrix, output_matrix.T], axis=0))
        w_query = jnp.concatenate([piece[:width] for piece in pieces], axis=1)
        wo_t = jnp.concatenate([piece[width:] for piece in pieces], axis=1)
        if shared_kv:

            def own_head(piece):
                whole = lax.all_gather(piece, ("seq", "fsdp"), axis=0, tiled=True)
                return lax.dynamic_slice_in_dim(whole, kv_head * HEAD_DIM, HEAD_DIM, 0)

            w_pair = jnp.concatenate([own_head(key_matrix.T), own_head(value_matrix.T)], axis=0)
            k_bias = own_head(key_bias_vector).astype(F32)
            v_bias = own_head(value_bias_vector).astype(F32)
        else:
            kv_pieces = in_order(from_all(jnp.concatenate([key_matrix.T, value_matrix.T], axis=0)))
            w_pair = jnp.concatenate(
                [piece[:kv_part] for piece in kv_pieces] + [piece[kv_part:] for piece in kv_pieces],
                axis=0,
            )
        lin_bias = jnp.concatenate([q_bias, k_bias, v_bias])
        return (
            attn_gain_f,
            ffn_gain_f,
            out_bias_f,
            down_bias_f,
            router_t,
            sinks_f,
            router_bias_f,
            w_query,
            wo_t,
            w_pair,
            lin_bias,
        )

    work.add(
        "parameters",
        parameters,
        attn_gain,
        ffn_gain,
        output_bias_vector,
        sink_logit_values,
        router_bias,
        query_bias_vector,
        key_bias_vector,
        value_bias_vector,
        expert_down_bias,
        router_weight,
        query_matrix,
        output_matrix,
        key_matrix,
        value_matrix,
    )

    columns = jnp.concatenate(
        [
            (seq_index * fsdp_count + at) * q_part + jnp.arange(q_part, dtype=jnp.int32)
            for at in near_first
        ]
    )
    whole_heads = q_part % HEAD_DIM == 0

    cosine_table, sine_table = rope_tables(length)
    doc_row = lax.dynamic_slice_in_dim(doc_lengths, fsdp_index, 1, 0)[0]
    doc_ends = jnp.cumsum(doc_row)

    def project(pair):
        pair_f = pair.astype(F32)
        normed = (pair_f * rms_scale(pair_f) * attn_gain_f).astype(BF)
        query_part = dot(normed, w_query, 1, 0) + lin_bias[:q_width]
        return normed, query_part, dot(normed, w_pair, 1, 1) + lin_bias[q_width:]

    pairs = []

    def arrive(at, pair):
        pairs.append(pair)
        return pair

    line.gather(layer_input[0], lambda at, pair: (work.take("parameters"), arrive(at, pair))[1])
    (
        attn_gain_f,
        ffn_gain_f,
        out_bias_f,
        down_bias_f,
        router_t,
        sinks_f,
        router_bias_f,
        w_query,
        wo_t,
        w_pair,
        lin_bias,
    ) = work.take("parameters")
    projected = [project(pair) for pair in pairs]
    normed_rows = jnp.zeros((length, width), BF)
    lin = jnp.zeros((length, q_width + 2 * HEAD_DIM), F32)
    for start, (normed, query_part, pair_part) in zip(starts, projected):
        normed_rows = place_rows(normed_rows, normed, start)
        lin = lax.dynamic_update_slice(lin, query_part, (start, 0))
        lin = lax.dynamic_update_slice(lin, pair_part, (start, q_width))
    if not whole_heads:
        order = jnp.argsort(columns)
        w_query = w_query[:, order]
        wo_t = wo_t[:, order]
        lin = jnp.concatenate([lin[:, :q_width][:, order], lin[:, q_width:]], axis=1)
        head_numbers = seq_index * heads_here + jnp.arange(heads_here, dtype=jnp.int32)
    else:
        head_numbers = columns[::HEAD_DIM] // HEAD_DIM
    head_lane = (head_numbers[:, None] == jnp.arange(QUERY_HEADS)[None, :]).astype(F32)
    sinks_here = jnp.sum(head_lane * sinks_f[None, :], axis=1)
    turned, heads = attend(lin, cosine_table, sine_table, doc_ends, sinks_here)
    attn_sum = line.scatter(
        lambda at: dot(taken(heads, starts[at]), wo_t, 1, 1).astype(BF), counts=(0, 0, 0, 0)
    )

    resid_in = layer_input[0].astype(F32)
    resid_mid = resid_in + attn_sum + out_bias_f
    norm_two = rms_scale(resid_mid)
    unit_mid = resid_mid * norm_two
    normed_mid = (unit_mid * ffn_gain_f).astype(BF)
    logits = dot(normed_mid, router_t, 1, 1) + router_bias_f
    gates = jax.nn.softmax(jnp.where(member_here, logits, -1e30), axis=-1)
    gates = jnp.where(member_here, gates, 0.0)
    gate_high, gate_low = split_low(gates)
    mid_packed = jnp.concatenate(
        [
            normed_mid,
            slot_here,
            gate_high,
            gate_low,
            jnp.zeros((tokens_here, padded - width - 3 * expert_count), BF),
        ],
        axis=1,
    )

    expert_lane = (jnp.arange(expert_count, dtype=jnp.int32) == seq_index).astype(F32)
    slots = block_capacity * (chunk // tokens_here)
    slot_number = jnp.arange(block_capacity, dtype=F32) + 1.0
    selects = {}

    def pick_rows(at, pair):
        rank = jnp.sum(pair[:, width : width + expert_count].astype(F32) * expert_lane, axis=1)
        blocks = chunk // tokens_here
        hit = slot_number[None, :, None] == rank.reshape(blocks, 1, tokens_here)
        same = jnp.eye(blocks, dtype=jnp.bool_)[:, None, :, None]
        select = (hit[:, :, None, :] & same).reshape(slots, chunk).astype(BF)
        return select, dot(select, pair, 1, 0).astype(BF)

    def send_rows(at, used):
        return to_core(used[1]), to_chip(used[1])

    picked, sent = line.gather(mid_packed, pick_rows, send_rows)
    selects = [select for select, _ in picked]
    own_rows = [rows for _, rows in picked]
    core_rows = [core for core, _ in sent]
    chip_rows = [chip for _, chip in sent]
    spare = padded - width
    units_w = jnp.pad(jnp.swapaxes(expert_gate_up[0], 1, 2), ((0, 0), (0, 0), (0, spare)))
    down_w = jnp.pad(expert_down[0], ((0, 0), (0, spare)))
    units_b = expert_gate_up_bias[0].astype(F32)[:, None, :]

    def joined(pieces):
        whole = jnp.zeros((2 * capacity, pieces[0].shape[1]), BF)
        first = 0
        for piece in pieces:
            whole = place_rows(whole, piece, first)
            first += piece.shape[0]
        return whole

    def einsum(form, left, right):
        return jnp.einsum(form, left, right, preferred_element_type=F32)

    def hidden_step(rows):
        tail = rows[:, width + expert_count :].astype(F32)
        share = jnp.sum(
            (tail[:, :expert_count] + tail[:, expert_count : 2 * expert_count]) * expert_lane,
            axis=1,
            keepdims=True,
        )
        before = einsum("rd,khd->krh", rows, units_w) + units_b
        hidden = swiglu(before[0], before[1]).astype(BF)
        return share, before, hidden, (hidden.astype(F32) * share).astype(BF)

    def mix_step(made):
        return dot(made[3], down_w, 1, 0).astype(BF)

    def back_step(made, cot):
        share, before, hidden, _ = made
        grad_hidden = dot(cot, down_w, 1, 1)
        score = jnp.sum(hidden.astype(F32) * grad_hidden, axis=1, keepdims=True)
        _, glu_back = jax.vjp(swiglu, before[0], before[1])
        grad_gate_pre, grad_up_pre = glu_back(grad_hidden * share)
        return score, jnp.stack([grad_gate_pre.astype(BF), grad_up_pre.astype(BF)])

    def row_step(made):
        return einsum("krh,khd->rd", made[1], units_w).astype(BF)

    cot_block = jnp.concatenate([cot_here, jnp.zeros((tokens_here, spare), BF)], axis=1)
    cot_block, own_rows = work.tie(cot_block, own_rows)
    cot_rows = gather_seq(cot_block)
    near = joined(own_rows + core_rows)
    made_n = hidden_step(near)
    made_n, chip_rows = work.tie(made_n, chip_rows)
    far = joined(chip_rows + [to_core(chip) for chip in chip_rows])
    mix_n = mix_step(made_n)
    made_o = hidden_step(far)
    mix_o = mix_step(made_o)
    mix_core_n = to_core(mix_n[capacity:])
    mix_core_o = to_core(mix_o[capacity:])
    cot_rows, made_o, mix_n, mix_o, mix_core_n = work.tie(
        cot_rows, made_o, mix_n, mix_o, mix_core_n
    )
    cot_own = [dot(select, taken(cot_rows, at), 1, 0).astype(BF) for select, at in zip(selects, starts)]
    half = (len(cot_own) + 1) // 2
    cot_own = [jnp.concatenate(cot_own[:half])] + (
        [jnp.concatenate(cot_own[half:])] if cot_own[half:] else []
    )
    cot_chip = [to_chip(rows) for rows in cot_own]
    cot_near = joined(cot_own + [to_core(rows) for rows in cot_own])

    def core_sum(part, from_core):
        return (part[:capacity].astype(F32) + from_core.astype(F32)).astype(part.dtype)

    def total(near_part, from_core, arrived, at):
        return (
            slot_rows(near_part, at).astype(F32)
            + slot_rows(from_core, at).astype(F32)
            + arrived.astype(F32)
        )

    def slot_rows(rows, at):
        return rows[at * slots : (at + 1) * slots]

    def from_chip(far_sum):
        return [to_chip(slot_rows(far_sum, at)) for at in reversed(range(len(starts)))][::-1]

    def score_step(back_n, back_o):
        scores = jnp.concatenate([back_n[0], back_o[0]], axis=1)
        return scores[:capacity] + to_core(scores[capacity:])

    back_n = back_step(made_n, cot_near)
    row_n = row_step(back_n)
    back_n, row_n, cot_chip = work.tie(back_n, row_n, cot_chip)
    row_near_core = to_core(row_n[capacity:])
    cot_far = joined(cot_chip + [to_core(rows) for rows in cot_chip])
    back_o = back_step(made_o, cot_far)
    back_n, back_o, row_near_core = work.tie(back_n, back_o, row_near_core)
    score = score_step(back_n, back_o)
    score = score[:, :1] + to_chip(score[:, 1:])
    row_o = row_step(back_o)
    row_o, score = work.tie(row_o, score)
    (score_n, low_n), (score_o, low_o) = back_n, back_o
    row_far_core = to_core(row_o[capacity:])

    def units_step(low_n, rows_n, low_o, rows_o):
        return einsum("krh,rd->khd", low_n, rows_n[:, :width]) + einsum(
            "krh,rd->khd", low_o, rows_o[:, :width]
        )

    def down_step(hidden_n, cot_n, hidden_o, cot_o):
        return dot(hidden_n, cot_n[:, :width], 0, 0) + dot(hidden_o, cot_o[:, :width], 0, 0)

    work.add("units", units_step, low_n, near, low_o, far)
    work.add("down", down_step, made_n[3], cot_near, made_o[3], cot_far)
    (row_far_core,) = work.tie(row_far_core)
    arrivals = from_chip(core_sum(row_o, row_far_core))

    def back_term(at):
        row_sum = total(row_n, row_near_core, arrivals[at], at)
        grad_high, grad_low = split_low(slot_rows(score, at) * expert_lane)
        back_packed = jnp.concatenate(
            [
                row_sum[:, :width].astype(BF),
                grad_high,
                grad_low,
                jnp.zeros((slots, padded - width - 2 * expert_count), BF),
            ],
            axis=1,
        )
        return dot(selects[at], back_packed, 0, 0).astype(BF)

    back = line.scatter(back_term, counts=(1, 0, 0, 0))

    mix_far = core_sum(mix_o, mix_core_o)
    mix_far, arrivals_end = lax.optimization_barrier((mix_far, arrivals[0][:8]))
    mix_chip = to_chip(mix_far)

    def mix_place(mix_chip):
        whole = jnp.zeros((length, width), BF)
        for at, start in enumerate(starts):
            mix_sum = total(mix_n, mix_core_n, slot_rows(mix_chip, at), at)
            term = dot(selects[at], mix_sum[:, :width].astype(BF), 0, 0).astype(BF)
            whole = place_rows(whole, term, start)
        return whole

    cot_f = cot_here.astype(F32)
    grad_gates = (
        back[:, width : width + expert_count]
        + back[:, width + expert_count : width + 2 * expert_count]
        + dot(cot_f, down_bias_f, 1, 1, EXACT)
    )
    mean_gate = jnp.sum(gates * grad_gates, axis=-1, keepdims=True)
    grad_logits = gates * (grad_gates - mean_gate)
    router_grad_t = dot(grad_logits, normed_mid.astype(F32), 0, 0, EXACT)
    router_bias_grad = jnp.sum(grad_logits, axis=0)
    down_bias_grad = dot(gates, cot_f, 0, 0, EXACT)
    grad_normed_mid = back[:, :width] + dot(grad_logits, router_t.astype(F32), 1, 0, EXACT)
    ffn_gain_grad = jnp.sum(grad_normed_mid * unit_mid, axis=0)
    grad_unit_mid = grad_normed_mid * ffn_gain_f
    grad_mid = (
        norm_two
        * (grad_unit_mid - unit_mid * jnp.mean(grad_unit_mid * unit_mid, axis=-1, keepdims=True))
        + cot_f
    )
    grad_attn = grad_mid.astype(BF)
    out_bias_grad = jnp.sum(grad_attn.astype(F32), axis=0)

    def to_core_owners(blocks, kind=BF):
        both = to_core(jnp.stack([blocks[1], blocks[3]]).astype(kind))
        return blocks[0] + both[0].astype(F32), (blocks[2] + both[1].astype(F32)).astype(kind)

    def to_owners(sums):
        own, chip = sums
        return own + to_chip(chip).astype(F32)

    def seq_sum(values):
        step = 1
        while step < seq_count:
            values = values + lax.ppermute(values, "seq", [(i, i ^ step) for i in range(seq_count)])
            step *= 2
        return values

    def small_step(rows):
        blocks = [lax.dynamic_slice_in_dim(rows, at * part, part, 1) for at in near_first]
        return to_core_owners(blocks, F32)

    tiny_grad = jnp.zeros((fsdp_count, part), F32)
    tiny_grad = lax.dynamic_update_slice(
        tiny_grad, router_bias_grad.reshape(fsdp_count, -1), (0, 0)
    ).reshape(1, width)
    small_grad = jnp.concatenate(
        [out_bias_grad[None], ffn_gain_grad[None], tiny_grad, down_bias_grad, router_grad_t],
        axis=0,
    )

    attn_rows = jnp.zeros((length, width), BF)
    grad_heads = jnp.zeros((length, q_width), BF)

    def head_grads(at, pair):
        return pair, dot(pair, wo_t, 1, 0).astype(BF)

    work.take("units")
    grads, _ = line.gather(grad_attn, head_grads, counts=(1, 0, 0, 0))
    mixture = scatter_seq(mix_place(mix_chip)).astype(F32)
    mixture = mixture + dot(gates, down_bias_f, 1, 0, EXACT)
    layer_output = (resid_mid + mixture).astype(BF)[None]
    for start, (pair, grad_part) in zip(starts, grads):
        attn_rows = place_rows(attn_rows, pair, start)
        grad_heads = place_rows(grad_heads, grad_part, start)

    lin_grad, lin_sums, sink_here_grad = attend_back(
        turned, cosine_table, sine_table, doc_ends, sinks_here, grad_heads
    )

    order = None if whole_heads else jnp.argsort(columns)
    back_order = None if whole_heads else jnp.argsort(order)

    def column_blocks(whole):
        if back_order is not None:
            whole = whole[:, back_order]
        return [whole[:, at * q_part : (at + 1) * q_part] for at in range(fsdp_count)]

    def query_step(rows, grads):
        return dot(rows, grads[:, :q_width], 0, 0)

    def pair_step(rows, grads):
        return dot(grads[:, q_width:], rows, 0, 0)

    sink_all_grad = jnp.sum(head_lane * sink_here_grad[:, None], axis=0)

    def row_blocks(query_w_part, pair_w_part):
        attn_gain_grad = (
            jnp.sum(query_w_part * w_query.astype(F32), axis=1)
            + jnp.sum(pair_w_part * w_pair.astype(F32), axis=0)
        ) / attn_gain_f
        query_sums = lin_sums[:q_width]
        if back_order is not None:
            query_sums = query_sums[back_order]
        pair_sums = lin_sums[q_width:]
        blocks = []
        for turn, at in enumerate(near_first):
            gain = lax.dynamic_slice_in_dim(attn_gain_grad, at * part, part, 0)
            row = [gain, sink_all_grad, query_sums[turn * q_part : (turn + 1) * q_part]]
            block = []
            if not shared_kv:
                for first in (0, HEAD_DIM):
                    row.append(lax.dynamic_slice_in_dim(pair_sums, first + at * kv_part, kv_part, 0))
                    block.append(
                        lax.dynamic_slice_in_dim(pair_w_part, first + at * kv_part, kv_part, 0)
                    )
            row = jnp.concatenate(row)
            row = jnp.concatenate([row, jnp.zeros((width - row.shape[0],), F32)])
            block.append(jnp.broadcast_to(row[None], (16, width)))
            blocks.append(jnp.concatenate(block, axis=0))
        return to_core_owners(blocks)

    work.add("query_w", query_step, normed_rows, lin_grad)
    work.add("out_w", lambda a, b: dot(a, b, 0, 0), attn_rows, heads)
    work.add("pair_w", pair_step, normed_rows, lin_grad)
    work.add("query_core", lambda whole: to_core_owners(column_blocks(whole)), "query_w")
    work.add("out_core", lambda whole: to_core_owners(column_blocks(whole)), "out_w")
    work.add("small_core", small_step, small_grad)
    work.add("row_core", row_blocks, "query_w", "pair_w")
    work.add("small_chip", to_owners, "small_core")
    work.add("row_chip", to_owners, "row_core")
    work.add("query_chip", to_owners, "query_core")

    def input_term(at):
        grad_part = taken(lin_grad, starts[at])
        return (
            dot(grad_part[:, :q_width], w_query, 1, 1) + dot(grad_part[:, q_width:], w_pair, 1, 0)
        ).astype(BF)

    grad_normed_in = line.scatter(input_term, counts=(1, 2, 4, 3))
    query_w_own = work.take("query_chip")
    out_w_own = to_owners(work.take("out_core")).T
    owned, small_own = work.take("row_chip"), seq_sum(work.take("small_chip"))
    down_grad = work.take("down")
    gate_up_grad = jnp.swapaxes(work.take("units"), 1, 2)
    gate_up_bias_grad = jnp.sum(low_n.astype(F32), axis=1) + jnp.sum(low_o.astype(F32), axis=1)

    resid_scale = rms_scale(resid_in)
    unit_in = resid_in * resid_scale
    grad_unit_in = grad_normed_in * attn_gain_f
    input_grad = (
        resid_scale
        * (grad_unit_in - unit_in * jnp.mean(grad_unit_in * unit_in, axis=-1, keepdims=True))
        + grad_mid
    )

    owned_row = owned[-1]
    gain_own = seq_sum(owned_row[None, : part + QUERY_HEADS])[0]
    sink_own = lax.dynamic_slice_in_dim(
        gain_own[part:], fsdp_index * sink_logit_values.shape[0], sink_logit_values.shape[0], 0
    )
    at = part + QUERY_HEADS
    query_b_own = owned_row[at : at + q_part]
    if shared_kv:

        def whole_sum(part_grad):
            whole = jnp.zeros((KEY_VALUE_HEADS * HEAD_DIM,) + part_grad.shape[1:], F32)
            whole = lax.dynamic_update_slice_in_dim(whole, part_grad, kv_head * HEAD_DIM, 0)
            return lax.psum_scatter(whole, ("seq", "fsdp"), scatter_dimension=0, tiled=True)

        pair_w_part = work.take("pair_w")
        key_w_own = whole_sum(pair_w_part[:HEAD_DIM]).T
        value_w_own = whole_sum(pair_w_part[HEAD_DIM:]).T
        key_b_own = whole_sum(lin_sums[q_width : q_width + HEAD_DIM])
        value_b_own = whole_sum(lin_sums[q_width + HEAD_DIM :])
    else:
        key_w_own, value_w_own = owned[:kv_part].T, owned[kv_part : 2 * kv_part].T
        at = at + q_part
        key_b_own, value_b_own = owned_row[at : at + kv_part], owned_row[at + kv_part : at + 2 * kv_part]

    return (
        layer_output,
        input_grad[None],
        gain_own[:part],
        query_w_own,
        query_b_own,
        key_w_own,
        key_b_own,
        value_w_own,
        value_b_own,
        sink_own,
        out_w_own,
        small_own[0],
        small_own[1],
        small_own[3 + expert_count :].T,
        lax.dynamic_slice_in_dim(small_own[2], 0, router_bias.shape[0], 0),
        gate_up_grad[None],
        gate_up_bias_grad[None],
        down_grad[None],
        small_own[3 : 3 + expert_count],
    )


def solution(mesh):
    return jax.shard_map(
        per_device,
        mesh=mesh,
        in_specs=(
            P("fsdp", "seq", None),
            P("fsdp"),
            P(None, ("seq", "fsdp")),
            P(("seq", "fsdp")),
            P(None, ("seq", "fsdp")),
            P(("seq", "fsdp")),
            P(None, ("seq", "fsdp")),
            P(("seq", "fsdp")),
            P("fsdp"),
            P(("seq", "fsdp"), None),
            P("fsdp"),
            P("fsdp"),
            P("fsdp", None),
            P("fsdp"),
            P("seq", None, None, "fsdp"),
            P("seq", None, "fsdp"),
            P("seq", "fsdp", None),
            P(None, "fsdp"),
            P("fsdp", "seq", None),
            P(),
            P("fsdp", "seq", None),
        ),
        out_specs=(
            P("fsdp", "seq", None),
            P("fsdp", "seq", None),
            P("fsdp"),
            P(None, ("seq", "fsdp")),
            P(("seq", "fsdp")),
            P(None, ("seq", "fsdp")),
            P(("seq", "fsdp")),
            P(None, ("seq", "fsdp")),
            P(("seq", "fsdp")),
            P("fsdp"),
            P(("seq", "fsdp"), None),
            P("fsdp"),
            P("fsdp"),
            P("fsdp", None),
            P("fsdp"),
            P("seq", None, None, "fsdp"),
            P("seq", None, "fsdp"),
            P("seq", "fsdp", None),
            P(None, "fsdp"),
        ),
        check_vma=False,
    )
```

```python
import jax
import jax.numpy as jnp
from jax import lax
from jax.experimental import pallas as pl
from jax.experimental.pallas import tpu as pltpu
from jax.sharding import PartitionSpec as P

QUERY_HEADS = 64
KEY_VALUE_HEADS = 8
HEAD_DIM = 64
WINDOW_LENGTH = 128


ROPE_BASE = 150000.0
NORM_EPS = 1e-05
GLU_ALPHA = 1.702
GLU_LIMIT = 7.0
EXACT = lax.Precision.HIGHEST
BF = jnp.bfloat16
F32 = jnp.float32
VMEM_BYTES = 60 * 2**20


def dot(left, right, left_dim, right_dim, precision=None):
    return lax.dot_general(
        left,
        right,
        (((left_dim,), (right_dim,)), ((), ())),
        precision=precision,
        preferred_element_type=jnp.float32,
    )


def turn_halves(values, cosines, sines):
    rows, width = values.shape
    half = HEAD_DIM // 2
    lane = lax.broadcasted_iota(jnp.int32, (rows, width), 1) % HEAD_DIM
    ahead = pltpu.roll(values, width - half, 1)
    behind = pltpu.roll(values, half, 1)
    other = jnp.where(lane < half, ahead, behind)
    copies = width // cosines.shape[1]
    wide_cos = jnp.concatenate([cosines] * copies, axis=1)
    wide_sin = jnp.concatenate([sines] * copies, axis=1)
    return values * wide_cos + other * wide_sin


def turn_keys(pair, cosines, sines, direction):
    lane = lax.broadcasted_iota(jnp.int32, pair.shape, 1)
    keys = lane < HEAD_DIM
    return turn_halves(pair, jnp.where(keys, cosines, 1.0), jnp.where(keys, direction * sines, 0.0))


def stack_heads(rows):
    return jnp.concatenate(
        [rows[:, at : at + HEAD_DIM] for at in range(0, rows.shape[1], HEAD_DIM)], axis=0
    )


def unstack_heads(stacked, rows):
    return jnp.concatenate(
        [stacked[at : at + rows] for at in range(0, stacked.shape[0], rows)], axis=1
    )


def block_probs(block, ends_ref, sinks_ref, queries, keys, rows):
    heads = queries.shape[0] // rows
    spread = lax.broadcasted_iota(jnp.int32, (rows, 2 * rows), 0)
    key_at = lax.broadcasted_iota(jnp.int32, (rows, 2 * rows), 1)
    position = block * rows + spread
    key_pos = (block - 1) * rows + key_at
    offset = position - key_pos
    allowed = (key_pos >= 0) & (offset >= 0) & (offset <= WINDOW_LENGTH)
    for document in range(ends_ref.shape[0]):
        end = ends_ref[document]
        allowed = allowed & ((position >= end) == (key_pos >= end))
    scores = dot(queries, keys, 1, 1) * 0.125
    scores = scores.reshape(heads, rows, 2 * rows)
    scores = jnp.where(allowed[None], scores, -1e30)
    head = lax.broadcasted_iota(jnp.int32, (heads, rows, 1), 0)
    sink = jnp.zeros((heads, rows, 1), F32)
    for at in range(heads):
        sink = jnp.where(head == at, sinks_ref[at], sink)
    top = jnp.maximum(jnp.max(scores, axis=-1, keepdims=True), sink)
    weights = jnp.exp(scores - top)
    sink_weight = jnp.exp(sink - top)
    inverse = 1.0 / (jnp.sum(weights, axis=-1, keepdims=True) + sink_weight)
    probs = (weights * inverse).reshape(heads * rows, 2 * rows)
    return probs, sink_weight * inverse


def attend_kernel(
    ends_ref, sinks_ref, lin_ref, before_ref, cos_ref, sin_ref, cos_before_ref, sin_before_ref,
    turned_ref, heads_ref,
):
    block = pl.program_id(0)
    rows = lin_ref.shape[0]
    wide = lin_ref.shape[1] - 2 * HEAD_DIM
    cosines, sines = cos_ref[...], sin_ref[...]
    queries = turn_halves(lin_ref[:, :wide], cosines, sines).astype(BF)
    own = turn_keys(lin_ref[:, wide:], cosines, sines, 1.0).astype(BF)
    before = turn_keys(before_ref[...], cos_before_ref[...], sin_before_ref[...], 1.0).astype(BF)
    turned_ref[:, :wide] = queries
    turned_ref[:, wide:] = own
    pair = jnp.concatenate([before, own], axis=0)
    probs, _ = block_probs(
        block, ends_ref, sinks_ref, stack_heads(queries), pair[:, :HEAD_DIM], rows
    )
    mixed = dot(probs.astype(BF), pair[:, HEAD_DIM:], 1, 0)
    heads_ref[...] = unstack_heads(mixed.astype(BF), rows)


def attend(lin, cosines, sines, doc_ends, sinks):
    length, full = lin.shape
    rows = WINDOW_LENGTH
    wide = full - 2 * HEAD_DIM
    pair_at = wide // (2 * HEAD_DIM)
    smem = pl.BlockSpec(memory_space=pltpu.SMEM)
    here = lambda block: (block, 0)
    previous = lambda block: (jnp.maximum(block - 1, 0), 0)
    table = pl.BlockSpec((rows, 2 * HEAD_DIM), here)
    table_before = pl.BlockSpec((rows, 2 * HEAD_DIM), previous)
    return pl.pallas_call(
        attend_kernel,
        grid=(length // rows,),
        in_specs=[
            smem,
            smem,
            pl.BlockSpec((rows, full), here),
            pl.BlockSpec((rows, 2 * HEAD_DIM), lambda block: (jnp.maximum(block - 1, 0), pair_at)),
            table,
            table,
            table_before,
            table_before,
        ],
        out_specs=[pl.BlockSpec((rows, full), here), pl.BlockSpec((rows, wide), here)],
        out_shape=[
            jax.ShapeDtypeStruct((length, full), BF),
            jax.ShapeDtypeStruct((length, wide), BF),
        ],
        compiler_params=pltpu.CompilerParams(vmem_limit_bytes=VMEM_BYTES),
        cost_estimate=pl.CostEstimate(
            flops=8 * length * rows * full, bytes_accessed=10 * length * full,
            transcendentals=2 * length * rows * wide // HEAD_DIM,
        ),
    )(doc_ends, sinks, lin, lin, cosines, sines, cosines, sines)


def attend_back_kernel(
    ends_ref, sinks_ref, turned_ref, before_ref, cos_ref, sin_ref, grad_ref,
    out_ref, sums_ref, sink_ref, carry_ref,
):
    step = pl.program_id(0)
    block = pl.num_programs(0) - 1 - step
    rows = turned_ref.shape[0]
    wide = turned_ref.shape[1] - 2 * HEAD_DIM

    @pl.when(step == 0)
    def _():
        carry_ref[...] = jnp.zeros_like(carry_ref)
        sums_ref[...] = jnp.zeros_like(sums_ref)
        sink_ref[...] = jnp.zeros_like(sink_ref)

    queries = stack_heads(turned_ref[:, :wide])
    grads = stack_heads(grad_ref[...])
    pair = jnp.concatenate([before_ref[...], turned_ref[:, wide:]], axis=0)
    keys, values = pair[:, :HEAD_DIM], pair[:, HEAD_DIM:]
    probs, sink_share = block_probs(block, ends_ref, sinks_ref, queries, keys, rows)
    grad_probs = dot(grads, values, 1, 1)
    row_delta = jnp.sum(probs * grad_probs, axis=-1, keepdims=True)
    grad_scores = (probs * (grad_probs - row_delta)).astype(BF)
    heads = wide // HEAD_DIM
    sink_part = sink_share * row_delta.reshape(heads, rows, 1)
    sink_ref[...] -= jnp.broadcast_to(jnp.sum(sink_part, axis=1), sink_ref.shape)
    grad_query = unstack_heads(dot(grad_scores, keys, 1, 0) * 0.125, rows)
    grad_pair = jnp.concatenate(
        [dot(grad_scores, queries, 0, 0) * 0.125, dot(probs.astype(BF), grads, 0, 0)], axis=1
    )
    own_pair = grad_pair[rows:] + carry_ref[...]
    carry_ref[...] = grad_pair[:rows]
    cosines, sines = cos_ref[...], sin_ref[...]
    query_out = turn_halves(grad_query, cosines, -sines).astype(BF)
    pair_out = turn_keys(own_pair, cosines, sines, -1.0).astype(BF)
    out_ref[:, :wide] = query_out
    out_ref[:, wide:] = pair_out
    sums_ref[:, :wide] += jnp.broadcast_to(
        jnp.sum(query_out.astype(F32), axis=0, keepdims=True), (sums_ref.shape[0], wide)
    )
    sums_ref[:, wide:] += jnp.broadcast_to(
        jnp.sum(pair_out.astype(F32), axis=0, keepdims=True), (sums_ref.shape[0], 2 * HEAD_DIM)
    )


def attend_back(turned, cosines, sines, doc_ends, sinks, grads):
    length, full = turned.shape
    rows = WINDOW_LENGTH
    wide = full - 2 * HEAD_DIM
    heads = wide // HEAD_DIM
    pair_at = wide // (2 * HEAD_DIM)
    last = length // rows - 1
    smem = pl.BlockSpec(memory_space=pltpu.SMEM)
    here = lambda step: (last - step, 0)
    still = lambda step: (0, 0)
    table = pl.BlockSpec((rows, 2 * HEAD_DIM), here)
    grad_all, sums, sink_grad = pl.pallas_call(
        attend_back_kernel,
        grid=(length // rows,),
        in_specs=[
            smem,
            smem,
            pl.BlockSpec((rows, full), here),
            pl.BlockSpec(
                (rows, 2 * HEAD_DIM), lambda step: (jnp.maximum(last - step - 1, 0), pair_at)
            ),
            table,
            table,
            pl.BlockSpec((rows, wide), here),
        ],
        out_specs=[
            pl.BlockSpec((rows, full), here),
            pl.BlockSpec((8, full), still),
            pl.BlockSpec((heads, 128), still),
        ],
        out_shape=[
            jax.ShapeDtypeStruct((length, full), BF),
            jax.ShapeDtypeStruct((8, full), F32),
            jax.ShapeDtypeStruct((heads, 128), F32),
        ],
        scratch_shapes=[pltpu.VMEM((rows, 2 * HEAD_DIM), F32)],
        compiler_params=pltpu.CompilerParams(vmem_limit_bytes=VMEM_BYTES),
        cost_estimate=pl.CostEstimate(
            flops=20 * length * rows * full, bytes_accessed=10 * length * full,
            transcendentals=2 * length * rows * heads,
        ),
    )(doc_ends, sinks, turned, turned, cosines, sines, grads)
    return grad_all, sums[0], sink_grad[:, 0]


def rms_scale(values):
    return lax.rsqrt(jnp.mean(values * values, axis=-1, keepdims=True) + NORM_EPS)


def rope_tables(length):
    lane = jnp.arange(2 * HEAD_DIM, dtype=jnp.int32)
    frequency = ROPE_BASE ** (-(lane % (HEAD_DIM // 2)).astype(F32) * 2.0 / HEAD_DIM)
    angles = jnp.arange(length, dtype=F32)[:, None] * frequency[None, :]
    sign = jnp.where(lane % HEAD_DIM < HEAD_DIM // 2, -1.0, 1.0)
    return jnp.cos(angles), jnp.sin(angles) * sign


def swiglu(gate_pre, up_pre):
    gate_soft = GLU_LIMIT - jax.nn.softplus(GLU_LIMIT - gate_pre)
    up_soft = GLU_LIMIT * jnp.tanh(up_pre / GLU_LIMIT)
    return (up_soft + 1.0) * gate_soft * jax.nn.sigmoid(GLU_ALPHA * gate_soft)


class Work:
    def __init__(self):
        self.waiting = []
        self.done = {}
        self.pool = {}

    def add(self, name, make, *inputs):
        self.waiting.append([name, make, list(inputs)])

    def run(self, entry):
        _, make, inputs = entry
        return make(*(self.done[item] if isinstance(item, str) else item for item in inputs))

    def take(self, name):
        while name not in self.done:
            entry = self.waiting.pop(0)
            self.done[entry[0]] = self.run(entry)
        return self.done[name]

    def tie(self, *arrays, count=0, pool=()):
        taken = []
        for entry in self.waiting[:count]:
            result = self.run(entry)
            self.done[entry[0]] = result
            taken.append((entry[0], result))
        self.waiting = self.waiting[count:]
        coming = self.waiting[:2]
        held = [[item for item in entry[2] if not isinstance(item, str)] for entry in coming]
        arrays, made, held, pooled = lax.optimization_barrier(
            (arrays, [r for _, r in taken], held, [self.pool[name] for name in pool])
        )
        self.pool.update(zip(pool, pooled))
        for (name, _), result in zip(taken, made):
            self.done[name] = result
        for entry, kept in zip(coming, held):
            kept = list(kept)
            entry[2] = [item if isinstance(item, str) else kept.pop(0) for item in entry[2]]
        return arrays


class Line:
    def __init__(self, work):
        self.work = work
        index = lax.axis_index("seq")
        self.place, self.side = index // 2, index % 2
        at_low, at_high = self.place == 0, self.place == 3
        self.at_end = at_low | at_high
        self.at_low = at_low
        place = self.place
        self.order = [
            place,
            jnp.where(at_low, 1, place - 1),
            jnp.where(at_low, 2, jnp.where(at_high, 1, place + 1)),
            jnp.where(place < 2, 3, 0),
        ]

    @staticmethod
    def along(block, moves):
        route = [(2 * i + k, 2 * j + k) for i, j in moves for k in range(2)]
        return lax.ppermute(block, "seq", route)

    @staticmethod
    def across(block):
        return lax.ppermute(block, "seq", [(i, i ^ 1) for i in range(8)])

    def as_pair(self, own, other):
        first = jnp.where(self.side == 0, own, other)
        second = jnp.where(self.side == 0, other, own)
        return jnp.concatenate([first, second], axis=0)

    def gather(self, block, use, later=None, counts=(0, 0, 0, 0), pools=((), (), (), ())):
        tie = self.work.tie
        later = later or (lambda at, used: ())
        up, down, side_0 = (
            self.along(block, [(0, 1), (1, 2), (2, 3)]),
            self.along(block, [(1, 0), (2, 1), (3, 2)]),
            self.across(block),
        )
        up, down, side_0 = tie(up, down, side_0, count=counts[0], pool=pools[0])
        near = jnp.where(self.at_low, down, up)
        up_2, down_2, side_1 = (
            self.along(up, [(1, 2), (2, 3)]),
            self.along(down, [(2, 1), (1, 0)]),
            self.across(near),
        )
        used_0 = use(0, self.as_pair(block, side_0))
        up_2, down_2, side_1, down, near, used_0 = tie(
            up_2, down_2, side_1, down, near, used_0, count=counts[1], pool=pools[1]
        )
        sent_0 = later(0, used_0)
        second = up_2 + down_2
        far = jnp.where(self.at_end, second, down)
        third, side_2 = self.along(second, [(2, 3), (1, 0)]), self.across(far)
        used_1 = use(1, self.as_pair(near, side_1))
        third, side_2, second, far, used_1, sent_0 = tie(
            third, side_2, second, far, used_1, sent_0, count=counts[2], pool=pools[2]
        )
        sent_1 = later(1, used_1)
        last = jnp.where(self.at_end, third, second)
        side_3 = self.across(last)
        used_2 = use(2, self.as_pair(far, side_2))
        side_3, last, used_2, sent_1 = tie(
            side_3, last, used_2, sent_1, count=counts[3], pool=pools[3]
        )
        sent_2 = later(2, used_2)
        used_3 = use(3, self.as_pair(last, side_3))
        return [used_0, used_1, used_2, used_3], [sent_0, sent_1, sent_2, later(3, used_3)]

    def halves(self, pair):
        rows = pair.shape[0] // 2
        own = lax.dynamic_slice_in_dim(pair, self.side * rows, rows, 0)
        other = lax.dynamic_slice_in_dim(pair, (1 - self.side) * rows, rows, 0)
        return own, other

    def scatter(self, term, counts=(0, 0, 0, 0), pools=((), (), (), ())):
        tie = self.work.tie
        own_3, other_3 = self.halves(term(3))
        side_3 = self.across(other_3)
        own_2, other_2 = self.halves(term(2))
        side_3, other_2, own_2 = tie(side_3, other_2, own_2, count=counts[0], pool=pools[0])
        sum_3 = own_3.astype(F32) + side_3.astype(F32)
        step_1, side_2 = self.along(sum_3.astype(BF), [(0, 1), (3, 2)]), self.across(other_2)
        own_1, other_1 = self.halves(term(1))
        step_1, side_2, other_1, own_1 = tie(
            step_1, side_2, other_1, own_1, count=counts[1], pool=pools[1]
        )
        sum_2 = own_2.astype(F32) + side_2.astype(F32)
        sent = jnp.where(self.at_end, sum_2, sum_3 + step_1.astype(F32)).astype(BF)
        up, down, side_1 = (
            self.along(sent, [(0, 1), (1, 2)]),
            self.along(sent, [(3, 2), (2, 1)]),
            self.across(other_1),
        )
        own_0, other_0 = self.halves(term(0))
        up, down, side_1, own_0, other_0 = tie(
            up, down, side_1, own_0, other_0, count=counts[2], pool=pools[2]
        )
        sum_1 = own_1.astype(F32) + side_1.astype(F32)
        sent_up = jnp.where(self.at_low, sum_1, sum_2 + up.astype(F32)).astype(BF)
        sent_down = (sum_1 + down.astype(F32)).astype(BF)
        up, down, side_0 = (
            self.along(sent_up, [(0, 1), (1, 2), (2, 3)]),
            self.along(sent_down, [(1, 0), (2, 1), (3, 2)]),
            self.across(other_0),
        )
        if counts[3] is not None:
            up, down, side_0 = tie(up, down, side_0, count=counts[3], pool=pools[3])
        return own_0.astype(F32) + side_0.astype(F32) + up.astype(F32) + down.astype(F32)


class Whole:
    def __init__(self, work):
        self.order = [jnp.int32(0)]

    def gather(self, block, use, later=None, counts=(), pools=()):
        used = use(0, gather_seq(block))
        return [used], [later(0, used) if later else ()]

    def scatter(self, term, counts=(), pools=()):
        return scatter_seq(term(0)).astype(F32)


def gather_seq(block):
    return lax.all_gather(block, "seq", axis=0, tiled=True)


def scatter_seq(partial_rows):
    return lax.psum_scatter(partial_rows, "seq", scatter_dimension=0, tiled=True)


def to_core(block):
    return lax.ppermute(block, "fsdp", [(i, i ^ 1) for i in range(4)])


def to_chip(block):
    return lax.ppermute(block, "fsdp", [(i, i ^ 2) for i in range(4)])


def split_low(values):
    high = values.astype(BF)
    low = (values - high.astype(F32)).astype(BF)
    return high, low


def place_rows(whole, piece, start):
    return lax.dynamic_update_slice_in_dim(whole, piece, start, 0)


def per_device(
    layer_input,
    attn_gain,
    query_matrix,
    query_bias_vector,
    key_matrix,
    key_bias_vector,
    value_matrix,
    value_bias_vector,
    sink_logit_values,
    output_matrix,
    output_bias_vector,
    ffn_gain,
    router_weight,
    router_bias,
    expert_gate_up,
    expert_gate_up_bias,
    expert_down,
    expert_down_bias,
    route_ids,
    doc_lengths,
    out_cotangent,
):
    seq_count = lax.axis_size("seq")
    fsdp_count = lax.axis_size("fsdp")
    seq_index = lax.axis_index("seq")
    fsdp_index = lax.axis_index("fsdp")
    tokens_here, width = layer_input.shape[1:]
    choose_count = route_ids.shape[2]
    expert_count = seq_count
    length = seq_count * tokens_here
    block_capacity = max(2, tokens_here * choose_count * 5 // (4 * expert_count))
    capacity = block_capacity * seq_count
    padded = -(-(width + 3 * expert_count) // 128) * 128
    heads_here = QUERY_HEADS // seq_count
    shared_kv = seq_count > KEY_VALUE_HEADS
    q_width = heads_here * HEAD_DIM
    q_part, kv_part = query_matrix.shape[1], key_matrix.shape[1]
    work = Work()
    line = Line(work) if seq_count == 8 else Whole(work)
    chunk = length // len(line.order)
    starts = [place * chunk for place in line.order]
    last = len(starts) - 1

    def taken(rows, start):
        return lax.dynamic_slice_in_dim(rows, start, chunk, 0)

    member_here = jnp.any(
        route_ids[0][:, :, None] == jnp.arange(expert_count, dtype=jnp.int32), axis=1
    )
    cot_here = out_cotangent[0]
    ranks = jnp.cumsum(member_here.astype(jnp.int32), axis=0)
    slot_here = jnp.where(member_here, ranks, 0).astype(BF)

    part = attn_gain.shape[0]
    near_first = [fsdp_index ^ turn for turn in range(fsdp_count)]

    def from_all(piece):
        core, chip = to_core(piece), to_chip(piece)
        return [piece, core, chip, to_core(chip)]

    def in_order(pieces):
        core_bit, chip_bit = fsdp_index % 2 == 0, fsdp_index < 2
        pairs = []
        for own, other in ((pieces[0], pieces[1]), (pieces[2], pieces[3])):
            pairs.append((jnp.where(core_bit, own, other), jnp.where(core_bit, other, own)))
        first = [jnp.where(chip_bit, a, b) for a, b in zip(*pairs)]
        second = [jnp.where(chip_bit, b, a) for a, b in zip(*pairs)]
        return first + second

    kv_head = seq_index // max(1, seq_count // KEY_VALUE_HEADS)

    tiny = jnp.concatenate(
        [sink_logit_values, router_bias, query_bias_vector, key_bias_vector, value_bias_vector]
    )
    tiny = jnp.concatenate([tiny, jnp.zeros((part - tiny.shape[0],), BF)])
    small = jnp.concatenate(
        [
            attn_gain[None],
            ffn_gain[None],
            output_bias_vector[None],
            tiny[None],
            expert_down_bias,
            router_weight.T,
        ],
        axis=0,
    )
    work.pool["small"] = to_core(small), to_chip(small)
    work.pool["wo"] = output_matrix.T

    def parameters(query_matrix, key_matrix, value_matrix):
        small_core, small_chip = work.pool["small"]
        small_all = jnp.stack(in_order([small, small_core, small_chip, to_core(small_chip)]))
        wide = jnp.swapaxes(small_all, 0, 1).reshape(small.shape[0], width).astype(F32)
        attn_gain_f, ffn_gain_f, out_bias_f = wide[0], wide[1], wide[2]
        down_bias_f = wide[4 : 4 + expert_count]
        router_t = wide[4 + expert_count :].astype(BF)
        tiny_all = small_all[:, 3]
        places = [0]
        for piece in (sink_logit_values, router_bias, query_bias_vector, key_bias_vector, value_bias_vector):
            places.append(places[-1] + piece.shape[0])
        sinks_f, router_bias_f, q_bias, k_bias, v_bias = (
            tiny_all[:, a:b].astype(F32) for a, b in zip(places[:-1], places[1:])
        )
        sinks_f, router_bias_f = sinks_f.reshape(-1), router_bias_f.reshape(-1)
        k_bias, v_bias = k_bias.reshape(-1), v_bias.reshape(-1)
        q_bias = jnp.concatenate(
            [lax.dynamic_slice_in_dim(q_bias, at, 1, 0)[0] for at in near_first]
        )
        w_query = jnp.concatenate(from_all(query_matrix), axis=1)
        if shared_kv:

            def own_head(piece):
                whole = lax.all_gather(piece, ("seq", "fsdp"), axis=0, tiled=True)
                return lax.dynamic_slice_in_dim(whole, kv_head * HEAD_DIM, HEAD_DIM, 0)

            w_pair = jnp.concatenate([own_head(key_matrix.T), own_head(value_matrix.T)], axis=0)
            k_bias = own_head(key_bias_vector).astype(F32)
            v_bias = own_head(value_bias_vector).astype(F32)
        else:
            kv_pieces = in_order(from_all(jnp.concatenate([key_matrix.T, value_matrix.T], axis=0)))
            w_pair = jnp.concatenate(
                [piece[:kv_part] for piece in kv_pieces] + [piece[kv_part:] for piece in kv_pieces],
                axis=0,
            )
        lin_bias = jnp.concatenate([q_bias, k_bias, v_bias])
        return (
            attn_gain_f,
            ffn_gain_f,
            out_bias_f,
            down_bias_f,
            router_t,
            sinks_f,
            router_bias_f,
            w_query,
            w_pair,
            lin_bias,
        )

    work.add("parameters", parameters, query_matrix, key_matrix, value_matrix)

    columns = jnp.concatenate(
        [
            (seq_index * fsdp_count + at) * q_part + jnp.arange(q_part, dtype=jnp.int32)
            for at in near_first
        ]
    )
    whole_heads = q_part % HEAD_DIM == 0

    cosine_table, sine_table = rope_tables(length)
    doc_row = lax.dynamic_slice_in_dim(doc_lengths, fsdp_index, 1, 0)[0]
    doc_ends = jnp.cumsum(doc_row)

    def project(pair):
        pair_f = pair.astype(F32)
        normed = (pair_f * rms_scale(pair_f) * attn_gain_f).astype(BF)
        query_part = dot(normed, w_query, 1, 0) + lin_bias[:q_width]
        return normed, query_part, dot(normed, w_pair, 1, 1) + lin_bias[q_width:]

    pairs = []

    def arrive(at, pair):
        pairs.append(pair)
        return pair

    line.gather(
        layer_input[0],
        lambda at, pair: (work.take("parameters"), arrive(at, pair))[1],
        pools=(("small",), (), ("wo",), ()),
    )
    wo_t = jnp.concatenate(from_all(work.pool["wo"]), axis=1)
    (
        attn_gain_f,
        ffn_gain_f,
        out_bias_f,
        down_bias_f,
        router_t,
        sinks_f,
        router_bias_f,
        w_query,
        w_pair,
        lin_bias,
    ) = work.take("parameters")
    projected = [project(pair) for pair in pairs]
    normed_rows = jnp.zeros((length, width), BF)
    lin = jnp.zeros((length, q_width + 2 * HEAD_DIM), F32)
    for start, (normed, query_part, pair_part) in zip(starts, projected):
        normed_rows = place_rows(normed_rows, normed, start)
        lin = lax.dynamic_update_slice(lin, query_part, (start, 0))
        lin = lax.dynamic_update_slice(lin, pair_part, (start, q_width))
    if not whole_heads:
        order = jnp.argsort(columns)
        w_query = w_query[:, order]
        wo_t = wo_t[:, order]
        lin = jnp.concatenate([lin[:, :q_width][:, order], lin[:, q_width:]], axis=1)
        head_numbers = seq_index * heads_here + jnp.arange(heads_here, dtype=jnp.int32)
    else:
        head_numbers = columns[::HEAD_DIM] // HEAD_DIM
    head_lane = (head_numbers[:, None] == jnp.arange(QUERY_HEADS)[None, :]).astype(F32)
    sinks_here = jnp.sum(head_lane * sinks_f[None, :], axis=1)
    turned, heads = attend(lin, cosine_table, sine_table, doc_ends, sinks_here)
    attn_sum = line.scatter(
        lambda at: dot(taken(heads, starts[at]), wo_t, 1, 1).astype(BF), counts=(0, 0, 0, 0)
    )

    resid_in = layer_input[0].astype(F32)
    resid_mid = resid_in + attn_sum + out_bias_f
    norm_two = rms_scale(resid_mid)
    unit_mid = resid_mid * norm_two
    normed_mid = (unit_mid * ffn_gain_f).astype(BF)
    logits = dot(normed_mid, router_t, 1, 1) + router_bias_f
    gates = jax.nn.softmax(jnp.where(member_here, logits, -1e30), axis=-1)
    gates = jnp.where(member_here, gates, 0.0)
    gate_high, gate_low = split_low(gates)
    mid_packed = jnp.concatenate(
        [
            normed_mid,
            slot_here,
            gate_high,
            gate_low,
            jnp.zeros((tokens_here, padded - width - 3 * expert_count), BF),
        ],
        axis=1,
    )

    expert_lane = (jnp.arange(expert_count, dtype=jnp.int32) == seq_index).astype(F32)
    slots = block_capacity * (chunk // tokens_here)
    slot_number = jnp.arange(block_capacity, dtype=F32) + 1.0
    selects = {}

    def pick_rows(at, pair):
        rank = jnp.sum(pair[:, width : width + expert_count].astype(F32) * expert_lane, axis=1)
        blocks = chunk // tokens_here
        hit = slot_number[None, :, None] == rank.reshape(blocks, 1, tokens_here)
        same = jnp.eye(blocks, dtype=jnp.bool_)[:, None, :, None]
        select = (hit[:, :, None, :] & same).reshape(slots, chunk).astype(BF)
        return select, dot(select, pair, 1, 0).astype(BF)

    def send_rows(at, used):
        return to_core(used[1]), to_chip(used[1])

    spare = padded - width
    work.pool["cot"] = jnp.concatenate([cot_here, jnp.zeros((tokens_here, spare), BF)], axis=1)
    picked, sent = line.gather(mid_packed, pick_rows, send_rows, pools=((), ("cot",), (), ()))
    selects = [select for select, _ in picked]
    own_rows = [rows for _, rows in picked]
    core_rows = [core for core, _ in sent]
    chip_rows = [chip for _, chip in sent]
    units_w = jnp.pad(jnp.swapaxes(expert_gate_up[0], 1, 2), ((0, 0), (0, 0), (0, spare)))
    down_w = jnp.pad(expert_down[0], ((0, 0), (0, spare)))
    units_b = expert_gate_up_bias[0].astype(F32)[:, None, :]

    def joined(pieces):
        whole = jnp.zeros((2 * capacity, pieces[0].shape[1]), BF)
        first = 0
        for piece in pieces:
            whole = place_rows(whole, piece, first)
            first += piece.shape[0]
        return whole

    def einsum(form, left, right):
        return jnp.einsum(form, left, right, preferred_element_type=F32)

    def hidden_step(rows):
        tail = rows[:, width + expert_count :].astype(F32)
        share = jnp.sum(
            (tail[:, :expert_count] + tail[:, expert_count : 2 * expert_count]) * expert_lane,
            axis=1,
            keepdims=True,
        )
        before = einsum("rd,khd->krh", rows, units_w) + units_b
        hidden = swiglu(before[0], before[1]).astype(BF)
        return share, before, hidden, (hidden.astype(F32) * share).astype(BF)

    def mix_step(made):
        return dot(made[3], down_w, 1, 0).astype(BF)

    def back_step(made, cot):
        share, before, hidden, _ = made
        grad_hidden = dot(cot, down_w, 1, 1)
        score = jnp.sum(hidden.astype(F32) * grad_hidden, axis=1, keepdims=True)
        _, glu_back = jax.vjp(swiglu, before[0], before[1])
        grad_gate_pre, grad_up_pre = glu_back(grad_hidden * share)
        return score, jnp.stack([grad_gate_pre.astype(BF), grad_up_pre.astype(BF)])

    def row_step(made):
        return einsum("krh,khd->rd", made, units_w).astype(BF)

    cot_rows = gather_seq(work.pool["cot"])
    near = joined(own_rows + core_rows)
    select_all = jnp.zeros((capacity, length), BF)
    for at, (select, start) in enumerate(zip(selects, starts)):
        select_all = lax.dynamic_update_slice(select_all, select, (at * slots, start))
    made_n = hidden_step(near)
    select_chip = to_chip(select_all)
    mix_n = mix_step(made_n)
    made_n, chip_rows, mix_n = work.tie(made_n, chip_rows, mix_n)
    far = joined(chip_rows + [to_core(chip) for chip in chip_rows])
    made_o = hidden_step(far)
    mix_o = mix_step(made_o)
    mix_core_n, mix_core_o = to_core(mix_n[capacity:]), to_core(mix_o[capacity:])
    cot_rows, made_n, made_o, mix_n, mix_o, mix_core_n, select_chip = work.tie(
        cot_rows, made_n, made_o, mix_n, mix_o, mix_core_n, select_chip
    )
    cot_own = dot(select_all, cot_rows, 1, 0).astype(BF)
    half = (len(selects) + 1) // 2 * slots
    cot_own = [cot_own[:half], cot_own[half:]] if half < capacity else [cot_own]
    cot_first = to_chip(cot_own[0])
    cot_near = joined(cot_own + [to_core(rows) for rows in cot_own])
    def core_sum(part, from_core):
        return (part[:capacity].astype(F32) + from_core.astype(F32)).astype(BF)

    def total(near_part, from_core, arrived, at):
        return (
            slot_rows(near_part, at).astype(F32)
            + slot_rows(from_core, at).astype(F32)
            + arrived.astype(F32)
        )

    def slot_rows(rows, at):
        return rows[at * slots : (at + 1) * slots]

    low_rows = (len(starts) // 2) * slots

    def score_step(back_n, back_o):
        scores = jnp.concatenate([back_n[0], back_o[0]], axis=1)
        return scores[:capacity] + to_core(scores[capacity:])

    mix_own = dot(select_all, core_sum(mix_n, mix_core_n), 0, 0).astype(BF)
    mix_other = dot(select_chip, core_sum(mix_o, mix_core_o), 0, 0).astype(BF)
    mix_own, mix_other, cot_near, cot_first, cot_own = work.tie(
        mix_own, mix_other, cot_near, cot_first, cot_own
    )
    cot_chip = [cot_first] + [to_chip(rows) for rows in cot_own[1:]]
    mix_own, mix_other = scatter_seq(mix_own), scatter_seq(mix_other)

    back_n = back_step(made_n, cot_near)
    row_n = row_step(back_n[1])

    back_n, row_n, cot_chip = work.tie(back_n, row_n, cot_chip)
    row_near_core = to_core(row_n[capacity:])
    cot_far = joined(cot_chip + [to_core(rows) for rows in cot_chip])
    back_o = back_step(made_o, cot_far)
    back_n, back_o, row_near_core = work.tie(back_n, back_o, row_near_core)
    score = score_step(back_n, back_o)
    score = score[:, :1] + to_chip(score[:, 1:])
    row_o_core = row_step(back_o[1][:, capacity:])
    row_o_core, back_o, score = work.tie(row_o_core, back_o, score)
    row_far_core = to_core(row_o_core)
    row_o = row_step(back_o[1][:, :capacity])
    (score_n, low_n), (score_o, low_o) = back_n, back_o


    def chunk_of(low, high, at):
        first = at * slots
        if first < low_rows:
            return low[first : first + slots]
        return high[first - low_rows : first - low_rows + slots]

    def units_step(low_n, rows_n, low_o, rows_o):
        return einsum("krh,rd->khd", low_n, rows_n[:, :width]) + einsum(
            "krh,rd->khd", low_o, rows_o[:, :width]
        )

    def down_step(hidden_n, cot_n, hidden_o, cot_o):
        return dot(hidden_n, cot_n[:, :width], 0, 0) + dot(hidden_o, cot_o[:, :width], 0, 0)

    work.add("units", units_step, low_n, near, low_o, far)
    work.add("down", down_step, made_n[3], cot_near, made_o[3], cot_far)
    row_far_core, row_o, mix_own = work.tie(row_far_core, row_o, mix_own)
    row_sum_far = core_sum(row_o, row_far_core)
    row_high, row_low = to_chip(row_sum_far[low_rows:]), row_sum_far[:low_rows]
    row_high, row_low = work.tie(row_high, row_low, count=1)
    row_low = to_chip(row_low)
    def back_term(at):
        row_sum = total(row_n, row_near_core, chunk_of(row_low, row_high, at), at)
        grad_high, grad_low = split_low(slot_rows(score, at) * expert_lane)
        back_packed = jnp.concatenate(
            [
                row_sum[:, :width].astype(BF),
                grad_high,
                grad_low,
                jnp.zeros((slots, padded - width - 2 * expert_count), BF),
            ],
            axis=1,
        )
        return dot(selects[at], back_packed, 0, 0).astype(BF)

    work.pool["mix"] = mix_other
    back = line.scatter(back_term, counts=(1, 0, 0, 0))

    cot_f = cot_here.astype(F32)
    grad_gates = (
        back[:, width : width + expert_count]
        + back[:, width + expert_count : width + 2 * expert_count]
        + dot(cot_f, down_bias_f, 1, 1, EXACT)
    )
    mean_gate = jnp.sum(gates * grad_gates, axis=-1, keepdims=True)
    grad_logits = gates * (grad_gates - mean_gate)
    router_grad_t = dot(grad_logits, normed_mid.astype(F32), 0, 0, EXACT)
    router_bias_grad = jnp.sum(grad_logits, axis=0)
    down_bias_grad = dot(gates, cot_f, 0, 0, EXACT)
    grad_normed_mid = back[:, :width] + dot(grad_logits, router_t.astype(F32), 1, 0, EXACT)
    ffn_gain_grad = jnp.sum(grad_normed_mid * unit_mid, axis=0)
    grad_unit_mid = grad_normed_mid * ffn_gain_f
    grad_mid = (
        norm_two
        * (grad_unit_mid - unit_mid * jnp.mean(grad_unit_mid * unit_mid, axis=-1, keepdims=True))
        + cot_f
    )
    grad_attn = grad_mid.astype(BF)
    out_bias_grad = jnp.sum(grad_attn.astype(F32), axis=0)

    def to_core_owners(blocks, kind=BF):
        both = to_core(jnp.stack([blocks[1], blocks[3]]).astype(kind))
        return blocks[0] + both[0].astype(F32), (blocks[2] + both[1].astype(F32)).astype(kind)

    def to_owners(sums):
        own, chip = sums
        return own + to_chip(chip).astype(F32)

    def fsdp_sum(values):
        values = values + to_core(values)
        return values + to_chip(values)

    def seq_step(step):
        def add_other(values):
            return values + lax.ppermute(values, "seq", [(i, i ^ step) for i in range(seq_count)])

        return add_other

    def own_part(whole_array, axis_number):
        piece_size = whole_array.shape[axis_number] // fsdp_count
        return lax.dynamic_slice_in_dim(
            whole_array, fsdp_index * piece_size, piece_size, axis_number
        )

    tiny_grad = jnp.concatenate([router_bias_grad, jnp.zeros((width - expert_count,), F32)])[None]
    small_grad = jnp.concatenate(
        [out_bias_grad[None], ffn_gain_grad[None], tiny_grad, down_bias_grad, router_grad_t],
        axis=0,
    )

    work.add("small_fsdp", fsdp_sum, small_grad)

    attn_rows = jnp.zeros((length, width), BF)
    grad_heads = jnp.zeros((length, q_width), BF)

    def head_grads(at, pair):
        return pair, dot(pair, wo_t, 1, 0).astype(BF)

    grads, _ = line.gather(
        grad_attn, head_grads, counts=(0, 0, 1, 0), pools=(("mix",), (), (), ())
    )
    mixture = (mix_own.astype(F32) + to_chip(work.pool["mix"]).astype(F32))[:, :width]
    mixture = mixture + dot(gates, down_bias_f, 1, 0, EXACT)
    layer_output = (resid_mid + mixture).astype(BF)[None]
    for start, (pair, grad_part) in zip(starts, grads):
        attn_rows = place_rows(attn_rows, pair, start)
        grad_heads = place_rows(grad_heads, grad_part, start)

    def column_blocks(whole):
        if back_order is not None:
            whole = whole[:, back_order]
        return [whole[:, at * q_part : (at + 1) * q_part] for at in range(fsdp_count)]

    order = None if whole_heads else jnp.argsort(columns)
    back_order = None if whole_heads else jnp.argsort(order)
    out_sums = to_core_owners(column_blocks(dot(attn_rows, heads, 0, 0)))
    lin_grad, lin_sums, sink_here_grad = attend_back(
        turned, cosine_table, sine_table, doc_ends, sinks_here, grad_heads
    )

    lin_grad, lin_sums, out_sums = work.tie(lin_grad, lin_sums, out_sums)

    def query_step(rows, grads):
        return dot(rows, grads[:, :q_width], 0, 0)

    def pair_step(rows, grads):
        return dot(grads[:, q_width:], rows, 0, 0)

    def gain_step(query_w_part, pair_w_part):
        attn_gain_grad = (
            jnp.sum(query_w_part * w_query.astype(F32), axis=1)
            + jnp.sum(pair_w_part * w_pair.astype(F32), axis=0)
        ) / attn_gain_f
        sink_all_grad = jnp.sum(head_lane * sink_here_grad[:, None], axis=0)
        sink_row = jnp.concatenate([sink_all_grad, jnp.zeros((width - QUERY_HEADS,), F32)])
        return jnp.stack([attn_gain_grad, sink_row])

    def sums_step(lin_sums):
        query_sums = lin_sums[:q_width]
        if back_order is not None:
            query_sums = query_sums[back_order]
        pieces = [query_sums[at * q_part : (at + 1) * q_part] for at in range(fsdp_count)]
        return fsdp_sum(jnp.concatenate(in_order(pieces) + [lin_sums[q_width:]])[None])[0]

    def pair_sum(pair_w_part):
        if shared_kv:
            return ()
        summed = pair_w_part + to_core(pair_w_part.astype(BF)).astype(F32)
        return summed + to_chip(summed.astype(BF)).astype(F32)

    work.add("query_w", query_step, normed_rows, lin_grad)
    work.add("pair_w", pair_step, normed_rows, lin_grad)
    work.add("out_chip", lambda own, chip: to_owners((own, chip)), *out_sums)
    work.add("query_core", lambda whole: to_core_owners(column_blocks(whole)), "query_w")
    work.add("gain", gain_step, "query_w", "pair_w")
    work.add("query_chip", to_owners, "query_core")
    work.add("gain_core", lambda values: values + to_core(values), "gain")
    work.add("sums", sums_step, lin_sums)
    work.add("pair_sum", pair_sum, "pair_w")
    work.add(
        "all_1",
        lambda values, small: jnp.concatenate([values + to_chip(values), small]),
        "gain_core",
        "small_fsdp",
    )
    step = 1
    while step < seq_count:
        work.add("all_%d" % (2 * step), seq_step(step), "all_%d" % step)
        step *= 2

    def input_term(at):
        grad_part = taken(lin_grad, starts[at])
        return (
            dot(grad_part[:, :q_width], w_query, 1, 1) + dot(grad_part[:, q_width:], w_pair, 1, 0)
        ).astype(BF)

    grad_normed_in = line.scatter(input_term, counts=(1, 3, 2, 4))
    query_w_own = work.take("query_chip")
    out_w_own = work.take("out_chip").T
    pair_all, small_sum = work.take("pair_sum"), work.take("all_%d" % seq_count)
    small_own = own_part(small_sum, 1)
    down_grad = work.take("down")
    gate_up_grad = jnp.swapaxes(work.take("units"), 1, 2)
    gate_up_bias_grad = jnp.sum(low_n.astype(F32), axis=1) + jnp.sum(low_o.astype(F32), axis=1)

    resid_scale = rms_scale(resid_in)
    unit_in = resid_in * resid_scale
    grad_unit_in = grad_normed_in * attn_gain_f
    input_grad = (
        resid_scale
        * (grad_unit_in - unit_in * jnp.mean(grad_unit_in * unit_in, axis=-1, keepdims=True))
        + grad_mid
    )

    sums = work.take("sums")
    query_b_own = own_part(sums[: fsdp_count * q_part], 0)
    if shared_kv:

        def whole_sum(part_grad):
            whole = jnp.zeros((KEY_VALUE_HEADS * HEAD_DIM,) + part_grad.shape[1:], F32)
            whole = lax.dynamic_update_slice_in_dim(whole, part_grad, kv_head * HEAD_DIM, 0)
            return lax.psum_scatter(whole, ("seq", "fsdp"), scatter_dimension=0, tiled=True)

        pair_w_part = work.take("pair_w")
        key_w_own = whole_sum(pair_w_part[:HEAD_DIM]).T
        value_w_own = whole_sum(pair_w_part[HEAD_DIM:]).T
        key_b_own = whole_sum(lin_sums[q_width : q_width + HEAD_DIM])
        value_b_own = whole_sum(lin_sums[q_width + HEAD_DIM :])
    else:
        key_w_own = own_part(pair_all[:HEAD_DIM], 0).T
        value_w_own = own_part(pair_all[HEAD_DIM:], 0).T
        key_b_own, value_b_own = (
            own_part(sums[q_width : q_width + HEAD_DIM], 0),
            own_part(sums[q_width + HEAD_DIM :], 0),
        )

    return (
        layer_output,
        input_grad[None],
        small_own[0],
        query_w_own,
        query_b_own,
        key_w_own,
        key_b_own,
        value_w_own,
        value_b_own,
        own_part(small_sum[1, :QUERY_HEADS], 0),
        out_w_own,
        small_own[2],
        small_own[3],
        small_own[5 + expert_count :].T,
        own_part(small_sum[4, :expert_count], 0),
        gate_up_grad[None],
        gate_up_bias_grad[None],
        down_grad[None],
        small_own[5 : 5 + expert_count],
    )


def solution(mesh):
    return jax.shard_map(
        per_device,
        mesh=mesh,
        in_specs=(
            P("fsdp", "seq", None),
            P("fsdp"),
            P(None, ("seq", "fsdp")),
            P(("seq", "fsdp")),
            P(None, ("seq", "fsdp")),
            P(("seq", "fsdp")),
            P(None, ("seq", "fsdp")),
            P(("seq", "fsdp")),
            P("fsdp"),
            P(("seq", "fsdp"), None),
            P("fsdp"),
            P("fsdp"),
            P("fsdp", None),
            P("fsdp"),
            P("seq", None, None, "fsdp"),
            P("seq", None, "fsdp"),
            P("seq", "fsdp", None),
            P(None, "fsdp"),
            P("fsdp", "seq", None),
            P(),
            P("fsdp", "seq", None),
        ),
        out_specs=(
            P("fsdp", "seq", None),
            P("fsdp", "seq", None),
            P("fsdp"),
            P(None, ("seq", "fsdp")),
            P(("seq", "fsdp")),
            P(None, ("seq", "fsdp")),
            P(("seq", "fsdp")),
            P(None, ("seq", "fsdp")),
            P(("seq", "fsdp")),
            P("fsdp"),
            P(("seq", "fsdp"), None),
            P("fsdp"),
            P("fsdp"),
            P("fsdp", None),
            P("fsdp"),
            P("seq", None, None, "fsdp"),
            P("seq", None, "fsdp"),
            P("seq", "fsdp", None),
            P(None, "fsdp"),
        ),
        check_vma=False,
    )
```

```python
import jax
import jax.numpy as jnp
from jax import lax
from jax.experimental import pallas as pl
from jax.experimental.pallas import tpu as pltpu
from jax.sharding import PartitionSpec as P

QUERY_HEADS = 64
KEY_VALUE_HEADS = 8
HEAD_DIM = 64
WINDOW_LENGTH = 128


ROPE_BASE = 150000.0
NORM_EPS = 1e-05
GLU_ALPHA = 1.702
GLU_LIMIT = 7.0
EXACT = lax.Precision.HIGHEST
BF = jnp.bfloat16
F32 = jnp.float32
VMEM_BYTES = 60 * 2**20


def dot(left, right, left_dim, right_dim, precision=None):
    return lax.dot_general(
        left,
        right,
        (((left_dim,), (right_dim,)), ((), ())),
        precision=precision,
        preferred_element_type=jnp.float32,
    )


def turn_halves(values, cosines, sines):
    rows, width = values.shape
    half = HEAD_DIM // 2
    lane = lax.broadcasted_iota(jnp.int32, (rows, width), 1) % HEAD_DIM
    ahead = pltpu.roll(values, width - half, 1)
    behind = pltpu.roll(values, half, 1)
    other = jnp.where(lane < half, ahead, behind)
    copies = width // cosines.shape[1]
    wide_cos = jnp.concatenate([cosines] * copies, axis=1)
    wide_sin = jnp.concatenate([sines] * copies, axis=1)
    return values * wide_cos + other * wide_sin


def turn_keys(pair, cosines, sines, direction):
    lane = lax.broadcasted_iota(jnp.int32, pair.shape, 1)
    keys = lane < HEAD_DIM
    return turn_halves(pair, jnp.where(keys, cosines, 1.0), jnp.where(keys, direction * sines, 0.0))


def stack_heads(rows):
    return jnp.concatenate(
        [rows[:, at : at + HEAD_DIM] for at in range(0, rows.shape[1], HEAD_DIM)], axis=0
    )


def unstack_heads(stacked, rows):
    return jnp.concatenate(
        [stacked[at : at + rows] for at in range(0, stacked.shape[0], rows)], axis=1
    )


def block_probs(block, ends_ref, sinks_ref, queries, keys, rows):
    heads = queries.shape[0] // rows
    spread = lax.broadcasted_iota(jnp.int32, (rows, 2 * rows), 0)
    key_at = lax.broadcasted_iota(jnp.int32, (rows, 2 * rows), 1)
    position = block * rows + spread
    key_pos = (block - 1) * rows + key_at
    offset = position - key_pos
    allowed = (key_pos >= 0) & (offset >= 0) & (offset <= WINDOW_LENGTH)
    for document in range(ends_ref.shape[0]):
        end = ends_ref[document]
        allowed = allowed & ((position >= end) == (key_pos >= end))
    scores = dot(queries, keys, 1, 1) * 0.125
    scores = scores.reshape(heads, rows, 2 * rows)
    scores = jnp.where(allowed[None], scores, -1e30)
    head = lax.broadcasted_iota(jnp.int32, (heads, rows, 1), 0)
    sink = jnp.zeros((heads, rows, 1), F32)
    for at in range(heads):
        sink = jnp.where(head == at, sinks_ref[at], sink)
    top = jnp.maximum(jnp.max(scores, axis=-1, keepdims=True), sink)
    weights = jnp.exp(scores - top)
    sink_weight = jnp.exp(sink - top)
    inverse = 1.0 / (jnp.sum(weights, axis=-1, keepdims=True) + sink_weight)
    probs = (weights * inverse).reshape(heads * rows, 2 * rows)
    return probs, sink_weight * inverse


def attend_kernel(
    ends_ref, sinks_ref, lin_ref, before_ref, cos_ref, sin_ref, cos_before_ref, sin_before_ref,
    turned_ref, heads_ref,
):
    block = pl.program_id(0)
    rows = lin_ref.shape[0]
    wide = lin_ref.shape[1] - 2 * HEAD_DIM
    cosines, sines = cos_ref[...], sin_ref[...]
    queries = turn_halves(lin_ref[:, :wide], cosines, sines).astype(BF)
    own = turn_keys(lin_ref[:, wide:], cosines, sines, 1.0).astype(BF)
    before = turn_keys(before_ref[...], cos_before_ref[...], sin_before_ref[...], 1.0).astype(BF)
    turned_ref[:, :wide] = queries
    turned_ref[:, wide:] = own
    pair = jnp.concatenate([before, own], axis=0)
    probs, _ = block_probs(
        block, ends_ref, sinks_ref, stack_heads(queries), pair[:, :HEAD_DIM], rows
    )
    mixed = dot(probs.astype(BF), pair[:, HEAD_DIM:], 1, 0)
    heads_ref[...] = unstack_heads(mixed.astype(BF), rows)


def attend(lin, cosines, sines, doc_ends, sinks):
    length, full = lin.shape
    rows = WINDOW_LENGTH
    wide = full - 2 * HEAD_DIM
    pair_at = wide // (2 * HEAD_DIM)
    smem = pl.BlockSpec(memory_space=pltpu.SMEM)
    here = lambda block: (block, 0)
    previous = lambda block: (jnp.maximum(block - 1, 0), 0)
    table = pl.BlockSpec((rows, 2 * HEAD_DIM), here)
    table_before = pl.BlockSpec((rows, 2 * HEAD_DIM), previous)
    return pl.pallas_call(
        attend_kernel,
        grid=(length // rows,),
        in_specs=[
            smem,
            smem,
            pl.BlockSpec((rows, full), here),
            pl.BlockSpec((rows, 2 * HEAD_DIM), lambda block: (jnp.maximum(block - 1, 0), pair_at)),
            table,
            table,
            table_before,
            table_before,
        ],
        out_specs=[pl.BlockSpec((rows, full), here), pl.BlockSpec((rows, wide), here)],
        out_shape=[
            jax.ShapeDtypeStruct((length, full), BF),
            jax.ShapeDtypeStruct((length, wide), BF),
        ],
        compiler_params=pltpu.CompilerParams(vmem_limit_bytes=VMEM_BYTES),
        cost_estimate=pl.CostEstimate(
            flops=8 * length * rows * full, bytes_accessed=10 * length * full,
            transcendentals=2 * length * rows * wide // HEAD_DIM,
        ),
    )(doc_ends, sinks, lin, lin, cosines, sines, cosines, sines)


def attend_back_kernel(
    ends_ref, sinks_ref, turned_ref, before_ref, cos_ref, sin_ref, grad_ref,
    out_ref, sums_ref, sink_ref, carry_ref,
):
    step = pl.program_id(0)
    block = pl.num_programs(0) - 1 - step
    rows = turned_ref.shape[0]
    wide = turned_ref.shape[1] - 2 * HEAD_DIM

    @pl.when(step == 0)
    def _():
        carry_ref[...] = jnp.zeros_like(carry_ref)
        sums_ref[...] = jnp.zeros_like(sums_ref)
        sink_ref[...] = jnp.zeros_like(sink_ref)

    queries = stack_heads(turned_ref[:, :wide])
    grads = stack_heads(grad_ref[...])
    pair = jnp.concatenate([before_ref[...], turned_ref[:, wide:]], axis=0)
    keys, values = pair[:, :HEAD_DIM], pair[:, HEAD_DIM:]
    probs, sink_share = block_probs(block, ends_ref, sinks_ref, queries, keys, rows)
    grad_probs = dot(grads, values, 1, 1)
    row_delta = jnp.sum(probs * grad_probs, axis=-1, keepdims=True)
    grad_scores = (probs * (grad_probs - row_delta)).astype(BF)
    heads = wide // HEAD_DIM
    sink_part = sink_share * row_delta.reshape(heads, rows, 1)
    sink_ref[...] -= jnp.broadcast_to(jnp.sum(sink_part, axis=1), sink_ref.shape)
    grad_query = unstack_heads(dot(grad_scores, keys, 1, 0) * 0.125, rows)
    grad_pair = jnp.concatenate(
        [dot(grad_scores, queries, 0, 0) * 0.125, dot(probs.astype(BF), grads, 0, 0)], axis=1
    )
    own_pair = grad_pair[rows:] + carry_ref[...]
    carry_ref[...] = grad_pair[:rows]
    cosines, sines = cos_ref[...], sin_ref[...]
    query_out = turn_halves(grad_query, cosines, -sines).astype(BF)
    pair_out = turn_keys(own_pair, cosines, sines, -1.0).astype(BF)
    out_ref[:, :wide] = query_out
    out_ref[:, wide:] = pair_out
    sums_ref[:, :wide] += jnp.broadcast_to(
        jnp.sum(query_out.astype(F32), axis=0, keepdims=True), (sums_ref.shape[0], wide)
    )
    sums_ref[:, wide:] += jnp.broadcast_to(
        jnp.sum(pair_out.astype(F32), axis=0, keepdims=True), (sums_ref.shape[0], 2 * HEAD_DIM)
    )


def attend_back(turned, cosines, sines, doc_ends, sinks, grads):
    length, full = turned.shape
    rows = WINDOW_LENGTH
    wide = full - 2 * HEAD_DIM
    heads = wide // HEAD_DIM
    pair_at = wide // (2 * HEAD_DIM)
    last = length // rows - 1
    smem = pl.BlockSpec(memory_space=pltpu.SMEM)
    here = lambda step: (last - step, 0)
    still = lambda step: (0, 0)
    table = pl.BlockSpec((rows, 2 * HEAD_DIM), here)
    grad_all, sums, sink_grad = pl.pallas_call(
        attend_back_kernel,
        grid=(length // rows,),
        in_specs=[
            smem,
            smem,
            pl.BlockSpec((rows, full), here),
            pl.BlockSpec(
                (rows, 2 * HEAD_DIM), lambda step: (jnp.maximum(last - step - 1, 0), pair_at)
            ),
            table,
            table,
            pl.BlockSpec((rows, wide), here),
        ],
        out_specs=[
            pl.BlockSpec((rows, full), here),
            pl.BlockSpec((8, full), still),
            pl.BlockSpec((heads, 128), still),
        ],
        out_shape=[
            jax.ShapeDtypeStruct((length, full), BF),
            jax.ShapeDtypeStruct((8, full), F32),
            jax.ShapeDtypeStruct((heads, 128), F32),
        ],
        scratch_shapes=[pltpu.VMEM((rows, 2 * HEAD_DIM), F32)],
        compiler_params=pltpu.CompilerParams(vmem_limit_bytes=VMEM_BYTES),
        cost_estimate=pl.CostEstimate(
            flops=20 * length * rows * full, bytes_accessed=10 * length * full,
            transcendentals=2 * length * rows * heads,
        ),
    )(doc_ends, sinks, turned, turned, cosines, sines, grads)
    return grad_all, sums[0], sink_grad[:, 0]


def rms_scale(values):
    return lax.rsqrt(jnp.mean(values * values, axis=-1, keepdims=True) + NORM_EPS)


def rope_tables(length):
    lane = jnp.arange(2 * HEAD_DIM, dtype=jnp.int32)
    frequency = ROPE_BASE ** (-(lane % (HEAD_DIM // 2)).astype(F32) * 2.0 / HEAD_DIM)
    angles = jnp.arange(length, dtype=F32)[:, None] * frequency[None, :]
    sign = jnp.where(lane % HEAD_DIM < HEAD_DIM // 2, -1.0, 1.0)
    return jnp.cos(angles), jnp.sin(angles) * sign


def swiglu(gate_pre, up_pre):
    gate_soft = GLU_LIMIT - jax.nn.softplus(GLU_LIMIT - gate_pre)
    up_soft = GLU_LIMIT * jnp.tanh(up_pre / GLU_LIMIT)
    return (up_soft + 1.0) * gate_soft * jax.nn.sigmoid(GLU_ALPHA * gate_soft)


class Work:
    def __init__(self):
        self.waiting = []
        self.done = {}
        self.pool = {}

    def add(self, name, make, *inputs):
        self.waiting.append([name, make, list(inputs)])

    def run(self, entry):
        _, make, inputs = entry
        return make(*(self.done[item] if isinstance(item, str) else item for item in inputs))

    def take(self, name):
        while name not in self.done:
            entry = self.waiting.pop(0)
            self.done[entry[0]] = self.run(entry)
        return self.done[name]

    def tie(self, *arrays, count=0, pool=()):
        taken = []
        for entry in self.waiting[:count]:
            result = self.run(entry)
            self.done[entry[0]] = result
            taken.append((entry[0], result))
        self.waiting = self.waiting[count:]
        coming = self.waiting[:2]
        held = [[item for item in entry[2] if not isinstance(item, str)] for entry in coming]
        arrays, made, held, pooled = lax.optimization_barrier(
            (arrays, [r for _, r in taken], held, [self.pool[name] for name in pool])
        )
        self.pool.update(zip(pool, pooled))
        for (name, _), result in zip(taken, made):
            self.done[name] = result
        for entry, kept in zip(coming, held):
            kept = list(kept)
            entry[2] = [item if isinstance(item, str) else kept.pop(0) for item in entry[2]]
        return arrays


class Line:
    def __init__(self, work):
        self.work = work
        index = lax.axis_index("seq")
        self.place, self.side = index // 2, index % 2
        at_low, at_high = self.place == 0, self.place == 3
        self.at_end = at_low | at_high
        self.at_low = at_low
        place = self.place
        self.order = [
            place,
            jnp.where(at_low, 1, place - 1),
            jnp.where(at_low, 2, jnp.where(at_high, 1, place + 1)),
            jnp.where(place < 2, 3, 0),
        ]

    @staticmethod
    def along(block, moves):
        route = [(2 * i + k, 2 * j + k) for i, j in moves for k in range(2)]
        return lax.ppermute(block, "seq", route)

    @staticmethod
    def across(block):
        return lax.ppermute(block, "seq", [(i, i ^ 1) for i in range(8)])

    def as_pair(self, own, other):
        first = jnp.where(self.side == 0, own, other)
        second = jnp.where(self.side == 0, other, own)
        return jnp.concatenate([first, second], axis=0)

    def gather(self, block, use, later=None, counts=(0, 0, 0, 0), pools=((), (), (), ())):
        tie = self.work.tie
        later = later or (lambda at, used: ())
        up, down, side_0 = (
            self.along(block, [(0, 1), (1, 2), (2, 3)]),
            self.along(block, [(1, 0), (2, 1), (3, 2)]),
            self.across(block),
        )
        up, down, side_0 = tie(up, down, side_0, count=counts[0], pool=pools[0])
        near = jnp.where(self.at_low, down, up)
        up_2, down_2, side_1 = (
            self.along(up, [(1, 2), (2, 3)]),
            self.along(down, [(2, 1), (1, 0)]),
            self.across(near),
        )
        used_0 = use(0, self.as_pair(block, side_0))
        up_2, down_2, side_1, down, near, used_0 = tie(
            up_2, down_2, side_1, down, near, used_0, count=counts[1], pool=pools[1]
        )
        sent_0 = later(0, used_0)
        second = up_2 + down_2
        far = jnp.where(self.at_end, second, down)
        third, side_2 = self.along(second, [(2, 3), (1, 0)]), self.across(far)
        used_1 = use(1, self.as_pair(near, side_1))
        third, side_2, second, far, used_1, sent_0 = tie(
            third, side_2, second, far, used_1, sent_0, count=counts[2], pool=pools[2]
        )
        sent_1 = later(1, used_1)
        last = jnp.where(self.at_end, third, second)
        side_3 = self.across(last)
        used_2 = use(2, self.as_pair(far, side_2))
        side_3, last, used_2, sent_1 = tie(
            side_3, last, used_2, sent_1, count=counts[3], pool=pools[3]
        )
        sent_2 = later(2, used_2)
        used_3 = use(3, self.as_pair(last, side_3))
        return [used_0, used_1, used_2, used_3], [sent_0, sent_1, sent_2, later(3, used_3)]

    def halves(self, pair):
        rows = pair.shape[0] // 2
        own = lax.dynamic_slice_in_dim(pair, self.side * rows, rows, 0)
        other = lax.dynamic_slice_in_dim(pair, (1 - self.side) * rows, rows, 0)
        return own, other

    def scatter(self, term, counts=(0, 0, 0, 0), pools=((), (), (), ())):
        tie = self.work.tie
        own_3, other_3 = self.halves(term(3))
        side_3 = self.across(other_3)
        own_2, other_2 = self.halves(term(2))
        side_3, other_2, own_2 = tie(side_3, other_2, own_2, count=counts[0], pool=pools[0])
        sum_3 = own_3.astype(F32) + side_3.astype(F32)
        step_1, side_2 = self.along(sum_3.astype(BF), [(0, 1), (3, 2)]), self.across(other_2)
        own_1, other_1 = self.halves(term(1))
        step_1, side_2, other_1, own_1 = tie(
            step_1, side_2, other_1, own_1, count=counts[1], pool=pools[1]
        )
        sum_2 = own_2.astype(F32) + side_2.astype(F32)
        sent = jnp.where(self.at_end, sum_2, sum_3 + step_1.astype(F32)).astype(BF)
        up, down, side_1 = (
            self.along(sent, [(0, 1), (1, 2)]),
            self.along(sent, [(3, 2), (2, 1)]),
            self.across(other_1),
        )
        own_0, other_0 = self.halves(term(0))
        up, down, side_1, own_0, other_0 = tie(
            up, down, side_1, own_0, other_0, count=counts[2], pool=pools[2]
        )
        sum_1 = own_1.astype(F32) + side_1.astype(F32)
        sent_up = jnp.where(self.at_low, sum_1, sum_2 + up.astype(F32)).astype(BF)
        sent_down = (sum_1 + down.astype(F32)).astype(BF)
        up, down, side_0 = (
            self.along(sent_up, [(0, 1), (1, 2), (2, 3)]),
            self.along(sent_down, [(1, 0), (2, 1), (3, 2)]),
            self.across(other_0),
        )
        if counts[3] is not None:
            up, down, side_0 = tie(up, down, side_0, count=counts[3], pool=pools[3])
        return own_0.astype(F32) + side_0.astype(F32) + up.astype(F32) + down.astype(F32)


class Whole:
    def __init__(self, work):
        self.order = [jnp.int32(0)]

    def gather(self, block, use, later=None, counts=(), pools=()):
        used = use(0, gather_seq(block))
        return [used], [later(0, used) if later else ()]

    def scatter(self, term, counts=(), pools=()):
        return scatter_seq(term(0)).astype(F32)


def gather_seq(block):
    return lax.all_gather(block, "seq", axis=0, tiled=True)


def scatter_seq(partial_rows):
    return lax.psum_scatter(partial_rows, "seq", scatter_dimension=0, tiled=True)


def to_core(block):
    return lax.ppermute(block, "fsdp", [(i, i ^ 1) for i in range(4)])


def to_chip(block):
    return lax.ppermute(block, "fsdp", [(i, i ^ 2) for i in range(4)])


def split_low(values):
    high = values.astype(BF)
    low = (values - high.astype(F32)).astype(BF)
    return high, low


def place_rows(whole, piece, start):
    return lax.dynamic_update_slice_in_dim(whole, piece, start, 0)


def per_device(
    layer_input,
    attn_gain,
    query_matrix,
    query_bias_vector,
    key_matrix,
    key_bias_vector,
    value_matrix,
    value_bias_vector,
    sink_logit_values,
    output_matrix,
    output_bias_vector,
    ffn_gain,
    router_weight,
    router_bias,
    expert_gate_up,
    expert_gate_up_bias,
    expert_down,
    expert_down_bias,
    route_ids,
    doc_lengths,
    out_cotangent,
):
    seq_count = lax.axis_size("seq")
    fsdp_count = lax.axis_size("fsdp")
    seq_index = lax.axis_index("seq")
    fsdp_index = lax.axis_index("fsdp")
    tokens_here, width = layer_input.shape[1:]
    choose_count = route_ids.shape[2]
    expert_count = seq_count
    length = seq_count * tokens_here
    block_capacity = max(2, tokens_here * choose_count * 5 // (4 * expert_count))
    capacity = block_capacity * seq_count
    padded = -(-(width + 3 * expert_count) // 128) * 128
    heads_here = QUERY_HEADS // seq_count
    shared_kv = seq_count > KEY_VALUE_HEADS
    q_width = heads_here * HEAD_DIM
    q_part, kv_part = query_matrix.shape[1], key_matrix.shape[1]
    work = Work()
    line = Line(work) if seq_count == 8 else Whole(work)
    chunk = length // len(line.order)
    starts = [place * chunk for place in line.order]
    last = len(starts) - 1

    def taken(rows, start):
        return lax.dynamic_slice_in_dim(rows, start, chunk, 0)

    member_here = jnp.any(
        route_ids[0][:, :, None] == jnp.arange(expert_count, dtype=jnp.int32), axis=1
    )
    cot_here = out_cotangent[0]
    ranks = jnp.cumsum(member_here.astype(jnp.int32), axis=0)
    slot_here = jnp.where(member_here, ranks, 0).astype(BF)

    part = attn_gain.shape[0]
    near_first = [fsdp_index ^ turn for turn in range(fsdp_count)]

    def from_all(piece):
        core, chip = to_core(piece), to_chip(piece)
        return [piece, core, chip, to_core(chip)]

    def in_order(pieces):
        core_bit, chip_bit = fsdp_index % 2 == 0, fsdp_index < 2
        pairs = []
        for own, other in ((pieces[0], pieces[1]), (pieces[2], pieces[3])):
            pairs.append((jnp.where(core_bit, own, other), jnp.where(core_bit, other, own)))
        first = [jnp.where(chip_bit, a, b) for a, b in zip(*pairs)]
        second = [jnp.where(chip_bit, b, a) for a, b in zip(*pairs)]
        return first + second

    kv_head = seq_index // max(1, seq_count // KEY_VALUE_HEADS)

    tiny = jnp.concatenate(
        [sink_logit_values, router_bias, query_bias_vector, key_bias_vector, value_bias_vector]
    )
    tiny = jnp.concatenate([tiny, jnp.zeros((part - tiny.shape[0],), BF)])
    small = jnp.concatenate(
        [
            attn_gain[None],
            ffn_gain[None],
            output_bias_vector[None],
            tiny[None],
            expert_down_bias,
            router_weight.T,
        ],
        axis=0,
    )
    work.pool["small"] = to_core(small), to_chip(small)

    def gather_columns(local):
        whole = lax.all_gather(local, "fsdp", axis=1, tiled=True)
        size = local.shape[1]
        pieces = [whole[:, at * size : (at + 1) * size] for at in range(fsdp_count)]
        return jnp.concatenate(in_order(pieces), axis=1)

    w_query, wo_t = gather_columns(query_matrix), gather_columns(output_matrix.T)
    if not shared_kv:
        kv_all = lax.all_gather(jnp.stack([key_matrix.T, value_matrix.T]), "fsdp", axis=1, tiled=True)

    def parameters():
        small_core, small_chip = work.pool["small"]
        small_all = jnp.stack(in_order([small, small_core, small_chip, to_core(small_chip)]))
        wide = jnp.swapaxes(small_all, 0, 1).reshape(small.shape[0], width).astype(F32)
        attn_gain_f, ffn_gain_f, out_bias_f = wide[0], wide[1], wide[2]
        down_bias_f = wide[4 : 4 + expert_count]
        router_t = wide[4 + expert_count :].astype(BF)
        tiny_all = small_all[:, 3]
        places = [0]
        for piece in (sink_logit_values, router_bias, query_bias_vector, key_bias_vector, value_bias_vector):
            places.append(places[-1] + piece.shape[0])
        sinks_f, router_bias_f, q_bias, k_bias, v_bias = (
            tiny_all[:, a:b].astype(F32) for a, b in zip(places[:-1], places[1:])
        )
        sinks_f, router_bias_f = sinks_f.reshape(-1), router_bias_f.reshape(-1)
        k_bias, v_bias = k_bias.reshape(-1), v_bias.reshape(-1)
        q_bias = jnp.concatenate(
            [lax.dynamic_slice_in_dim(q_bias, at, 1, 0)[0] for at in near_first]
        )
        if shared_kv:

            def own_head(piece):
                whole = lax.all_gather(piece, ("seq", "fsdp"), axis=0, tiled=True)
                return lax.dynamic_slice_in_dim(whole, kv_head * HEAD_DIM, HEAD_DIM, 0)

            w_pair = jnp.concatenate([own_head(key_matrix.T), own_head(value_matrix.T)], axis=0)
            k_bias = own_head(key_bias_vector).astype(F32)
            v_bias = own_head(value_bias_vector).astype(F32)
        else:
            w_pair = kv_all.reshape(2 * HEAD_DIM, width)
        lin_bias = jnp.concatenate([q_bias, k_bias, v_bias])
        return (
            attn_gain_f,
            ffn_gain_f,
            out_bias_f,
            down_bias_f,
            router_t,
            sinks_f,
            router_bias_f,
            w_pair,
            lin_bias,
        )

    work.add("parameters", parameters)

    columns = jnp.concatenate(
        [
            (seq_index * fsdp_count + at) * q_part + jnp.arange(q_part, dtype=jnp.int32)
            for at in near_first
        ]
    )
    whole_heads = q_part % HEAD_DIM == 0

    cosine_table, sine_table = rope_tables(length)
    doc_row = lax.dynamic_slice_in_dim(doc_lengths, fsdp_index, 1, 0)[0]
    doc_ends = jnp.cumsum(doc_row)

    def project(pair):
        pair_f = pair.astype(F32)
        normed = (pair_f * rms_scale(pair_f) * attn_gain_f).astype(BF)
        query_part = dot(normed, w_query, 1, 0) + lin_bias[:q_width]
        return normed, query_part, dot(normed, w_pair, 1, 1) + lin_bias[q_width:]

    pairs = []

    def arrive(at, pair):
        pairs.append(pair)
        return pair

    line.gather(
        layer_input[0],
        lambda at, pair: (work.take("parameters"), arrive(at, pair))[1],
        pools=(("small",), (), (), ()),
    )
    (
        attn_gain_f,
        ffn_gain_f,
        out_bias_f,
        down_bias_f,
        router_t,
        sinks_f,
        router_bias_f,
        w_pair,
        lin_bias,
    ) = work.take("parameters")
    projected = [project(pair) for pair in pairs]
    normed_rows = jnp.zeros((length, width), BF)
    lin = jnp.zeros((length, q_width + 2 * HEAD_DIM), F32)
    for start, (normed, query_part, pair_part) in zip(starts, projected):
        normed_rows = place_rows(normed_rows, normed, start)
        lin = lax.dynamic_update_slice(lin, query_part, (start, 0))
        lin = lax.dynamic_update_slice(lin, pair_part, (start, q_width))
    if not whole_heads:
        order = jnp.argsort(columns)
        w_query = w_query[:, order]
        wo_t = wo_t[:, order]
        lin = jnp.concatenate([lin[:, :q_width][:, order], lin[:, q_width:]], axis=1)
        head_numbers = seq_index * heads_here + jnp.arange(heads_here, dtype=jnp.int32)
    else:
        head_numbers = columns[::HEAD_DIM] // HEAD_DIM
    head_lane = (head_numbers[:, None] == jnp.arange(QUERY_HEADS)[None, :]).astype(F32)
    sinks_here = jnp.sum(head_lane * sinks_f[None, :], axis=1)
    turned, heads = attend(lin, cosine_table, sine_table, doc_ends, sinks_here)
    attn_sum = line.scatter(
        lambda at: dot(taken(heads, starts[at]), wo_t, 1, 1).astype(BF), counts=(0, 0, 0, 0)
    )

    resid_in = layer_input[0].astype(F32)
    resid_mid = resid_in + attn_sum + out_bias_f
    norm_two = rms_scale(resid_mid)
    unit_mid = resid_mid * norm_two
    normed_mid = (unit_mid * ffn_gain_f).astype(BF)
    logits = dot(normed_mid, router_t, 1, 1) + router_bias_f
    gates = jax.nn.softmax(jnp.where(member_here, logits, -1e30), axis=-1)
    gates = jnp.where(member_here, gates, 0.0)
    gate_high, gate_low = split_low(gates)
    mid_packed = jnp.concatenate(
        [
            normed_mid,
            slot_here,
            gate_high,
            gate_low,
            jnp.zeros((tokens_here, padded - width - 3 * expert_count), BF),
        ],
        axis=1,
    )

    expert_lane = (jnp.arange(expert_count, dtype=jnp.int32) == seq_index).astype(F32)
    slots = block_capacity * (chunk // tokens_here)
    slot_number = jnp.arange(block_capacity, dtype=F32) + 1.0
    selects = {}

    def pick_rows(at, pair):
        rank = jnp.sum(pair[:, width : width + expert_count].astype(F32) * expert_lane, axis=1)
        blocks = chunk // tokens_here
        hit = slot_number[None, :, None] == rank.reshape(blocks, 1, tokens_here)
        same = jnp.eye(blocks, dtype=jnp.bool_)[:, None, :, None]
        select = (hit[:, :, None, :] & same).reshape(slots, chunk).astype(BF)
        return select, dot(select, pair, 1, 0).astype(BF)

    def send_rows(at, used):
        return to_core(used[1]), to_chip(used[1])

    spare = padded - width
    work.pool["cot"] = jnp.concatenate([cot_here, jnp.zeros((tokens_here, spare), BF)], axis=1)
    picked, sent = line.gather(mid_packed, pick_rows, send_rows, pools=((), ("cot",), (), ()))
    selects = [select for select, _ in picked]
    own_rows = [rows for _, rows in picked]
    core_rows = [core for core, _ in sent]
    chip_rows = [chip for _, chip in sent]
    units_w = jnp.pad(jnp.swapaxes(expert_gate_up[0], 1, 2), ((0, 0), (0, 0), (0, spare)))
    down_w = jnp.pad(expert_down[0], ((0, 0), (0, spare)))
    units_b = expert_gate_up_bias[0].astype(F32)[:, None, :]

    def joined(pieces):
        whole = jnp.zeros((2 * capacity, pieces[0].shape[1]), BF)
        first = 0
        for piece in pieces:
            whole = place_rows(whole, piece, first)
            first += piece.shape[0]
        return whole

    def einsum(form, left, right):
        return jnp.einsum(form, left, right, preferred_element_type=F32)

    def hidden_step(rows):
        tail = rows[:, width + expert_count :].astype(F32)
        share = jnp.sum(
            (tail[:, :expert_count] + tail[:, expert_count : 2 * expert_count]) * expert_lane,
            axis=1,
            keepdims=True,
        )
        before = einsum("rd,khd->krh", rows, units_w) + units_b
        hidden = swiglu(before[0], before[1]).astype(BF)
        return share, before, hidden, (hidden.astype(F32) * share).astype(BF)

    def mix_step(made):
        return dot(made[3], down_w, 1, 0).astype(BF)

    def back_step(made, cot):
        share, before, hidden, _ = made
        grad_hidden = dot(cot, down_w, 1, 1)
        score = jnp.sum(hidden.astype(F32) * grad_hidden, axis=1, keepdims=True)
        _, glu_back = jax.vjp(swiglu, before[0], before[1])
        grad_gate_pre, grad_up_pre = glu_back(grad_hidden * share)
        return score, jnp.stack([grad_gate_pre.astype(BF), grad_up_pre.astype(BF)])

    def row_step(made):
        return einsum("krh,khd->rd", made, units_w).astype(BF)

    cot_rows = gather_seq(work.pool["cot"])
    near = joined(own_rows + core_rows)
    select_all = jnp.zeros((capacity, length), BF)
    for at, (select, start) in enumerate(zip(selects, starts)):
        select_all = lax.dynamic_update_slice(select_all, select, (at * slots, start))
    made_n = hidden_step(near)
    select_chip = to_chip(select_all)
    mix_n = mix_step(made_n)
    made_n, chip_rows, mix_n = work.tie(made_n, chip_rows, mix_n)
    far = joined(chip_rows + [to_core(chip) for chip in chip_rows])
    made_o = hidden_step(far)
    mix_o = mix_step(made_o)
    mix_core_n, mix_core_o = to_core(mix_n[capacity:]), to_core(mix_o[capacity:])
    cot_rows, made_n, made_o, mix_n, mix_o, mix_core_n, select_chip = work.tie(
        cot_rows, made_n, made_o, mix_n, mix_o, mix_core_n, select_chip
    )
    cot_own = dot(select_all, cot_rows, 1, 0).astype(BF)
    half = (len(selects) + 1) // 2 * slots
    cot_own = [cot_own[:half], cot_own[half:]] if half < capacity else [cot_own]
    cot_first = to_chip(cot_own[0])
    cot_near = joined(cot_own + [to_core(rows) for rows in cot_own])
    def core_sum(part, from_core):
        return (part[:capacity].astype(F32) + from_core.astype(F32)).astype(BF)

    def total(near_part, from_core, arrived, at):
        return (
            slot_rows(near_part, at).astype(F32)
            + slot_rows(from_core, at).astype(F32)
            + arrived.astype(F32)
        )

    def slot_rows(rows, at):
        return rows[at * slots : (at + 1) * slots]

    low_rows = (len(starts) // 2) * slots

    def score_step(back_n, back_o):
        scores = jnp.concatenate([back_n[0], back_o[0]], axis=1)
        return scores[:capacity] + to_core(scores[capacity:])

    mix_own = dot(select_all, core_sum(mix_n, mix_core_n), 0, 0).astype(BF)
    mix_other = dot(select_chip, core_sum(mix_o, mix_core_o), 0, 0).astype(BF)
    mix_own, mix_other, cot_near, cot_first, cot_own = work.tie(
        mix_own, mix_other, cot_near, cot_first, cot_own
    )
    cot_chip = [cot_first] + [to_chip(rows) for rows in cot_own[1:]]
    mix_own, mix_other = scatter_seq(mix_own), scatter_seq(mix_other)

    back_n = back_step(made_n, cot_near)
    row_n = row_step(back_n[1])

    back_n, row_n, cot_chip = work.tie(back_n, row_n, cot_chip)
    row_near_core = to_core(row_n[capacity:])
    cot_far = joined(cot_chip + [to_core(rows) for rows in cot_chip])
    back_o = back_step(made_o, cot_far)
    back_n, back_o, row_near_core = work.tie(back_n, back_o, row_near_core)
    score = score_step(back_n, back_o)
    score = score[:, :1] + to_chip(score[:, 1:])
    row_o_core = row_step(back_o[1][:, capacity:])
    row_o_core, back_o, score = work.tie(row_o_core, back_o, score)
    row_far_core = to_core(row_o_core)
    row_o = row_step(back_o[1][:, :capacity])
    (score_n, low_n), (score_o, low_o) = back_n, back_o


    def chunk_of(low, high, at):
        first = at * slots
        if first < low_rows:
            return low[first : first + slots]
        return high[first - low_rows : first - low_rows + slots]

    def units_step(low_n, rows_n, low_o, rows_o):
        return einsum("krh,rd->khd", low_n, rows_n[:, :width]) + einsum(
            "krh,rd->khd", low_o, rows_o[:, :width]
        )

    def down_step(hidden_n, cot_n, hidden_o, cot_o):
        return dot(hidden_n, cot_n[:, :width], 0, 0) + dot(hidden_o, cot_o[:, :width], 0, 0)

    work.add("units", units_step, low_n, near, low_o, far)
    work.add("down", down_step, made_n[3], cot_near, made_o[3], cot_far)
    row_far_core, row_o, mix_own = work.tie(row_far_core, row_o, mix_own)
    row_sum_far = core_sum(row_o, row_far_core)
    row_high, row_low = to_chip(row_sum_far[low_rows:]), row_sum_far[:low_rows]
    row_high, row_low = work.tie(row_high, row_low, count=1)
    row_low = to_chip(row_low)
    def back_term(at):
        row_sum = total(row_n, row_near_core, chunk_of(row_low, row_high, at), at)
        grad_high, grad_low = split_low(slot_rows(score, at) * expert_lane)
        back_packed = jnp.concatenate(
            [
                row_sum[:, :width].astype(BF),
                grad_high,
                grad_low,
                jnp.zeros((slots, padded - width - 2 * expert_count), BF),
            ],
            axis=1,
        )
        return dot(selects[at], back_packed, 0, 0).astype(BF)

    work.pool["mix"] = mix_other
    back = line.scatter(back_term, counts=(1, 0, 0, 0))

    cot_f = cot_here.astype(F32)
    grad_gates = (
        back[:, width : width + expert_count]
        + back[:, width + expert_count : width + 2 * expert_count]
        + dot(cot_f, down_bias_f, 1, 1, EXACT)
    )
    mean_gate = jnp.sum(gates * grad_gates, axis=-1, keepdims=True)
    grad_logits = gates * (grad_gates - mean_gate)
    router_grad_t = dot(grad_logits, normed_mid.astype(F32), 0, 0, EXACT)
    router_bias_grad = jnp.sum(grad_logits, axis=0)
    down_bias_grad = dot(gates, cot_f, 0, 0, EXACT)
    grad_normed_mid = back[:, :width] + dot(grad_logits, router_t.astype(F32), 1, 0, EXACT)
    ffn_gain_grad = jnp.sum(grad_normed_mid * unit_mid, axis=0)
    grad_unit_mid = grad_normed_mid * ffn_gain_f
    grad_mid = (
        norm_two
        * (grad_unit_mid - unit_mid * jnp.mean(grad_unit_mid * unit_mid, axis=-1, keepdims=True))
        + cot_f
    )
    grad_attn = grad_mid.astype(BF)
    out_bias_grad = jnp.sum(grad_attn.astype(F32), axis=0)

    def to_core_owners(blocks, kind=BF):
        both = to_core(jnp.stack([blocks[1], blocks[3]]).astype(kind))
        return blocks[0] + both[0].astype(F32), (blocks[2] + both[1].astype(F32)).astype(kind)

    def to_owners(sums):
        own, chip = sums
        return own + to_chip(chip).astype(F32)

    def fsdp_sum(values):
        values = values + to_core(values)
        return values + to_chip(values)

    def seq_step(step):
        def add_other(values):
            return values + lax.ppermute(values, "seq", [(i, i ^ step) for i in range(seq_count)])

        return add_other

    def own_part(whole_array, axis_number):
        piece_size = whole_array.shape[axis_number] // fsdp_count
        return lax.dynamic_slice_in_dim(
            whole_array, fsdp_index * piece_size, piece_size, axis_number
        )

    tiny_grad = jnp.concatenate([router_bias_grad, jnp.zeros((width - expert_count,), F32)])[None]
    small_grad = jnp.concatenate(
        [out_bias_grad[None], ffn_gain_grad[None], tiny_grad, down_bias_grad, router_grad_t],
        axis=0,
    )

    work.add("small_fsdp", fsdp_sum, small_grad)

    attn_rows = jnp.zeros((length, width), BF)
    grad_heads = jnp.zeros((length, q_width), BF)

    def head_grads(at, pair):
        return pair, dot(pair, wo_t, 1, 0).astype(BF)

    grads, _ = line.gather(
        grad_attn, head_grads, counts=(0, 0, 1, 0), pools=(("mix",), (), (), ())
    )
    mixture = (mix_own.astype(F32) + to_chip(work.pool["mix"]).astype(F32))[:, :width]
    mixture = mixture + dot(gates, down_bias_f, 1, 0, EXACT)
    layer_output = (resid_mid + mixture).astype(BF)[None]
    for start, (pair, grad_part) in zip(starts, grads):
        attn_rows = place_rows(attn_rows, pair, start)
        grad_heads = place_rows(grad_heads, grad_part, start)

    def column_blocks(whole):
        if back_order is not None:
            whole = whole[:, back_order]
        return [whole[:, at * q_part : (at + 1) * q_part] for at in range(fsdp_count)]

    order = None if whole_heads else jnp.argsort(columns)
    back_order = None if whole_heads else jnp.argsort(order)
    out_sums = to_core_owners(column_blocks(dot(attn_rows, heads, 0, 0)))
    lin_grad, lin_sums, sink_here_grad = attend_back(
        turned, cosine_table, sine_table, doc_ends, sinks_here, grad_heads
    )

    lin_grad, lin_sums, out_sums = work.tie(lin_grad, lin_sums, out_sums)

    def query_step(rows, grads):
        return dot(rows, grads[:, :q_width], 0, 0)

    def pair_step(rows, grads):
        return dot(grads[:, q_width:], rows, 0, 0)

    def gain_step(query_w_part, pair_w_part):
        attn_gain_grad = (
            jnp.sum(query_w_part * w_query.astype(F32), axis=1)
            + jnp.sum(pair_w_part * w_pair.astype(F32), axis=0)
        ) / attn_gain_f
        sink_all_grad = jnp.sum(head_lane * sink_here_grad[:, None], axis=0)
        sink_row = jnp.concatenate([sink_all_grad, jnp.zeros((width - QUERY_HEADS,), F32)])
        return jnp.stack([attn_gain_grad, sink_row])

    def sums_step(lin_sums):
        query_sums = lin_sums[:q_width]
        if back_order is not None:
            query_sums = query_sums[back_order]
        pieces = [query_sums[at * q_part : (at + 1) * q_part] for at in range(fsdp_count)]
        return fsdp_sum(jnp.concatenate(in_order(pieces) + [lin_sums[q_width:]])[None])[0]

    def pair_sum(pair_w_part):
        if shared_kv:
            return ()
        summed = pair_w_part + to_core(pair_w_part.astype(BF)).astype(F32)
        return summed + to_chip(summed.astype(BF)).astype(F32)

    work.add("query_w", query_step, normed_rows, lin_grad)
    work.add("pair_w", pair_step, normed_rows, lin_grad)
    work.add("out_chip", lambda own, chip: to_owners((own, chip)), *out_sums)
    work.add("query_core", lambda whole: to_core_owners(column_blocks(whole)), "query_w")
    work.add("gain", gain_step, "query_w", "pair_w")
    work.add("query_chip", to_owners, "query_core")
    work.add("gain_core", lambda values: values + to_core(values), "gain")
    work.add("sums", sums_step, lin_sums)
    work.add("pair_sum", pair_sum, "pair_w")
    work.add(
        "all_1",
        lambda values, small: jnp.concatenate([values + to_chip(values), small]),
        "gain_core",
        "small_fsdp",
    )
    step = 1
    while step < seq_count:
        work.add("all_%d" % (2 * step), seq_step(step), "all_%d" % step)
        step *= 2

    def input_term(at):
        grad_part = taken(lin_grad, starts[at])
        return (
            dot(grad_part[:, :q_width], w_query, 1, 1) + dot(grad_part[:, q_width:], w_pair, 1, 0)
        ).astype(BF)

    grad_normed_in = line.scatter(input_term, counts=(1, 3, 2, 4))
    query_w_own = work.take("query_chip")
    out_w_own = work.take("out_chip").T
    pair_all, small_sum = work.take("pair_sum"), work.take("all_%d" % seq_count)
    small_own = own_part(small_sum, 1)
    down_grad = work.take("down")
    gate_up_grad = jnp.swapaxes(work.take("units"), 1, 2)
    gate_up_bias_grad = jnp.sum(low_n.astype(F32), axis=1) + jnp.sum(low_o.astype(F32), axis=1)

    resid_scale = rms_scale(resid_in)
    unit_in = resid_in * resid_scale
    grad_unit_in = grad_normed_in * attn_gain_f
    input_grad = (
        resid_scale
        * (grad_unit_in - unit_in * jnp.mean(grad_unit_in * unit_in, axis=-1, keepdims=True))
        + grad_mid
    )

    sums = work.take("sums")
    query_b_own = own_part(sums[: fsdp_count * q_part], 0)
    if shared_kv:

        def whole_sum(part_grad):
            whole = jnp.zeros((KEY_VALUE_HEADS * HEAD_DIM,) + part_grad.shape[1:], F32)
            whole = lax.dynamic_update_slice_in_dim(whole, part_grad, kv_head * HEAD_DIM, 0)
            return lax.psum_scatter(whole, ("seq", "fsdp"), scatter_dimension=0, tiled=True)

        pair_w_part = work.take("pair_w")
        key_w_own = whole_sum(pair_w_part[:HEAD_DIM]).T
        value_w_own = whole_sum(pair_w_part[HEAD_DIM:]).T
        key_b_own = whole_sum(lin_sums[q_width : q_width + HEAD_DIM])
        value_b_own = whole_sum(lin_sums[q_width + HEAD_DIM :])
    else:
        key_w_own = own_part(pair_all[:HEAD_DIM], 0).T
        value_w_own = own_part(pair_all[HEAD_DIM:], 0).T
        key_b_own, value_b_own = (
            own_part(sums[q_width : q_width + HEAD_DIM], 0),
            own_part(sums[q_width + HEAD_DIM :], 0),
        )

    return (
        layer_output,
        input_grad[None],
        small_own[0],
        query_w_own,
        query_b_own,
        key_w_own,
        key_b_own,
        value_w_own,
        value_b_own,
        own_part(small_sum[1, :QUERY_HEADS], 0),
        out_w_own,
        small_own[2],
        small_own[3],
        small_own[5 + expert_count :].T,
        own_part(small_sum[4, :expert_count], 0),
        gate_up_grad[None],
        gate_up_bias_grad[None],
        down_grad[None],
        small_own[5 : 5 + expert_count],
    )


def solution(mesh):
    return jax.shard_map(
        per_device,
        mesh=mesh,
        in_specs=(
            P("fsdp", "seq", None),
            P("fsdp"),
            P(None, ("seq", "fsdp")),
            P(("seq", "fsdp")),
            P(None, ("seq", "fsdp")),
            P(("seq", "fsdp")),
            P(None, ("seq", "fsdp")),
            P(("seq", "fsdp")),
            P("fsdp"),
            P(("seq", "fsdp"), None),
            P("fsdp"),
            P("fsdp"),
            P("fsdp", None),
            P("fsdp"),
            P("seq", None, None, "fsdp"),
            P("seq", None, "fsdp"),
            P("seq", "fsdp", None),
            P(None, "fsdp"),
            P("fsdp", "seq", None),
            P(),
            P("fsdp", "seq", None),
        ),
        out_specs=(
            P("fsdp", "seq", None),
            P("fsdp", "seq", None),
            P("fsdp"),
            P(None, ("seq", "fsdp")),
            P(("seq", "fsdp")),
            P(None, ("seq", "fsdp")),
            P(("seq", "fsdp")),
            P(None, ("seq", "fsdp")),
            P(("seq", "fsdp")),
            P("fsdp"),
            P(("seq", "fsdp"), None),
            P("fsdp"),
            P("fsdp"),
            P("fsdp", None),
            P("fsdp"),
            P("seq", None, None, "fsdp"),
            P("seq", None, "fsdp"),
            P("seq", "fsdp", None),
            P(None, "fsdp"),
        ),
        check_vma=False,
    )
```
